32 devices in a mesh: dp: 8 (over y, x, core), expert: 4 (over z).
Axes of the slice: x: 2, y: 2, z: 4, core: 2. Of those that a mesh axis runs over, the one named last changes fastest.
Arguments:
- layer_inputs_matrix: bfloat16 [32768, 768], P(('dp', 'expert')), may hold values from -6 to 6
- upstream_output_sensitivity: bfloat16 [32768, 768], P(('dp', 'expert')), may hold values from -6 to 6
- mixer_layernorm_scale: float32 [768], replicated, may hold values from 0.5 to 1.5
- mixer_layernorm_offset: float32 [768], replicated, may hold values from -1 to 1
- asker_matrix: bfloat16 [768, 768], replicated, may hold values from -0.21875 to 0.21875
- lookup_label_matrix: bfloat16 [768, 768], replicated, may hold values from -0.21875 to 0.21875
- content_matrix: bfloat16 [768, 768], replicated, may hold values from -0.21875 to 0.21875
- mixer_result_matrix: bfloat16 [768, 768], replicated, may hold values from -1.75 to 1.75
- specialist_layernorm_scale: float32 [768], replicated, may hold values from 0.5 to 1.5
- specialist_layernorm_offset: float32 [768], replicated, may hold values from -0.5 to 0.5
- dispatch_projection_matrix: float32 [768, 16], replicated, may hold values from -0.21875 to 0.21875
- specialist_centroids: float32 [4, 16], replicated, may hold values from -5 to 5
- learned_sharpness: float32 [1], replicated, may hold values from 0.25 to 0.45
- specialist_widening_matrix: bfloat16 [4, 768, 3072], P('expert'), may hold values from -0.21875 to 0.21875
- specialist_narrowing_matrix: bfloat16 [4, 3072, 768], P('expert'), may hold values from -0.4375 to 0.4375
- document_labels: int32 [64, 512], P(('dp', 'expert')), may hold values from 0 to 7, never falling along the last dimension, each value on 1 to 256 neighbouring positions
- chosen_specialist: int32 [32768, 1], P(('dp', 'expert')), may hold values from 0 to 3; in each aligned block of 1024 rows (0 to 1023, 1024 to 2047, ...) at most 384 rows name the same one
- placement_ranks: int32 [32, 1024], P(('dp', 'expert')), may hold values from 0 to 1023, each once within a row
Outputs:
- layer_output: bfloat16 [32768, 768], P(('dp', 'expert'))
- tokens_grad: bfloat16 [32768, 768], P(('dp', 'expert'))
- attngain_grad: float32 [768], P(('dp', 'expert'))
- attnshift_grad: float32 [768], P(('dp', 'expert'))
- query_grad: float32 [768, 768], P(('dp', 'expert'))
- key_grad: float32 [768, 768], P(('dp', 'expert'))
- value_grad: float32 [768, 768], P(('dp', 'expert'))
- outer_grad: float32 [768, 768], P(('dp', 'expert'))
- routegain_grad: float32 [768], P(('dp', 'expert'))
- routeshift_grad: float32 [768], P(('dp', 'expert'))
- router_grad: float32 [768, 16], P(('dp', 'expert'))
- centroid_derivative: float32 [4, 16], replicated
- sharpness_derivative: float32 [1], replicated
- hidden_grad: float32 [4, 768, 3072], P('expert', 'dp')
- return_grad: float32 [4, 3072, 768], P('expert', 'dp')
The draws below stay inside these ranges and needn't reach their ends.
Inputs may be any that keep to these rules, and one draw needn't show every extreme that they name: `chosen_specialist`: within the 1024 rows of one device no expert is named by more than 384 rows, a bound that some block reaches. `document_labels`: ids never fall along a row; a segment has 1 to 256 rows. `placement_ranks`: each row is a permutation; a smaller value is placed first.
All inputs are finite; a program needn't handle non-finite values.
Results may differ from the reference program's by a relative error of at most 0.035.
Values may be sent and summed in bfloat16 or wider, within the bound.
No kernel may reach another device: no remote copies, remote signals or barrier semaphores. Data moves between devices by JAX's collectives and lax.ppermute only.
A program may use at most 256 MiB of HBM per device.

```python
import math
import jax
import jax.numpy as jnp
import numpy as np
from jax import lax

D = 768
HEADS = 12
HEAD_DIM = 64
FF = 3072
ROUTE = 16
LEN = 512
TOK_DEV = 1024
SEQS = 64
TOKENS = 32768
EXPERTS = 4
CAP = 1024
SLOTS = 384
N_DP = 8
N_EXPERT = 4
DEVICES = 32


def steps_of(key, shape, split, low, largest):
    loudness, own = 1.0, jax.random.fold_in(key, 6)
    for position, parts in split:
        draws = jnp.exp(jax.random.uniform(jax.random.fold_in(own, position), (parts,), jnp.float32, low / len(split), largest / len(split)))
        loudness = loudness * jnp.repeat(draws, shape[position] // parts).reshape([-1 if axis == position else 1 for axis in range(len(shape))])
    return loudness


def profile(amount, total, reach, lean):
    weights = [(1 << 20) // math.isqrt(rank ** lean) + 1 for rank in range(2, amount + 1)]
    spare, holding = total - reach - (amount - 1), [1] * (amount - 1)
    while spare > 0:
        candidates = [i for i in range(amount - 1) if holding[i] < reach]
        whole, remaining = sum([weights[i] for i in candidates]), spare
        for i in candidates:
            extra = min(reach - holding[i], max(1, remaining * weights[i] // whole), spare)
            holding[i] = holding[i] + extra
            spare = spare - extra
    return np.array([reach] + holding)


def ragged(stream_key, number_of, total, most, lean):
    if number_of == 2:
        one = jax.random.randint(stream_key, (), max(1, total - most), min(most, total - 1) + 1)
        return jnp.stack([one, total - one])
    sizes = jnp.asarray(profile(number_of, total, most, lean), jnp.int32)
    twos = (number_of - 1) // 2
    donor, sink = sizes[1:1 + 2 * twos:2], sizes[2:2 + 2 * twos:2]
    margin = jnp.minimum(donor - 1, most - sink)
    moved = jax.random.randint(jax.random.fold_in(stream_key, 1), (twos,), 0, 1 << 20) % (margin + 1)
    sizes = sizes.at[1:1 + 2 * twos:2].set(donor - moved).at[2:2 + 2 * twos:2].set(sink + moved)
    return sizes[jax.random.permutation(jax.random.fold_in(stream_key, 2), number_of)]


def shared_out(stream_key, own, number, rows, amount, top, reach, skew):
    ranking = jax.random.permutation(stream_key, amount)
    crowded, common = portions_of(amount, rows * top, reach, skew, True), portions_of(amount, rows * top, reach, skew, False)
    places = jnp.arange(amount)

    def named(sizes, offset_by):
        used = int((sizes > 0).sum())
        fixed = max(1, used // 4)
        passed = fixed + (places - fixed + offset_by * (used - fixed)) % max(1, amount - fixed)
        return jnp.zeros((amount,), jnp.int32).at[ranking[jnp.where(places < fixed, places, passed)]].set(jnp.asarray(sizes, jnp.int32))

    sizes = jnp.where(number % 4 == 0, named(crowded, number // 4), named(common, number - number // 4 - 1))
    mixed = jax.random.permutation(jax.random.fold_in(own, 3), amount)
    giver, taker = mixed[0:amount // 2 * 2:2], mixed[1:amount // 2 * 2:2]
    margin = jnp.minimum(sizes[giver] - 1, reach - sizes[taker]) // 2
    margin = jnp.where((giver == ranking[0]) | (taker == ranking[0]) | (sizes[taker] == 0), 0, jnp.maximum(margin, 0))
    passed = jax.random.randint(jax.random.fold_in(own, 4), (amount // 2,), 0, 1 << 20) % (margin + 1)
    sizes = sizes.at[giver].add(-passed).at[taker].add(passed)
    items = jnp.searchsorted(jnp.cumsum(sizes), jnp.arange(rows * top), side="right").astype(jnp.int32)
    listing = items.reshape(top, rows).T
    listing = listing[jax.random.permutation(jax.random.fold_in(own, 1), rows)]
    offset_by = jax.random.randint(jax.random.fold_in(own, 2), (rows, 1), 0, top)
    return jnp.take_along_axis(listing, (jnp.arange(top)[None, :] + offset_by) % top, axis=1)


def portions_of(count, total, reach, lean, full):
    loads = [(1 << 20) // math.isqrt(standing ** lean) + 1 for standing in range(1, count + 1)]
    largest = reach if full else min(reach, max(-(-total // count), total * loads[0] // sum(loads)))
    least = 1 if total - largest >= count - 1 else 0
    holding, spare = [largest] + [least] * (count - 1), total - largest - least * (count - 1)
    while spare > 0:
        candidates = [i for i in range(1, count) if holding[i] < largest] or [i for i in range(1, count) if holding[i] < reach]
        pool, remaining = sum([loads[i] for i in candidates]), spare
        for i in candidates:
            addition = min(reach - holding[i], max(1, remaining * loads[i] // pool), spare)
            holding[i] = holding[i] + addition
            spare = spare - addition
    return np.array(holding)


def bell_draw(key, shape, scale, limit, pieces=(), held_as=jnp.bfloat16):
    values = jax.random.normal(key, shape, jnp.float32) * scale
    if len(pieces) > 0:
        values = steps_of(key, shape, pieces, -0.22, 0.18) * values
    return jnp.clip(values, min=-limit, max=limit).astype(held_as)


def setup_inputs(seed: int = 0) -> dict:
    streams_of = jax.random.split(jax.random.key(seed), 19)
    layer_inputs_matrix = bell_draw(streams_of[0], (TOKENS, D), 1.0, 6.0, ((0, 32),))
    upstream_output_sensitivity = bell_draw(streams_of[1], (TOKENS, D), 1.0, 6.0, ((0, 32),))
    mixer_layernorm_scale = jnp.clip(1.0 + 0.1 * jax.random.normal(streams_of[2], (D,), jnp.float32), 0.5, 1.5)
    mixer_layernorm_offset = bell_draw(streams_of[3], (D,), 0.2, 1.0, (), jnp.float32)
    asker_matrix = bell_draw(streams_of[4], (D, D), D ** -0.5, 0.21875)
    lookup_label_matrix = bell_draw(streams_of[5], (D, D), D ** -0.5, 0.21875)
    content_matrix = bell_draw(streams_of[6], (D, D), D ** -0.5, 0.21875)
    mixer_result_matrix = bell_draw(streams_of[7], (D, D), (D // 64) ** -0.5, 1.75)
    specialist_layernorm_scale = jnp.clip(1.0 + 0.1 * jax.random.normal(streams_of[8], (D,), jnp.float32), 0.5, 1.5)
    specialist_layernorm_offset = bell_draw(streams_of[9], (D,), 0.1, 0.5, (), jnp.float32)
    dispatch_projection_matrix = bell_draw(streams_of[10], (D, ROUTE), D ** -0.5, 0.21875, (), jnp.float32)
    specialist_centroids = bell_draw(streams_of[11], (EXPERTS, ROUTE), 1.0, 5.0, (), jnp.float32)
    learned_sharpness = jnp.clip(jax.random.uniform(streams_of[12], (1,), jnp.float32, 0.25, 0.45), 0.25, 0.45)
    specialist_widening_matrix = bell_draw(streams_of[13], (EXPERTS, D, FF), D ** -0.5, 0.21875, ((0, 4),))
    specialist_narrowing_matrix = bell_draw(streams_of[14], (EXPERTS, FF, D), (max(1, FF // (EXPERTS * EXPERTS))) ** -0.5, 0.4375, ((0, 4),))
    document_labels = jax.vmap(lambda own: jnp.searchsorted(jnp.cumsum(ragged(own, 8, LEN, LEN // 2, 0)), jnp.arange(LEN), side="right"))(jax.random.split(streams_of[15], SEQS)).reshape((SEQS, LEN)).astype(jnp.int32)
    chosen_specialist_keys = jax.random.split(jax.random.fold_in(streams_of[16], 1), TOKENS // TOK_DEV)
    chosen_specialist_turns = jax.random.permutation(jax.random.fold_in(streams_of[16], 3), TOKENS // TOK_DEV)
    chosen_specialist = jax.vmap(lambda own, number: shared_out(jax.random.fold_in(streams_of[16], 2), own, number, TOK_DEV, EXPERTS, 1, SLOTS, 1))(chosen_specialist_keys, chosen_specialist_turns).reshape((TOKENS, 1))
    placement_ranks = jax.vmap(lambda own: jax.random.permutation(own, TOK_DEV))(jax.random.split(streams_of[17], DEVICES)).reshape((DEVICES, TOK_DEV)).astype(jnp.int32)
    return dict(layer_inputs_matrix=layer_inputs_matrix, upstream_output_sensitivity=upstream_output_sensitivity, mixer_layernorm_scale=mixer_layernorm_scale, mixer_layernorm_offset=mixer_layernorm_offset, asker_matrix=asker_matrix, lookup_label_matrix=lookup_label_matrix, content_matrix=content_matrix, mixer_result_matrix=mixer_result_matrix, specialist_layernorm_scale=specialist_layernorm_scale, specialist_layernorm_offset=specialist_layernorm_offset, dispatch_projection_matrix=dispatch_projection_matrix, specialist_centroids=specialist_centroids, learned_sharpness=learned_sharpness, specialist_widening_matrix=specialist_widening_matrix, specialist_narrowing_matrix=specialist_narrowing_matrix, document_labels=document_labels, chosen_specialist=chosen_specialist, placement_ranks=placement_ranks)


HIGHEST = lax.Precision.HIGHEST

@jax.custom_vjp
def low(v):
    return lax.optimization_barrier(v.astype(jnp.bfloat16)).astype(jnp.float32)

@jax.custom_vjp
def low_back(v):
    return v

def low_keep(v):
    return (low(v), None)

def low_pass(kept, grad):
    return (grad,)

def back_keep(v):
    return (v, None)

def back_low(kept, grad):
    return (low(grad),)
low.defvjp(low_keep, low_pass)
low_back.defvjp(back_keep, back_low)

def layer_norm(values, norm_gain, norm_shift):
    centered = values - lax.optimization_barrier(jnp.mean(values, axis=-1, keepdims=True))
    variance = lax.optimization_barrier(jnp.mean(centered * centered, axis=-1, keepdims=True))
    return centered * lax.rsqrt(variance + 1e-05) * norm_gain + norm_shift

def routing_gate_value(normed, router_mat, embed_mat, temper_val, selected_expert):
    projected = jnp.dot(normed, router_mat, precision=HIGHEST)
    unit_rows = projected * lax.rsqrt(lax.optimization_barrier(jnp.sum(projected * projected, axis=-1, keepdims=True)) + 1.0)
    unit_table = embed_mat * lax.rsqrt(lax.optimization_barrier(jnp.sum(embed_mat * embed_mat, axis=-1, keepdims=True)) + 1.0)
    logits = jnp.dot(unit_rows, unit_table.T, precision=HIGHEST) / temper_val[0]
    routed = jax.nn.softmax(logits, axis=-1)
    return lax.optimization_barrier(jnp.sum(routed * selected_expert, axis=-1))

def attend(block):
    query_rows, key_rows, value_rows, segment_row = block
    scores = jnp.einsum('qhd,khd->hqk', query_rows, key_rows, precision=HIGHEST) * HEAD_DIM ** (-0.5)
    scores = low_back(scores)
    allowed = segment_row[:, None] == segment_row[None, :]
    scores = jnp.where(allowed[None], scores, -1e+30)
    probs = jax.nn.softmax(scores, axis=-1)
    return jnp.einsum('hqk,khd->qhd', low(probs), value_rows, precision=HIGHEST)

def expert_apply(block):
    expert_rows, hidden_mat, return_mat = block
    expert_pre = low_back(jnp.einsum('gcd,df->gcf', expert_rows, hidden_mat, precision=HIGHEST))
    expert_act = low(jax.nn.gelu(expert_pre, approximate=False))
    return low_back(low(jnp.einsum('gcf,fd->gcd', expert_act, return_mat, precision=HIGHEST)))

def reference(layer_inputs_matrix, upstream_output_sensitivity, mixer_layernorm_scale, mixer_layernorm_offset, asker_matrix, lookup_label_matrix, content_matrix, mixer_result_matrix, specialist_layernorm_scale, specialist_layernorm_offset, dispatch_projection_matrix, specialist_centroids, learned_sharpness, specialist_widening_matrix, specialist_narrowing_matrix, document_labels, chosen_specialist, placement_ranks):
    token_ids = jnp.arange(TOKENS, dtype=jnp.int32)
    chosen_ids = chosen_specialist[:, 0].astype(jnp.int32)
    chosen_int = (chosen_ids[:, None] == jnp.arange(EXPERTS, dtype=jnp.int32)[None, :]).astype(jnp.int32)
    device_hot = chosen_int.reshape(DEVICES, TOK_DEV, EXPERTS)
    device_rows = jnp.arange(DEVICES, dtype=jnp.int32)[:, None]
    positions = jnp.broadcast_to(jnp.arange(TOK_DEV, dtype=jnp.int32)[None, :], (DEVICES, TOK_DEV))
    inverse = jnp.zeros((DEVICES, TOK_DEV), jnp.int32).at[device_rows, placement_ranks].set(positions)
    sorted_hot = jnp.take_along_axis(device_hot, inverse[:, :, None], axis=1)
    running = (jnp.cumsum(sorted_hot, axis=1) - sorted_hot).astype(jnp.int32)
    sorted_rank = lax.optimization_barrier(jnp.sum(running * sorted_hot, axis=2)).astype(jnp.int32)
    rank_local = jnp.take_along_axis(sorted_rank, placement_ranks, axis=1).astype(jnp.int32)
    tallies = lax.optimization_barrier(jnp.sum(device_hot, axis=1)).astype(jnp.int32).reshape(N_DP, N_EXPERT, EXPERTS)
    prior = (jnp.cumsum(tallies, axis=1) - tallies).astype(jnp.int32).reshape(DEVICES, EXPERTS)
    slot_index = (lax.optimization_barrier(jnp.sum(device_hot * prior[:, None, :], axis=2)).astype(jnp.int32) + rank_local).reshape(TOKENS)
    kept = slot_index < CAP
    group_ids = (token_ids // (TOK_DEV * N_EXPERT)).astype(jnp.int32)
    table = jnp.zeros((N_DP, EXPERTS, CAP), jnp.int32).at[group_ids, chosen_ids, slot_index].set(token_ids, mode='drop')
    filled = jnp.zeros((N_DP, EXPERTS, CAP), jnp.bool_).at[group_ids, chosen_ids, slot_index].set(True, mode='drop')
    slot_safe = jnp.minimum(slot_index, CAP - 1).astype(jnp.int32)
    selected_expert_float = chosen_int.astype(jnp.float32)
    kept_float = kept.astype(jnp.float32)

    def forward(input_rows, first_gain, first_shift, query_mat, key_mat, value_mat, outer_mat, second_gain, second_shift, router_mat, embed_mat, temper_val, hidden_mat, return_mat):
        normed_one = low(layer_norm(input_rows, first_gain, first_shift))

        def heads_of(weight_mat):
            projected = jnp.dot(normed_one, weight_mat, precision=HIGHEST)
            return low_back(low(projected)).reshape(SEQS, LEN, HEADS, HEAD_DIM)
        attended = lax.map(jax.checkpoint(attend), (heads_of(query_mat), heads_of(key_mat), heads_of(value_mat), document_labels))
        attended = low_back(low(attended.reshape(TOKENS, D)))
        residual = input_rows + low_back(jnp.dot(attended, outer_mat, precision=HIGHEST))
        second_normalized = layer_norm(residual, second_gain, second_shift)
        gate = routing_gate_value(second_normalized, router_mat, embed_mat, temper_val, selected_expert_float) * kept_float
        entering = low_back(low(second_normalized))
        expert_rows = jnp.where(filled[:, :, :, None], entering[table], 0.0)
        expert_rows = jnp.moveaxis(expert_rows, 1, 0)
        produced = lax.map(jax.checkpoint(expert_apply), (expert_rows, hidden_mat, return_mat))
        per_token = produced[chosen_ids, group_ids, slot_safe]
        return residual + gate[:, None] * per_token
    primal_inputs_saved = (layer_inputs_matrix.astype(jnp.float32), mixer_layernorm_scale, mixer_layernorm_offset, asker_matrix.astype(jnp.float32), lookup_label_matrix.astype(jnp.float32), content_matrix.astype(jnp.float32), mixer_result_matrix.astype(jnp.float32), specialist_layernorm_scale, specialist_layernorm_offset, dispatch_projection_matrix, specialist_centroids, learned_sharpness, specialist_widening_matrix.astype(jnp.float32), specialist_narrowing_matrix.astype(jnp.float32))
    layer_output, pullback = jax.vjp(forward, *primal_inputs_saved)
    grads = pullback(upstream_output_sensitivity.astype(jnp.float32))
    return (layer_output.astype(jnp.bfloat16), grads[0].astype(jnp.bfloat16), grads[1], grads[2], grads[3], grads[4], grads[5], grads[6], grads[7], grads[8], grads[9], grads[10], grads[11], grads[12], grads[13])
```

```python
from functools import partial

import jax
import jax.numpy as jnp
from jax import lax
from jax.sharding import PartitionSpec as P

HEAD_DIM = 64


EPSILON = 1e-05
MASKED = -1e30


def layer_norm(values, norm_gain, norm_shift):
    centered = values - jnp.mean(values, axis=-1, keepdims=True)
    variance = jnp.mean(centered * centered, axis=-1, keepdims=True)
    return centered * lax.rsqrt(variance + EPSILON) * norm_gain + norm_shift


def routing_gate_value(normed, router_mat, embed_mat, temper_val, selected_expert):
    projected = jnp.dot(normed, router_mat, precision=lax.Precision.HIGHEST)
    unit_rows = projected * lax.rsqrt(jnp.sum(projected * projected, axis=-1, keepdims=True) + 1.0)
    unit_table = embed_mat * lax.rsqrt(jnp.sum(embed_mat * embed_mat, axis=-1, keepdims=True) + 1.0)
    logits = jnp.dot(unit_rows, unit_table.T, precision=lax.Precision.HIGHEST) / temper_val[0]
    routed = jax.nn.softmax(logits, axis=-1)
    return jnp.sum(routed * selected_expert, axis=-1)


def exact_gelu(values):
    return jax.nn.gelu(values, approximate=False)


def halves(axis):
    size = lax.axis_size(axis)
    bits = []
    mask = 1
    while mask < size:
        bits.append(mask)
        mask *= 2
    return bits


def swap(values, axis, mask):
    size = lax.axis_size(axis)
    return lax.ppermute(values, axis, [(i, i ^ mask) for i in range(size)])


def shift(values, axis, step):
    size = lax.axis_size(axis)
    return lax.ppermute(values, axis, [(i, (i + step) % size) for i in range(size)])


def pick(values, index, axis):
    return lax.dynamic_index_in_dim(values, index, axis, keepdims=False)


def scatter_sum_dp(values, order=None):
    size = lax.axis_size("dp")
    bits = halves("dp")
    place = lax.axis_index("dp")
    left = values.reshape((2,) * len(bits) + values.shape[1:])
    axes = list(reversed(bits))
    for mask in order or bits:
        axis = axes.index(mask)
        mine = (place // mask) % 2
        left = pick(left, mine, axis) + swap(pick(left, 1 - mine, axis), "dp", mask)
        axes.remove(mask)
    return left


def split_scatter_sum_dp(values):
    bits = halves("dp")
    if len(bits) != 3:
        return scatter_sum_dp(values)
    place = lax.axis_index("dp")
    left = values.reshape((2, 2, 2) + values.shape[1:])
    mine = place % 2
    left = pick(left, mine, 2) + swap(pick(left, 1 - mine, 2), "dp", 1)
    cut = values.shape[-1] // 2
    parts = []
    for order, part in (((2, 4), left[..., :cut]), ((4, 2), left[..., cut:])):
        axes = [4, 2]
        for mask in order:
            axis = axes.index(mask)
            mine = (place // mask) % 2
            part = pick(part, mine, axis) + swap(pick(part, 1 - mine, axis), "dp", mask)
            axes.remove(mask)
        parts.append(part)
    return jnp.concatenate(parts, axis=-1)


def scatter_sum_expert(values):
    size = lax.axis_size("expert")
    place = lax.axis_index("expert")
    total = pick(values, place, 0).astype(jnp.float32)
    if size > 8:
        return lax.psum_scatter(values, "expert", scatter_dimension=0, tiled=False).astype(
            jnp.float32
        )
    for step in range(1, size):
        block = pick(values, lax.rem(place + step, size), 0)
        total = total + shift(block, "expert", step).astype(jnp.float32)
    return total


def exchange(blocks, sign):
    size = lax.axis_size("expert")
    if size <= 8:
        return [blocks[0]] + [shift(blocks[k], "expert", sign * k) for k in range(1, size)]
    stacked = jnp.stack(blocks)
    place = lax.axis_index("expert")
    across = (jnp.arange(size) - place) * sign % size
    there = lax.all_to_all(stacked[across], "expert", 0, 0, tiled=True)
    source = (place - sign * jnp.arange(size)) % size
    home = there[source]
    return [home[k] for k in range(size)]


def body(
    layer_inputs_matrix,
    upstream_output_sensitivity,
    mixer_layernorm_scale,
    mixer_layernorm_offset,
    asker_matrix,
    lookup_label_matrix,
    content_matrix,
    mixer_result_matrix,
    specialist_layernorm_scale,
    specialist_layernorm_offset,
    dispatch_projection_matrix,
    specialist_centroids,
    learned_sharpness,
    specialist_widening_matrix,
    specialist_narrowing_matrix,
    document_labels,
    chosen_specialist,
    placement_ranks,
):
    rows_here, model_width = layer_inputs_matrix.shape
    seq_total, seq_len = document_labels.shape
    head_count = model_width // HEAD_DIM
    score_scale = HEAD_DIM ** (-0.5)
    group_size = lax.axis_size("expert")
    expert_total = group_size
    place = lax.axis_index("expert")
    capacity = rows_here
    slot_count = 3 * rows_here // (2 * expert_total)
    buffer_rows = expert_total * slot_count
    wide = specialist_widening_matrix[0]
    narrow = specialist_narrowing_matrix[0]
    chosen_ids = chosen_specialist[:, 0]
    expert_ids = lax.broadcasted_iota(jnp.int32, (rows_here, expert_total), 1)
    selected_expert = chosen_ids[:, None] == expert_ids
    chosen_int = selected_expert.astype(jnp.int32)
    order_row = placement_ranks[0]
    earlier_mask = (order_row[None, :] < order_row[:, None]).astype(jnp.bfloat16)
    ahead = jnp.dot(
        earlier_mask, selected_expert.astype(jnp.bfloat16), preferred_element_type=jnp.float32
    )
    rank_local = jnp.sum(jnp.where(selected_expert, ahead, 0.0), axis=-1).astype(jnp.int32)
    tallies = jnp.sum(chosen_int, axis=0)
    position = (chosen_ids - place) % group_size * slot_count + rank_local
    spots = jnp.arange(buffer_rows, dtype=jnp.int32)
    to_spots = spots[:, None] == position[None, :]
    from_spots = position[:, None] == spots[None, :]

    def send_out(rows):
        placed = jnp.dot(to_spots.astype(jnp.bfloat16), rows, preferred_element_type=jnp.float32)
        placed = placed.astype(jnp.bfloat16).reshape(expert_total, slot_count, model_width)
        return exchange([placed[k] for k in range(expert_total)], 1)

    def take_home(blocks):
        rows = jnp.concatenate(exchange(blocks, -1), axis=0)
        return jnp.dot(from_spots.astype(jnp.bfloat16), rows, preferred_element_type=jnp.float32)

    upstream_there = send_out(upstream_output_sensitivity)
    if group_size <= 8:
        prior = jnp.zeros_like(tallies)
        for step in range(1, group_size):
            prior = prior + jnp.where(place >= step, shift(tallies, "expert", step), 0)
    else:
        all_tallies = lax.all_gather(tallies, "expert")
        before = jnp.arange(group_size) < place
        prior = jnp.sum(jnp.where(before[:, None], all_tallies, 0), axis=0)
    slot_index = jnp.sum(chosen_int * prior[None, :], axis=-1) + rank_local
    kept_float = (slot_index < capacity).astype(jnp.float32)

    inputs = layer_inputs_matrix.astype(jnp.float32)
    normed_one, norm_one_back = jax.vjp(
        layer_norm, inputs, mixer_layernorm_scale, mixer_layernorm_offset
    )
    normed_low = normed_one.astype(jnp.bfloat16)

    def heads_of(weight_mat):
        projected = jnp.dot(normed_low, weight_mat, preferred_element_type=jnp.float32)
        return projected.astype(jnp.bfloat16).reshape(seq_total, seq_len, head_count, HEAD_DIM)

    queries = heads_of(asker_matrix)
    keys_low = heads_of(lookup_label_matrix)
    values_low = heads_of(content_matrix)
    allowed = (document_labels[:, :, None] == document_labels[:, None, :])[:, None]

    def raw_scores():
        scores = (
            jnp.einsum("sqhd,skhd->shqk", queries, keys_low, preferred_element_type=jnp.float32)
            * score_scale
        )
        return jnp.where(allowed, scores, MASKED)

    scores = raw_scores()
    largest = jnp.max(scores, axis=-1, keepdims=True)
    weights = jnp.exp(scores - largest)
    log_total = largest + jnp.log(jnp.sum(weights, axis=-1, keepdims=True))
    probs = jnp.exp(scores - log_total)
    attended = jnp.einsum(
        "shqk,skhd->sqhd",
        probs.astype(jnp.bfloat16),
        values_low,
        preferred_element_type=jnp.float32,
    )
    attended_low = attended.astype(jnp.bfloat16).reshape(rows_here, model_width)
    residual = inputs + jnp.dot(
        attended_low, mixer_result_matrix, preferred_element_type=jnp.float32
    )
    second_normalized, norm_two_back = jax.vjp(
        layer_norm, residual, specialist_layernorm_scale, specialist_layernorm_offset
    )
    entering = second_normalized.astype(jnp.bfloat16)
    entering_there = send_out(entering)
    selected_expert_float = selected_expert.astype(jnp.float32)
    gate, dispatcher_reverse = jax.vjp(
        partial(routing_gate_value, selected_expert=selected_expert_float),
        second_normalized,
        dispatch_projection_matrix,
        specialist_centroids,
        learned_sharpness,
    )
    weighted = gate * kept_float
    weight_spots = jnp.sum(jnp.where(to_spots, weighted[None, :], 0.0), axis=1)
    weight_spots = weight_spots.reshape(expert_total, slot_count)
    weight_there = exchange([weight_spots[k] for k in range(expert_total)], 1)

    ways = 4 if group_size == 4 else 1
    each = group_size // ways

    def gather_up(blocks):
        return [jnp.concatenate(blocks[k * each : (k + 1) * each]) for k in range(ways)]

    entered, graded, weighed = map(gather_up, (entering_there, upstream_there, weight_there))
    produced, returned, gate_parts, actives, pres = [], [], [], [], []
    for rows, grads in zip(entered, graded):
        hidden_pre = jnp.dot(rows, wide, preferred_element_type=jnp.float32)
        active, gelu_back = jax.vjp(exact_gelu, hidden_pre)
        active = active.astype(jnp.bfloat16)
        out = jnp.dot(active, narrow, preferred_element_type=jnp.float32)
        out = out.astype(jnp.bfloat16)
        gate_parts.append(jnp.sum(out.astype(jnp.float32) * grads.astype(jnp.float32), axis=-1))
        produced.append(out)
        active_grad = jnp.dot(grads, narrow.T, preferred_element_type=jnp.float32)
        pre_grad = gelu_back(active_grad)[0].astype(jnp.bfloat16)
        back = jnp.dot(pre_grad, wide.T, preferred_element_type=jnp.float32)
        returned.append(back.astype(jnp.bfloat16))
        actives.append(active)
        pres.append(pre_grad)

    def spread(chunks):
        return [chunk.reshape((each, -1) + chunk.shape[1:])[k] for chunk in chunks for k in range(each)]

    expert_input_grad = take_home(spread(returned))
    gate_rows = jnp.concatenate(exchange(spread(gate_parts), -1))
    gate_home = jnp.sum(jnp.where(from_spots, gate_rows[None, :], 0.0), axis=1)
    hidden_full = sum(
        jnp.dot(
            (rows.astype(jnp.float32) * w[:, None]).astype(jnp.bfloat16).T,
            p,
            preferred_element_type=jnp.float32,
        )
        for rows, w, p in zip(entered, weighed, pres)
    )
    return_full = sum(
        jnp.dot(
            a.T,
            (rows.astype(jnp.float32) * w[:, None]).astype(jnp.bfloat16),
            preferred_element_type=jnp.float32,
        )
        for rows, w, a in zip(graded, weighed, actives)
    )
    dp_size = lax.axis_size("dp")

    def expert_sum(full):
        blocks = full.astype(jnp.bfloat16).reshape((dp_size, -1) + full.shape[1:])
        return split_scatter_sum_dp(blocks).astype(jnp.float32)[None]

    hidden_grad = expert_sum(hidden_full)
    return_grad = expert_sum(return_full)
    per_token = take_home(spread(produced))
    layer_output = (residual + weighted[:, None] * per_token).astype(jnp.bfloat16)

    upstream = upstream_output_sensitivity.astype(jnp.float32)
    dispatcher_piece, dispatcher_complete, centroid_picked, sharpness_picked = dispatcher_reverse(
        gate_home * kept_float
    )
    two_part, routegain_full, routeshift_full = norm_two_back(
        expert_input_grad * weighted[:, None] + dispatcher_piece
    )
    residual_grad = upstream + two_part
    branch_grad = residual_grad.astype(jnp.bfloat16)
    outer_full = jnp.dot(attended_low.T, branch_grad, preferred_element_type=jnp.float32)
    attended_grad = jnp.dot(branch_grad, mixer_result_matrix.T, preferred_element_type=jnp.float32)
    attended_grad = attended_grad.astype(jnp.bfloat16).reshape(
        seq_total, seq_len, head_count, HEAD_DIM
    )
    probs = jnp.exp(raw_scores() - log_total)
    prob_grad = jnp.einsum(
        "sqhd,skhd->shqk", attended_grad, values_low, preferred_element_type=jnp.float32
    )
    values_grad = jnp.einsum(
        "shqk,sqhd->skhd",
        probs.astype(jnp.bfloat16),
        attended_grad,
        preferred_element_type=jnp.float32,
    )
    values_grad = values_grad.astype(jnp.bfloat16).reshape(rows_here, model_width)
    centered_grad = jnp.sum(prob_grad * probs, axis=-1, keepdims=True)
    score_grad = (probs * (prob_grad - centered_grad)).astype(jnp.bfloat16)
    queries_grad = (
        jnp.einsum("shqk,skhd->sqhd", score_grad, keys_low, preferred_element_type=jnp.float32)
        * score_scale
    )
    queries_grad = queries_grad.astype(jnp.bfloat16).reshape(rows_here, model_width)
    keys_grad = (
        jnp.einsum("shqk,sqhd->skhd", score_grad, queries, preferred_element_type=jnp.float32)
        * score_scale
    )
    keys_grad = keys_grad.astype(jnp.bfloat16).reshape(rows_here, model_width)
    query_full = jnp.dot(normed_low.T, queries_grad, preferred_element_type=jnp.float32)
    key_full = jnp.dot(normed_low.T, keys_grad, preferred_element_type=jnp.float32)
    value_full = jnp.dot(normed_low.T, values_grad, preferred_element_type=jnp.float32)
    one_grad = jnp.dot(queries_grad, asker_matrix.T, preferred_element_type=jnp.float32)
    one_grad = one_grad + jnp.dot(
        keys_grad, lookup_label_matrix.T, preferred_element_type=jnp.float32
    )
    one_grad = one_grad + jnp.dot(values_grad, content_matrix.T, preferred_element_type=jnp.float32)
    one_part, attngain_full, attnshift_full = norm_one_back(one_grad)
    tokens_grad = (residual_grad + one_part).astype(jnp.bfloat16)

    def full_sum(full):
        low = full.astype(jnp.bfloat16)
        blocks = low.reshape((dp_size, group_size, -1) + full.shape[1:])
        return scatter_sum_expert(split_scatter_sum_dp(blocks))

    outer_grad = full_sum(outer_full)
    query_grad = full_sum(query_full)
    key_grad = full_sum(key_full)
    value_grad = full_sum(value_full)
    small = jnp.concatenate(
        [
            dispatcher_complete.reshape(-1),
            routegain_full,
            routeshift_full,
            centroid_picked.reshape(-1),
            sharpness_picked,
        ]
    )
    small = lax.psum(small, ("dp", "expert"))
    norms = lax.psum(jnp.stack([attngain_full, attnshift_full]), ("dp", "expert"))
    devices = dp_size * group_size
    here = lax.axis_index("dp") * group_size + place
    own = model_width // devices
    route = dispatch_projection_matrix.shape[1]
    router_total = small[: model_width * route].reshape(model_width, route)
    rest = small[model_width * route :]
    mine = lambda vector, axis=0: lax.dynamic_slice_in_dim(vector, here * own, own, axis)
    centroid_total = rest[2 * model_width : 2 * model_width + expert_total * route]
    return (
        layer_output,
        tokens_grad,
        mine(norms[0]),
        mine(norms[1]),
        query_grad,
        key_grad,
        value_grad,
        outer_grad,
        mine(rest[:model_width]),
        mine(rest[model_width : 2 * model_width]),
        mine(router_total),
        centroid_total.reshape(expert_total, route),
        rest[2 * model_width + expert_total * route :],
        hidden_grad,
        return_grad,
    )


def solution(mesh):
    placed = (
        P(("dp", "expert"), None),
        P(("dp", "expert"), None),
        P(),
        P(),
        P(),
        P(),
        P(),
        P(),
        P(),
        P(),
        P(),
        P(),
        P(),
        P("expert", None, None),
        P("expert", None, None),
        P(("dp", "expert"), None),
        P(("dp", "expert"), None),
        P(("dp", "expert"), None),
    )
    return jax.shard_map(
        body,
        mesh=mesh,
        in_specs=placed,
        out_specs=(
            P(("dp", "expert"), None),
            P(("dp", "expert"), None),
            P(("dp", "expert")),
            P(("dp", "expert")),
            P(("dp", "expert"), None),
            P(("dp", "expert"), None),
            P(("dp", "expert"), None),
            P(("dp", "expert"), None),
            P(("dp", "expert")),
            P(("dp", "expert")),
            P(("dp", "expert"), None),
            P(),
            P(),
            P("expert", "dp", None),
            P("expert", "dp", None),
        ),
        check_vma=False,
    )
```

```python
from functools import partial

import jax
import jax.numpy as jnp
from jax import lax
from jax.experimental import pallas as pl
from jax.experimental.pallas import tpu as pltpu
from jax.sharding import PartitionSpec as P

HEAD_DIM = 64
EPSILON = 1e-05
MASKED = -1e30
BF = jnp.bfloat16
F32 = jnp.float32
VMEM_LIMIT = 56 * 1024 * 1024
TAIL = 16
COST = 1
NN = (((1,), (0,)), ((), ()))
NT = (((1,), (1,)), ((), ()))
TN = (((0,), (0,)), ((), ()))


def mxu(left, right, dims=NN):
    return lax.dot_general(left, right, dims, preferred_element_type=F32)


def split_high(values):
    high = values.astype(BF)
    low = (values - high.astype(F32)).astype(BF)
    return high, low


def mxu_wide(left, right, dims=NN):
    left_high, left_low = split_high(left)
    right_high, right_low = split_high(right)
    return (
        mxu(left_high, right_high, dims)
        + mxu(left_high, right_low, dims)
        + mxu(left_low, right_high, dims)
    )


def kernel_call(body, cost, deps=(), **kwargs):
    deps = jax.tree.leaves(deps)
    inputs = len(kwargs["in_specs"])
    kwargs["in_specs"] = list(kwargs["in_specs"]) + [pl.BlockSpec(memory_space=pl.ANY)] * len(deps)

    def run(*refs):
        body(*refs[:inputs], *refs[inputs + len(deps) :])

    call = pl.pallas_call(
        run,
        compiler_params=pltpu.CompilerParams(
            vmem_limit_bytes=VMEM_LIMIT,
            dimension_semantics=("arbitrary",) * len(kwargs.get("grid", ())),
        ),
        cost_estimate=pl.CostEstimate(flops=cost[0] // COST, bytes_accessed=cost[1] // COST, transcendentals=0),
        **kwargs,
    )
    return lambda *args: call(*args, *deps)


def whole(shape):
    return pl.BlockSpec(shape, lambda *_: (0,) * len(shape))


def route_kernel(slots, place_ref, order_ref, chosen_ref, rows_ref, pos_ref, rank_ref, sent_ref):
    group = sent_ref.shape[0]
    order = order_ref[...].astype(F32)
    count = order.shape[1]
    chosen = chosen_ref[...]
    chosen_wide = jnp.transpose(jnp.broadcast_to(chosen.astype(F32), (128, count)))
    order_col = jnp.transpose(jnp.broadcast_to(order, (128, count)))[:, :1]
    before = (order_col < order) & (chosen_wide[:, :1] == chosen.astype(F32))
    rank = jnp.sum(before.astype(F32), axis=0, keepdims=True).astype(jnp.int32)
    place = place_ref[0]
    pos = jnp.where(chosen >= place, chosen - place, chosen - place + group) * slots + rank
    pos_ref[...] = pos
    rank_ref[...] = rank
    lanes = lax.broadcasted_iota(jnp.int32, (count, 128), 1).astype(F32)
    rows = rows_ref[...]
    tally = jnp.sum((chosen_wide == lanes).astype(F32), axis=0, keepdims=True)
    upper = jnp.floor(tally * (1.0 / 256.0))
    place_row = lax.broadcasted_iota(jnp.int32, (TAIL, 128), 0)
    tail = jnp.where(place_row == 0, upper, jnp.where(place_row == 1, tally - 256.0 * upper, 0.0))
    tail = jnp.concatenate([tail, jnp.zeros((TAIL, rows.shape[1] - 128), F32)], axis=1).astype(BF)
    for k in range(group):
        spots = lax.broadcasted_iota(jnp.int32, (slots, count), 0) + k * slots
        sent_ref[k, :slots, :] = mxu((spots == chosen * slots + rank).astype(F32).astype(BF), rows).astype(BF)
        sent_ref[k, slots:, :] = tail


def norm_of(values, gain, shift):
    centered = values - jnp.mean(values, axis=-1, keepdims=True)
    scale = lax.rsqrt(jnp.mean(centered * centered, axis=-1, keepdims=True) + EPSILON)
    unit = centered * scale
    return unit, scale, unit * gain + shift


def router_of(projected, table, temper):
    scale = lax.rsqrt(jnp.sum(projected * projected, axis=0, keepdims=True) + 1.0)
    unit = projected * scale
    table_scale = lax.rsqrt(jnp.sum(table * table, axis=1, keepdims=True) + 1.0)
    unit_table = table * table_scale
    logits = lax.dot_general(
        unit_table, unit, NN, precision=lax.Precision.HIGHEST, preferred_element_type=F32
    ) / temper
    return scale, unit, table_scale, unit_table, logits


def softmax_rows(logits, experts):
    valid = lax.broadcasted_iota(jnp.int32, logits.shape, 0) < experts
    logits = jnp.where(valid, logits, MASKED)
    weights = jnp.exp(logits - jnp.max(logits, axis=0, keepdims=True))
    return weights / jnp.sum(weights, axis=0, keepdims=True)


def same_label(label_ref):
    labels = label_ref[0].astype(F32)
    column = jnp.transpose(jnp.broadcast_to(labels, (128, labels.shape[1])))[:, :1]
    return jnp.where(column == labels, 0.0, MASKED)


def attend_kernel(experts, slots, x_ref, label_ref, gain_one_ref, shift_one_ref, wq_ref,
                  wk_ref, wv_ref, wo_ref, gain_two_ref, shift_two_ref, router_ref, table_ref, temper_ref,
                  chosen_ref, pos_ref, turned_ref, q_ref, k_ref, v_ref, att_ref, lse_ref, residual_ref,
                  projected_ref, *rest):
    sent_refs, bias_ref, lse_cols_ref = rest[:-2], rest[-2], rest[-1]
    step = pl.program_id(0)
    x = x_ref[...].astype(F32)
    rows, width = x.shape
    normed = norm_of(x, gain_one_ref[...], shift_one_ref[...])[2].astype(BF)
    turned_ref[...] = jnp.transpose(normed)
    q_ref[...] = (mxu(normed, wq_ref[...]).astype(BF).astype(F32) * HEAD_DIM ** (-0.5)).astype(BF)
    k_ref[...] = mxu(normed, wk_ref[...]).astype(BF)
    v_ref[...] = mxu(normed, wv_ref[...]).astype(BF)
    bias_ref[...] = same_label(label_ref)
    lane = lax.broadcasted_iota(jnp.int32, (rows, 128), 1)
    low_lanes = lane < HEAD_DIM
    lse_cols = jnp.zeros((rows, 128), F32)
    for pair in range(width // 128):
        columns = slice(pair * 128, pair * 128 + 128)
        q_pair, k_pair, v_pair = q_ref[:, columns], k_ref[:, columns], v_ref[:, columns]
        outs = []
        for half in range(2):
            own = low_lanes if half == 0 else jnp.logical_not(low_lanes)
            q_own = jnp.where(own, q_pair.astype(F32), 0.0).astype(BF)
            scores = mxu(q_own, k_pair, NT) + bias_ref[...]
            largest = jnp.max(scores, axis=-1, keepdims=True)
            weights = jnp.exp(scores - largest)
            total = jnp.sum(weights, axis=-1, keepdims=True)
            outs.append(mxu(weights.astype(BF), v_pair) * (1.0 / total))
            lse_cols = jnp.where(lane == pair * 2 + half, largest + jnp.log(total), lse_cols)
        att_ref[:, columns] = jnp.where(low_lanes, outs[0], outs[1]).astype(BF)
    lse_cols_ref[...] = lse_cols
    lse_ref[...] = jnp.transpose(lse_cols_ref[...])[: lse_ref.shape[0]]
    residual = x + mxu(att_ref[...], wo_ref[...])
    residual_ref[...] = residual
    normed_two = norm_of(residual, gain_two_ref[...], shift_two_ref[...])[2]
    projected = lax.dot_general(
        router_ref[...], normed_two, NT, precision=lax.Precision.HIGHEST, preferred_element_type=F32
    )
    projected_ref[...] = projected
    logits = router_of(projected, table_ref[...], temper_ref[0])[4]
    routed = softmax_rows(logits, experts)
    selected = chosen_ref[...] == lax.broadcasted_iota(jnp.int32, logits.shape, 0)
    gate = jnp.sum(jnp.where(selected, routed, 0.0), axis=0, keepdims=True)
    high = gate.astype(BF).astype(F32)
    mid = (gate - high).astype(BF).astype(F32)
    low = gate - high - mid
    place = lax.broadcasted_iota(jnp.int32, (TAIL, rows), 0)
    pieces = jnp.where(place == 0, high, jnp.where(place == 1, mid, jnp.where(place == 2, low, 0.0)))
    pieces = pieces.astype(BF)
    entering = normed_two.astype(BF)
    pos = pos_ref[...]
    for k in range(len(sent_refs)):
        spots = lax.broadcasted_iota(jnp.int32, (slots, rows), 0) + k * slots
        here = (spots == pos).astype(F32).astype(BF)
        sent = mxu(here, entering)
        gates = mxu(pieces, here, NT)
        tail = jnp.concatenate([gates, jnp.zeros((TAIL, width - slots), F32)], axis=1)

        @pl.when(step == 0)
        def _():
            sent_refs[k][:slots, :] = sent.astype(BF)
            sent_refs[k][slots:, :] = tail.astype(BF)

        @pl.when(step > 0)
        def _():
            sent_refs[k][:slots, :] = (sent_refs[k][:slots, :].astype(F32) + sent).astype(BF)
            sent_refs[k][slots:, :] = (sent_refs[k][slots:, :].astype(F32) + tail).astype(BF)


def gelu_parts(values):
    share = 0.5 * lax.erf(values * 0.5**0.5) + 0.5
    return share, jnp.exp(values * values * (-0.5)) * (2.0 * 3.141592653589793) ** (-0.5)


def pack_offsets(counts_ref, ids):
    offsets, total = [], 0
    for k in ids:
        offsets.append(pl.multiple_of(total, 16))
        total = total + (counts_ref[k] + 15) // 16 * 16
    return offsets, total


def source_of(place_ref, k, group):
    return lax.rem(place_ref[0] - k + group, group)


def expert_kernel(ids, earlier, block, counts_ref, place_ref, u_ref, *refs):
    chunks = len(ids)
    x_refs = refs[:chunks]
    wide_ref, narrow_ref = refs[chunks : chunks + 2]
    past_refs = refs[chunks + 2 : chunks + 2 + (len(earlier) > 0)]
    rest = refs[chunks + 2 + len(past_refs) :]
    out_ref, back_refs = rest[0], rest[1 : 1 + chunks]
    act_ref, pre_ref, xs, us, out_sum, back_sum, sums = rest[1 + chunks :]
    step, steps = pl.program_id(0), pl.num_programs(0)
    rows = x_refs[0].shape[0] - TAIL
    offsets, total = pack_offsets(counts_ref, ids)

    @pl.when(step == 0)
    def _():
        xs[...] = jnp.zeros_like(xs)
        us[...] = jnp.zeros_like(us)
        out_sum[...] = jnp.zeros_like(out_sum)
        back_sum[...] = jnp.zeros_like(back_sum)
        for k in range(chunks):
            xs[pl.ds(offsets[k], rows), :] = x_refs[k][:rows, :]
            us[pl.ds(offsets[k], rows), :] = u_ref[source_of(place_ref, ids[k], u_ref.shape[0]), :rows, :]

    def one(i, carry):
        here = pl.ds(pl.multiple_of(i * block, block), block)
        wide, narrow = wide_ref[...], narrow_ref[...]
        hidden = mxu(xs[here, :], wide)
        grad = mxu(us[here, :], narrow, NT)
        share, density = gelu_parts(hidden)
        act = (hidden * share).astype(BF)
        act_ref[here, :] = act
        pre = (grad * (share + hidden * density)).astype(BF)
        pre_ref[here, :] = pre
        out_sum[here, :] += mxu(act, narrow)
        back_sum[here, :] += mxu(pre, wide, NT)
        return carry

    blocks = (total + block - 1) // block
    lax.fori_loop(0, blocks, one, 0)

    def none(i, carry):
        here = pl.ds(pl.multiple_of(i * block, block), block)
        act_ref[here, :] = jnp.zeros((block, act_ref.shape[1]), BF)
        pre_ref[here, :] = jnp.zeros((block, pre_ref.shape[1]), BF)
        return carry

    lax.fori_loop(blocks, act_ref.shape[0] // block, none, 0)

    @pl.when(step == steps - 1)
    def _():
        for past_ref in past_refs:
            for k in earlier:
                at = source_of(place_ref, k, u_ref.shape[0])
                out_ref[at] = past_ref[at]
        out = out_sum[...].astype(BF).astype(F32)
        gates = jnp.sum(out * us[...].astype(F32), axis=1, keepdims=True)
        sums[...] = jnp.broadcast_to(gates, sums.shape)
        for k in range(chunks):
            here = pl.ds(offsets[k], rows)
            out_ref[source_of(place_ref, ids[k], u_ref.shape[0])] = out_sum[here, :].astype(BF)
            back_refs[k][:rows, :] = back_sum[here, :].astype(BF)
            gate = jnp.transpose(sums[here, :])[:1]
            high = gate.astype(BF).astype(F32)
            mid = (gate - high).astype(BF).astype(F32)
            place = lax.broadcasted_iota(jnp.int32, (TAIL, rows), 0)
            tail = jnp.where(place == 0, high, jnp.where(place == 1, mid, jnp.where(place == 2, gate - high - mid, 0.0)))
            tail = jnp.concatenate([tail, jnp.zeros((TAIL, out.shape[1] - rows), F32)], axis=1)
            back_refs[k][rows:, :] = tail.astype(BF)


def expert_call(counts, place, ids, earlier, past, xs, us, wide, narrow, deps, block=384, parts=4):
    chunks, (tailed, width), hidden = len(xs), xs[0].shape, wide.shape[1]
    rows = tailed - TAIL
    cut, most = hidden // parts, chunks * rows
    sd = jax.ShapeDtypeStruct
    smem = pl.BlockSpec(memory_space=pltpu.SMEM)
    chunk, every = whole((tailed, width)), (us.shape[0], rows, width)
    inner = pl.BlockSpec((most, cut), lambda f: (0, f))
    out, *rest = kernel_call(
        partial(expert_kernel, ids, earlier, block),
        (8 * most * width * hidden * 3 // 4, 4 * width * hidden + 4 * most * hidden),
        deps,
        grid=(parts,),
        in_specs=[smem] * 2 + [whole(us.shape)] + [chunk] * chunks
        + [pl.BlockSpec((width, cut), lambda f: (0, f)), pl.BlockSpec((cut, width), lambda f: (f, 0))]
        + [whole(every)] * len(past),
        out_specs=[whole(every)] + [chunk] * chunks + [inner, inner],
        out_shape=[sd(every, BF)] + [sd((tailed, width), BF)] * chunks + [sd((most, hidden), BF)] * 2,
        scratch_shapes=[pltpu.VMEM((most, width), BF)] * 2
        + [pltpu.VMEM((most, width), F32)] * 2 + [pltpu.VMEM((most, 128), F32)],
    )(counts, place, us, *xs, wide, narrow, *past)
    return out, rest[:chunks], rest[chunks], rest[chunks + 1]


def pack_weighed(ids, counts_ref, x_refs, rows_of, depth, packed_ref, turned_ref):
    rows = x_refs[0].shape[0] - TAIL
    offsets, _ = pack_offsets(counts_ref, ids)
    packed_ref[...] = jnp.zeros_like(packed_ref)
    lanes = lax.broadcasted_iota(jnp.int32, (128, rows), 1)
    for k in range(len(ids)):
        gates = jnp.sum(x_refs[k][rows:, :rows].astype(F32), axis=0, keepdims=True)
        gates = jnp.where(lanes < counts_ref[ids[k]], gates, 0.0)
        gates = jnp.transpose(gates)[:, :1]
        packed_ref[pl.ds(offsets[k], rows), :] = (rows_of(k).astype(F32) * gates).astype(BF)
    turned_ref[...] = jnp.transpose(packed_ref[:depth])


def pack_units(sets, counts_ref, part_refs, packed_ref):
    offsets, _ = pack_offsets(counts_ref, sum(sets, ()))
    first = 0
    for part, part_ref in zip(sets, part_refs):
        packed_ref[pl.ds(offsets[first], part_ref.shape[0]), :] = part_ref[...]
        first += len(part)


def wide_kernel(sets, depth, counts_ref, spot_ref, *refs):
    ids = sum(sets, ())
    x_refs, pre_refs = refs[: len(ids)], refs[len(ids) : len(ids) + len(sets)]
    keep_ref, send_ref, packed, turned, pres = refs[len(ids) + len(sets) :]
    rows = x_refs[0].shape[0] - TAIL

    @pl.when(pl.program_id(0) == 0)
    def _():
        pres[...] = jnp.zeros_like(pres)
        pack_weighed(ids, counts_ref, x_refs, lambda k: x_refs[k][:rows, :], depth, packed, turned)

    pack_units(sets, counts_ref, pre_refs, pres)
    put_halves(spot_ref[0], keep_ref, send_ref, slice(None), mxu(turned[...], pres[:depth]).astype(BF))


def narrow_kernel(sets, depth, counts_ref, spot_ref, place_ref, u_ref, *refs):
    ids = sum(sets, ())
    x_refs, act_refs = refs[: len(ids)], refs[len(ids) : len(ids) + len(sets)]
    keep_ref, send_ref, packed, turned, acts = refs[len(ids) + len(sets) :]
    rows = x_refs[0].shape[0] - TAIL
    step = pl.program_id(0)

    @pl.when(step == 0)
    def _():
        acts[...] = jnp.zeros_like(acts)
        rows_of = lambda k: u_ref[source_of(place_ref, ids[k], u_ref.shape[0]), :rows, :]
        pack_weighed(ids, counts_ref, x_refs, rows_of, depth, packed, turned)

    pack_units(sets, counts_ref, act_refs, acts)
    narrow = mxu(turned[...], acts[:depth]).astype(BF)
    spot = spot_ref[0]
    cut = keep_ref.shape[2]
    count = narrow.shape[1] // cut
    for k in range(count):
        part = narrow[:, k * cut : (k + 1) * cut]
        at = (step * count + k) // 2 ^ (spot // 2)

        @pl.when(spot % 2 == k % 2)
        def _():
            keep_ref[at] = part

        @pl.when(spot % 2 != k % 2)
        def _():
            send_ref[at] = part


def weight_calls(counts, spot, place, sets, xs, us, acts, pres, blocks, depth, deps, parts=4):
    chunks, (tailed, width), hidden = len(xs), xs[0].shape, acts[0].shape[1]
    half = blocks // 2
    cut, most = hidden // parts, chunks * (tailed - TAIL)
    smem = pl.BlockSpec(memory_space=pltpu.SMEM)
    inner = [pl.BlockSpec((act.shape[0], cut), lambda f: (0, f)) for act in acts]
    common = dict(
        cost=(2 * depth * width * hidden, 2 * width * hidden + 2 * most * hidden),
        grid=(parts,),
        scratch_shapes=[pltpu.VMEM((most, width), BF), pltpu.VMEM((width, depth), BF), pltpu.VMEM((most, cut), BF)],
    )
    chunk_specs = [whole((tailed, width))] * chunks
    wide = kernel_call(
        partial(wide_kernel, sets, depth),
        in_specs=[smem] * 2 + chunk_specs + inner,
        out_specs=[pl.BlockSpec((half, width // blocks, cut), lambda f: (0, 0, f))] * 2,
        out_shape=[jax.ShapeDtypeStruct((half, width // blocks, hidden), BF)] * 2,
        **common,
    )(counts, spot, *xs, *pres)
    narrow = kernel_call(
        partial(narrow_kernel, sets, depth),
        deps=[deps, wide],
        in_specs=[smem] * 3 + [whole(us.shape)] + chunk_specs + inner,
        out_specs=[whole((half, width, hidden // blocks))] * 2,
        out_shape=[jax.ShapeDtypeStruct((half, width, hidden // blocks), BF)] * 2,
        **common,
    )(counts, spot, place, us, *xs, *acts)
    return *wide, *narrow


def weight_first_kernel(keep_wide, came_wide, keep_narrow, came_narrow, *out_refs):
    rows, hidden = keep_wide.shape[1:]
    cut = keep_narrow.shape[2]
    for k, out_ref in enumerate(out_refs):
        out_ref[:, :hidden] = (keep_wide[k].astype(F32) + came_wide[k].astype(F32)).astype(BF)
        for slab in range(keep_narrow.shape[1] // rows):
            here = slice(slab * rows, (slab + 1) * rows)
            total = keep_narrow[k, here, :].astype(F32) + came_narrow[k, here, :].astype(F32)
            out_ref[:, hidden + slab * cut : hidden + (slab + 1) * cut] = total.astype(BF)


def weight_last_kernel(cut, *refs):
    wide_ref, narrow_ref = refs[-2:]
    rows, hidden = wide_ref.shape
    total = sum(ref[...].astype(F32) for ref in refs[:-2])
    wide_ref[...] = total[:, :hidden]
    for slab in range(narrow_ref.shape[1] // rows):
        piece = total[:, hidden + slab * cut : hidden + (slab + 1) * cut]
        narrow_ref[:, slab * rows : (slab + 1) * rows] = jnp.transpose(piece)


def as_column(row):
    return jnp.transpose(jnp.broadcast_to(row, (128, row.shape[1])))[:, :1]


def weight_row(gate, chosen, rank, prior, experts_padded, capacity):
    shape = (experts_padded, chosen.shape[1])
    selected = chosen == lax.broadcasted_iota(jnp.int32, shape, 0)
    before = jnp.sum(jnp.where(selected, prior, 0), axis=0, keepdims=True)
    return selected, (before + rank < capacity).astype(F32)


def put_halves(spot, keep_ref, send_ref, columns, values):
    half, rows = keep_ref.shape[:2]
    for block in range(2 * half):
        part = values[block * rows : (block + 1) * rows]

        @pl.when(spot % 2 == block % 2)
        def _():
            keep_ref[(block // 2) ^ (spot // 2), :, columns] = part

        @pl.when(spot % 2 != block % 2)
        def _():
            send_ref[(block // 2) ^ (spot // 2), :, columns] = part


EXACT = 32


def split_exact(values):
    lane = lax.broadcasted_iota(jnp.int32, values.shape, 1)
    high = values.astype(BF).astype(F32)
    mid = (values - high).astype(BF).astype(F32)
    low = values - high - mid
    band = (lane - EXACT) // 16
    mid, low = pltpu.roll(mid, 16, 1), pltpu.roll(low, 32, 1)
    return jnp.where(band == 0, high, jnp.where(band == 1, mid, jnp.where(band == 2, low, values)))


def join_exact(values):
    lane = lax.broadcasted_iota(jnp.int32, values.shape, 1)
    total = values + pltpu.roll(values, 128 - 16, 1) + pltpu.roll(values, 128 - 32, 1)
    return jnp.where((lane >= EXACT) & (lane < EXACT + 16), total, values)


def home_kernel(experts, slots, capacity, chunks, extra_rows, temper_ref, prior_ref, chosen_ref, rank_ref, pos_ref,
                residual_ref, upstream_ref, att_ref, projected_ref, table_ref, router_ref, gain_ref, shift_ref,
                wo_ref, heads_ref, *refs):
    back_refs = refs[:chunks]
    (weight_ref, grad_ref, att_grad_ref, delta_ref, outer_ref, extra_ref, tiny_ref,
     _, spots_ref, outer_sum, extra_sum, table_sum) = refs[chunks + 1 :]
    step, steps = pl.program_id(0), pl.num_programs(0)
    slots_all = spots_ref.shape[0]
    rows, width = residual_ref.shape
    route = projected_ref.shape[0]

    @pl.when(step == 0)
    def _():
        outer_sum[...] = jnp.zeros_like(outer_sum)
        extra_sum[...] = jnp.zeros_like(extra_sum)
        table_sum[...] = jnp.zeros_like(table_sum)
        for k in range(chunks):
            spots_ref[k * slots : (k + 1) * slots, :] = back_refs[k][:slots, :]

    temper = temper_ref[0]
    table = table_ref[...]
    projected = projected_ref[...]
    scale, unit, table_scale, unit_table, logits = router_of(projected, table, temper)
    routed = softmax_rows(logits, experts)
    selected, kept = weight_row(None, chosen_ref[...], rank_ref[...], prior_ref[...], table.shape[0], capacity)
    gate = jnp.sum(jnp.where(selected, routed, 0.0), axis=0, keepdims=True)
    weight = gate * kept
    weight_ref[...] = weight
    pos = pos_ref[...]
    gate_grad = jnp.zeros((1, rows), F32)
    for k in range(chunks):
        here = (lax.broadcasted_iota(jnp.int32, (slots, rows), 0) + k * slots == pos).astype(F32).astype(BF)
        gate_grad += jnp.sum(mxu(back_refs[k][slots:, :slots], here), axis=0, keepdims=True)
    gate_grad = gate_grad * kept
    logit_grad = gate_grad * routed * (selected.astype(F32) - gate)
    highest = dict(precision=lax.Precision.HIGHEST, preferred_element_type=F32)
    unit_grad = lax.dot_general(unit_table, logit_grad, TN, **highest) / temper
    table_sum[:, :route] += lax.dot_general(logit_grad, unit, NT, **highest) / temper
    sharp = -jnp.sum(logit_grad * logits, keepdims=True) / temper
    projected_grad = scale * unit_grad - scale * scale * scale * projected * jnp.sum(
        projected * unit_grad, axis=0, keepdims=True
    )
    padded = jnp.concatenate([projected_grad, jnp.zeros((128 - route, rows), F32)], axis=0)
    route_part = mxu_wide(jnp.transpose(padded), router_ref[...])
    column = pos.astype(F32)
    both = jnp.concatenate([column, weight, jnp.zeros((126, rows), F32)], axis=0)
    both = jnp.transpose(both)
    pos_column, weight_column = both[:, :1].astype(jnp.int32), both[:, 1:2]
    lanes = lax.broadcasted_iota(jnp.int32, (rows, slots_all), 1)
    home = mxu((lanes == pos_column).astype(F32).astype(BF), spots_ref[...])
    y_grad = home * weight_column + route_part
    unit_two, norm_scale, normed_two = norm_of(residual_ref[...], gain_ref[...], shift_ref[...])
    inner = y_grad * gain_ref[...]
    two_part = norm_scale * (
        inner
        - jnp.mean(inner, axis=-1, keepdims=True)
        - unit_two * jnp.mean(inner * unit_two, axis=-1, keepdims=True)
    )
    residual_grad = upstream_ref[...].astype(F32) + two_part
    grad_ref[...] = residual_grad
    branch = residual_grad.astype(BF)
    att = att_ref[...]
    outer_sum[...] += mxu(jnp.transpose(att), branch)
    att_grad = mxu(branch, wo_ref[...], NT).astype(BF)
    att_grad_ref[...] = att_grad
    product_high, product_low = split_high(att_grad.astype(F32) * att.astype(F32))
    heads = heads_ref[...]
    delta_ref[...] = mxu(heads, product_high, NT) + mxu(heads, product_low, NT)
    extra_sum[:route, :] += mxu_wide(projected_grad, normed_two)
    extra_sum[route : route + 1, :] += jnp.sum(y_grad * unit_two, axis=0, keepdims=True)
    extra_sum[route + 1 : route + 2, :] += jnp.sum(y_grad, axis=0, keepdims=True)
    extra_sum[route + 2 : route + 3, :128] += jnp.broadcast_to(sharp, (1, 128))

    @pl.when(step == steps - 1)
    def _():
        table_grad = table_sum[...]
        wide_table = jnp.concatenate([table, jnp.zeros((table.shape[0], 128 - route), F32)], axis=1)
        summed = jnp.sum(wide_table * table_grad, axis=1, keepdims=True)
        table_grad = table_scale * table_grad - table_scale * table_scale * table_scale * wide_table * summed
        sharp_row = jnp.broadcast_to(extra_sum[route + 2 : route + 3, :128], (8, 128))
        tiny = jnp.concatenate([table_grad, sharp_row], axis=0)
        tiny_ref[...] = tiny
        outer_ref[...] = outer_sum[...].astype(BF)
        extra = jnp.transpose(extra_sum[...])
        if chunks <= 8:
            tiny = jnp.concatenate([tiny, jnp.zeros((128 - tiny.shape[0], 128), F32)], axis=0)
            tiny = pltpu.roll(jnp.transpose(tiny)[: extra_rows], EXACT, 1)
            lane = lax.broadcasted_iota(jnp.int32, tiny.shape, 1)
            tiny = split_exact(jnp.where((lane >= EXACT) & (lane < EXACT + 16), tiny, 0.0))
            tiny = jnp.concatenate([tiny] * (extra.shape[0] // extra_rows), axis=0)
            lane = lax.broadcasted_iota(jnp.int32, tiny.shape, 1)
            extra = jnp.where(lane < EXACT, extra, tiny)
        extra_ref[...] = extra.astype(BF)


def score_back_kernel(pairs, heads_before, weights, spot_ref, label_ref, q_ref, k_ref, v_ref, att_grad_ref, lse_ref,
                      delta_ref, turned_ref, *refs):
    count = 3 + 2 * weights
    scratch = refs[-1 - weights :]
    out_refs = refs[-1 - weights - count : -1 - weights]
    more_refs = refs[: -1 - weights - count]
    dq_ref, dk_ref, dv_ref = out_refs[:3]
    bias_ref = scratch[0]
    rows = q_ref.shape[0]
    bias_ref[...] = same_label(label_ref)
    low_lanes = lax.broadcasted_iota(jnp.int32, (rows, 128), 1) < HEAD_DIM
    for pair in range(pairs):
        columns = slice(pair * 128, pair * 128 + 128)
        q_pair, k_pair, v_pair = q_ref[:, columns], k_ref[:, columns], v_ref[:, columns]
        g_pair = att_grad_ref[:, columns]
        k_turned = jnp.transpose(k_pair)
        dk = jnp.zeros((rows, 128), F32)
        dv = jnp.zeros((rows, 128), F32)
        dq_turned = []
        for half in range(2):
            own = low_lanes if half == 0 else jnp.logical_not(low_lanes)
            q_own = jnp.where(own, q_pair.astype(F32), 0.0).astype(BF)
            g_own = jnp.where(own, g_pair.astype(F32), 0.0).astype(BF)
            head = heads_before + pair * 2 + half
            probs = jnp.exp(mxu(k_pair, q_own, NT) + bias_ref[...] - lse_ref[head : head + 1, :])
            prob_grad = mxu(v_pair, g_own, NT)
            score_grad = (probs * (prob_grad - delta_ref[head : head + 1, :])).astype(BF)
            dv += mxu(probs.astype(BF), g_own)
            dk += mxu(score_grad, q_own)
            dq_turned.append(mxu(k_turned[half * HEAD_DIM : (half + 1) * HEAD_DIM], score_grad))
        dq = jnp.transpose(jnp.concatenate(dq_turned, axis=0)) * HEAD_DIM ** (-0.5)
        dq_ref[:, columns] = dq.astype(BF)
        dk_ref[:, columns] = dk.astype(BF)
        dv_ref[:, columns] = dv.astype(BF)
    if weights:
        weight_sums(spot_ref[0], turned_ref, (dq_ref, dk_ref, dv_ref), more_refs, out_refs[3], out_refs[4], scratch[1])


def weight_sums(spot, turned_ref, grad_refs, more_refs, keep_ref, send_ref, total_ref):
    step, steps = pl.program_id(0), pl.num_programs(0)
    width = grad_refs[0].shape[1]
    for part, ref in enumerate(grad_refs):
        columns = slice(part * width, (part + 1) * width)
        product = mxu(turned_ref[...], ref[...])

        @pl.when(step == 0)
        def _():
            total_ref[:, columns] = product

        @pl.when(step > 0)
        def _():
            total_ref[:, columns] += product

    @pl.when(step == steps - 1)
    def _():
        start = len(grad_refs) * width
        put_halves(spot, keep_ref, send_ref, slice(0, start), total_ref[...].astype(BF))
        for more_ref in more_refs:
            columns = slice(start, start + more_ref.shape[1])
            put_halves(spot, keep_ref, send_ref, columns, more_ref[...])
            start += more_ref.shape[1]


def tokens_kernel(groups, spot_ref, turned_ref, x_ref, grad_ref, wq_ref, wk_ref, wv_ref, gain_ref, shift_ref, *refs):
    tokens_ref, keep_ref, send_ref, sums_ref, joined_ref, total_ref, turned_sums_ref = refs[3 * groups :]
    step, steps = pl.program_id(0), pl.num_programs(0)
    one_grad = 0.0
    for part, w_ref in enumerate((wq_ref, wk_ref, wv_ref)):
        start = 0
        for group in range(groups):
            piece = refs[3 * group + part]
            joined_ref[part, :, start : start + piece.shape[1]] = piece[...]
            start += piece.shape[1]
        one_grad += mxu(joined_ref[part], w_ref[...], NT)
    unit, scale, _ = norm_of(x_ref[...].astype(F32), gain_ref[...], shift_ref[...])
    inner = one_grad * gain_ref[...]
    one_part = scale * (
        inner
        - jnp.mean(inner, axis=-1, keepdims=True)
        - unit * jnp.mean(inner * unit, axis=-1, keepdims=True)
    )
    tokens_ref[...] = (grad_ref[...] + one_part).astype(BF)

    @pl.when(step == 0)
    def _():
        sums_ref[...] = jnp.zeros_like(sums_ref)

    sums_ref[0:1, :] += jnp.sum(one_grad * unit, axis=0, keepdims=True)
    sums_ref[1:2, :] += jnp.sum(one_grad, axis=0, keepdims=True)

    @pl.when(step == steps - 1)
    def _():
        turned_sums_ref[...] = jnp.transpose(sums_ref[...]).astype(BF)

    weight_sums(
        spot_ref[0], turned_ref, refs[3 * groups - 3 : 3 * groups], [turned_sums_ref], keep_ref, send_ref, total_ref
    )


def first_sum_kernel(exact, keep_ref, came_ref, *out_refs):
    for k, out_ref in enumerate(out_refs):
        out_ref[...] = (keep_ref[k].astype(F32) + came_ref[k].astype(F32)).astype(BF)
        if exact is not None:
            block = keep_ref[k, :, exact : exact + 128].astype(F32) + came_ref[k, :, exact : exact + 128].astype(F32)
            out_ref[:, exact : exact + 128] = split_exact(join_exact(block)).astype(BF)


def second_sum_kernel(exact, place_ref, *refs):
    own_ref, send_refs, sum_ref = refs[4], refs[5:-1], refs[-1]
    sum_ref[...] = sum(ref[...].astype(F32) for ref in refs[:4])
    if exact is not None:
        sum_ref[:, exact : exact + 128] = split_exact(join_exact(sum_ref[:, exact : exact + 128]))
    size = own_ref.shape[0]
    group = len(send_refs) + 1
    own_ref[...] = sum_ref[pl.ds(pl.multiple_of(place_ref[0] * size, 8), size), :]
    for k, send_ref in enumerate(send_refs):
        there = lax.rem(place_ref[0] + k + 1, group)
        block = sum_ref[pl.ds(pl.multiple_of(there * size, 8), size), :]
        filler = jnp.zeros((send_ref.shape[0] - size, block.shape[1]), F32)
        send_ref[...] = jnp.concatenate([block, filler], axis=0).astype(BF)


def third_sum_kernel(exact, own_ref, *refs):
    total_ref = refs[-1]
    size = own_ref.shape[0]
    total_ref[...] = own_ref[...] + sum(ref[...].astype(F32)[:size] for ref in refs[:-1])
    if exact is not None:
        total_ref[:, exact : exact + 128] = join_exact(total_ref[:, exact : exact + 128])


def output_kernel(place_ref, residual_ref, weight_ref, pos_ref, out_ref, layer_ref, spots_ref):
    chunks, slots = out_ref.shape[:2]

    @pl.when(pl.program_id(0) == 0)
    def _():
        for k in range(chunks):
            spots_ref[k * slots : (k + 1) * slots, :] = out_ref[lax.rem(place_ref[0] + k, chunks)]

    rows = residual_ref.shape[0]
    both = jnp.concatenate([pos_ref[...].astype(F32), weight_ref[...], jnp.zeros((126, rows), F32)], axis=0)
    both = jnp.transpose(both)
    pos_column, weight_column = both[:, :1].astype(jnp.int32), both[:, 1:2]
    lanes = lax.broadcasted_iota(jnp.int32, (rows, spots_ref.shape[0]), 1)
    home = mxu((lanes == pos_column).astype(F32).astype(BF), spots_ref[...])
    layer_ref[...] = (residual_ref[...] + home * weight_column).astype(BF)


def swap(values, axis, mask):
    size = lax.axis_size(axis)
    return lax.ppermute(values, axis, [(i, i ^ mask) for i in range(size)])


def shift(values, axis, step):
    size = lax.axis_size(axis)
    return lax.ppermute(values, axis, [(i, (i + step) % size) for i in range(size)])


def pick(values, index, axis):
    return lax.dynamic_index_in_dim(values, index, axis, keepdims=False)


def first_sum(keep, send, exact=None, deps=()):
    half, rows, width = keep.shape
    came = swap(send, "dp", 1)
    return kernel_call(
        partial(first_sum_kernel, exact),
        (half * rows * width, 6 * half * rows * width),
        deps,
        in_specs=[pl.BlockSpec()] * 2,
        out_shape=[jax.ShapeDtypeStruct((rows, width), BF)] * half,
    )(keep, came)


def second_sum(parts, place_vec, exact=None, deps=()):
    group = lax.axis_size("expert")
    came = [parts[0]] + [swap(parts[k], "dp", 2 * k) for k in range(1, len(parts))]
    rows, width = parts[0].shape
    if group > 8:
        return sum(part.astype(F32) for part in came)
    size = rows // group
    padded = (size + 15) // 16 * 16
    sd = jax.ShapeDtypeStruct
    return kernel_call(
        partial(second_sum_kernel, exact),
        (4 * rows * width, 12 * rows * width),
        deps,
        in_specs=[pl.BlockSpec(memory_space=pltpu.SMEM)] + [pl.BlockSpec()] * len(came),
        out_shape=[sd((size, width), F32)] + [sd((padded, width), BF)] * (group - 1),
        scratch_shapes=[pltpu.VMEM((rows, width), F32)],
    )(place_vec, *came)


def third_sum(parts, exact=None, deps=()):
    group = lax.axis_size("expert")
    if group > 8:
        return lax.psum_scatter(parts, "expert", scatter_dimension=0, tiled=True)
    came = [shift(parts[k], "expert", k) for k in range(1, group)]
    return kernel_call(
        partial(third_sum_kernel, exact),
        (4 * parts[0].size, 12 * parts[0].size),
        deps,
        in_specs=[pl.BlockSpec()] * group,
        out_shape=jax.ShapeDtypeStruct(parts[0].shape, F32),
    )(parts[0], *came)


def small_sum(values):
    group = lax.axis_size("expert")
    if group > 8:
        return lax.psum(values, ("dp", "expert"))
    values = values + swap(values, "dp", 1)
    values = values + sum(swap(values, "dp", mask) for mask in range(2, lax.axis_size("dp"), 2))
    return values + sum(shift(values, "expert", k) for k in range(1, group))


def exchange(blocks, sign):
    size = lax.axis_size("expert")
    if size <= 8:
        return [blocks[0]] + [shift(blocks[k], "expert", sign * k) for k in range(1, size)]
    stacked = jnp.stack(blocks)
    place = lax.axis_index("expert")
    across = (jnp.arange(size) - place) * sign % size
    there = lax.all_to_all(stacked[across], "expert", 0, 0, tiled=True)
    source = (place - sign * jnp.arange(size)) % size
    home = there[source]
    return [home[k] for k in range(size)]


WAYS = 4
SETS = ((0, 2), (1, 3))
CUTS = (384, 384)


def body(
    layer_inputs_matrix,
    upstream_output_sensitivity,
    mixer_layernorm_scale,
    mixer_layernorm_offset,
    asker_matrix,
    lookup_label_matrix,
    content_matrix,
    mixer_result_matrix,
    specialist_layernorm_scale,
    specialist_layernorm_offset,
    dispatch_projection_matrix,
    specialist_centroids,
    learned_sharpness,
    specialist_widening_matrix,
    specialist_narrowing_matrix,
    document_labels,
    chosen_specialist,
    placement_ranks,
):
    rows, width = layer_inputs_matrix.shape
    seqs, length = document_labels.shape
    head_count = width // HEAD_DIM
    group = lax.axis_size("expert")
    place = lax.axis_index("expert")
    dp_size = lax.axis_size("dp")
    wide, narrow = specialist_widening_matrix[0], specialist_narrowing_matrix[0]
    hidden = wide.shape[1]
    route = dispatch_projection_matrix.shape[1]
    slots = 3 * rows // (2 * group)
    spots = group * slots
    experts_padded = (group + 7) // 8 * 8
    sd = jax.ShapeDtypeStruct
    smem = pl.BlockSpec(memory_space=pltpu.SMEM)
    int32 = jnp.int32
    place_vec = place.astype(int32).reshape(1)
    spot_vec = lax.axis_index("dp").astype(int32).reshape(1)
    vec = lambda v: v.reshape(1, -1)
    gain_one, shift_one = vec(mixer_layernorm_scale), vec(mixer_layernorm_offset)
    gain_two, shift_two = vec(specialist_layernorm_scale), vec(specialist_layernorm_offset)
    router = dispatch_projection_matrix.T
    table = jnp.zeros((experts_padded, route), F32).at[:group].set(specialist_centroids)
    labels = document_labels.reshape(seqs, 1, length)
    chosen = chosen_specialist.reshape(1, rows)

    row_block = pl.BlockSpec((length, width), lambda s: (s, 0))
    line = pl.BlockSpec((1, length), lambda s: (0, s))
    label_spec = pl.BlockSpec((1, 1, length), lambda s: (s, 0, 0))
    turned_block = pl.BlockSpec((width, length), lambda s: (0, s))
    heads_block = pl.BlockSpec((16, length), lambda s: (0, s))
    weight_spec = whole((width, width))
    vec_spec = whole((1, width))
    chunk_spec, tailed_spec = whole((slots, width)), whole((slots + TAIL, width))
    table_spec = whole((experts_padded, route))

    tailed = slots + TAIL
    pos, rank, upstream_sent = kernel_call(
        partial(route_kernel, slots),
        (2 * spots * rows * width, 8 * rows * width),
        in_specs=[smem] + [pl.BlockSpec()] * 3,
        out_shape=[sd((1, rows), int32)] * 2 + [sd((group, tailed, width), BF)],
    )(place_vec, placement_ranks, chosen, upstream_output_sensitivity)
    upstream_there = lax.all_to_all(upstream_sent, "expert", 0, 0, tiled=True)

    turned, queries, keys, values, attended, lse, residual, projected, *entering_sent = kernel_call(
        partial(attend_kernel, group, slots),
        (10 * rows * width * width + 4 * rows * length * width * 4, 20 * rows * width),
        grid=(seqs,),
        in_specs=[row_block, label_spec] + [vec_spec] * 2 + [weight_spec] * 4 + [vec_spec] * 2
        + [whole((route, width)), table_spec, smem, line, line],
        out_specs=[turned_block] + [row_block] * 4
        + [heads_block, row_block, pl.BlockSpec((route, length), lambda s: (0, s))] + [tailed_spec] * group,
        out_shape=[sd((width, rows), BF)] + [sd((rows, width), BF)] * 4
        + [sd((16, rows), F32), sd((rows, width), F32), sd((route, rows), F32)]
        + [sd((tailed, width), BF)] * group,
        scratch_shapes=[pltpu.VMEM((length, length), F32), pltpu.VMEM((length, 128), F32)],
    )(
        layer_inputs_matrix, labels, gain_one, shift_one, asker_matrix, lookup_label_matrix,
        content_matrix, mixer_result_matrix, gain_two, shift_two, router, table, learned_sharpness, chosen, pos,
    )
    entering_there = exchange(entering_sent, 1)
    tails = upstream_there[:, slots : slots + 2, :experts_padded].astype(F32)
    tallies = (tails[:, 0] * 256.0 + tails[:, 1]).astype(int32)
    sources = jnp.arange(group)
    prior = jnp.sum(jnp.where(sources[:, None] < place, tallies, 0), axis=0).reshape(experts_padded, 1)
    named = jnp.sum(jnp.where(jnp.arange(experts_padded) == place, tallies, 0), axis=1)
    earlier = jnp.sum(jnp.where(sources[:, None] < sources[None, :], named[:, None], 0), axis=0)
    counts = jnp.clip(rows - earlier, 0, named)
    relative = (place - sources) % group
    counts = jnp.sum(jnp.where(relative[:, None] == sources[None, :], counts[None, :], 0), axis=1)

    each = group // WAYS
    if each > 1:
        valid = jnp.arange(slots)[None, :] < counts[:, None]
        counts = jnp.full((WAYS,), each * slots, int32)

        def join(blocks, masks):
            chunks = []
            for k in range(0, group, each):
                tail = [jnp.where(masks[j], blocks[j][slots:, :slots], 0) for j in range(k, k + each)]
                tail = jnp.concatenate(tail, axis=1)
                tail = jnp.pad(tail, ((0, 0), (0, width - tail.shape[1])))
                chunks.append(jnp.concatenate([blocks[j][:slots] for j in range(k, k + each)] + [tail]))
            return chunks

        def split(chunks, with_tail):
            pieces = []
            for chunk in chunks:
                for j in range(each):
                    piece = chunk[j * slots : (j + 1) * slots]
                    if with_tail:
                        tail = chunk[each * slots :, j * slots : (j + 1) * slots]
                        piece = jnp.concatenate([piece, jnp.pad(tail, ((0, 0), (0, width - slots)))])
                    pieces.append(piece)
            return pieces
    else:
        valid = [True] * group
        join = split = lambda blocks, _: list(blocks)
    entered = join(entering_there, valid)
    if each > 1:
        graded = join([pick(upstream_there, relative[k], 0) for k in range(group)], valid)
        graded = jnp.stack([graded[-k % WAYS] for k in range(WAYS)])
        turn_vec = jnp.zeros((1,), int32)
    else:
        graded, turn_vec = upstream_there, place_vec
    produced, returned, earlier = [], [None] * WAYS, ()
    acts, pres = [], []
    for ids in SETS:
        out, backs, act, pre = expert_call(
            counts, turn_vec, ids, earlier, produced, [entered[k] for k in ids], graded, wide, narrow, acts
        )
        produced, earlier = [out], earlier + ids
        for at, k in enumerate(ids):
            returned[k] = backs[at]
        acts.append(act)
        pres.append(pre)
    returned_home = exchange(split(returned, True), -1)
    ordered = [k for ids in SETS for k in ids]
    arrange = lambda chunks: [chunks[k] for k in ordered]
    depth = rows + 128 if each == 1 else spots
    keep_wide, send_wide, keep_narrow, send_narrow = weight_calls(
        counts, spot_vec, turn_vec, SETS, arrange(entered), graded, acts, pres, dp_size, depth, returned_home[2]
    )
    half, block = dp_size // 2, width // dp_size
    weight_parts = kernel_call(
        weight_first_kernel,
        (width * hidden, 6 * width * hidden),
        in_specs=[pl.BlockSpec()] * 4,
        out_shape=[sd((block, 2 * hidden), BF)] * half,
    )(keep_wide, swap(send_wide, "dp", 1), keep_narrow, swap(send_narrow, "dp", 1))

    head_rows = jnp.arange(16)[:, None] == jnp.arange(width)[None, :] // HEAD_DIM
    (produced,) = produced
    if each > 1:
        pieces = jnp.stack(split([produced[-k % WAYS] for k in range(WAYS)], False))
        produced = pieces[relative]
    anywhere = pl.BlockSpec(memory_space=pl.ANY)
    weight, residual_grad, attended_grad, delta, outer_part, extra_part, tiny, produced_sent = kernel_call(
        partial(home_kernel, group, slots, rows, group, width // (dp_size * group)),
        (4 * rows * width * width + 2 * rows * spots * width, 30 * rows * width),
        weight_parts[0],
        grid=(seqs,),
        in_specs=[smem, whole((experts_padded, 1)), line, line, line, row_block, row_block, row_block,
                  pl.BlockSpec((route, length), lambda s: (0, s)), table_spec, whole((128, width)), vec_spec, vec_spec,
                  weight_spec, whole((16, width))]
        + [tailed_spec] * group + [anywhere],
        out_specs=[line, row_block, row_block, heads_block, weight_spec, whole((width, 128)),
                   whole((experts_padded + 8, 128)), anywhere],
        out_shape=[sd((1, rows), F32), sd((rows, width), F32), sd((rows, width), BF), sd((16, rows), F32),
                   sd((width, width), BF), sd((width, 128), BF), sd((experts_padded + 8, 128), F32),
                   sd((group, slots, width), BF)],
        input_output_aliases={15 + group: 7},
        scratch_shapes=[pltpu.VMEM((spots, width), BF), pltpu.VMEM((width, width), F32),
                        pltpu.VMEM((128, width), F32), pltpu.VMEM((experts_padded, 128), F32)],
    )(
        learned_sharpness, prior, chosen, rank, pos, residual, upstream_output_sensitivity, attended,
        projected, table, jnp.concatenate([router, jnp.zeros((128 - route, width), F32)]), gain_two, shift_two,
        mixer_result_matrix, head_rows.astype(BF), *returned_home, produced,
    )
    produced_home = lax.all_to_all(produced_sent, "expert", 0, 0, tiled=True)

    pieces, start = [], 0
    for cut in CUTS:
        early = start == 0
        part = pl.BlockSpec((length, cut), lambda s, at=start // cut: (s, at))
        own = pl.BlockSpec((length, cut), lambda s: (s, 0))
        more = [outer_part, extra_part] if early else []
        pack = [sd((half, block, 3 * cut + width + 128), BF)] * 2 if early else []
        *grads, = kernel_call(
            partial(score_back_kernel, cut // 128, start // HEAD_DIM, early),
            (8 * rows * length * cut * 4 + 6 * rows * width * cut, 20 * rows * cut),
            [] if early else [pieces, hidden_grad],
            grid=(seqs,),
            in_specs=[smem, label_spec] + [part] * 4 + [heads_block] * 2 + [turned_block]
            + [whole(array.shape) for array in more],
            out_specs=[own] * 3 + [whole(array.shape) for array in pack],
            out_shape=[sd((rows, cut), BF)] * 3 + pack,
            scratch_shapes=[pltpu.VMEM((length, length), F32)] + [pltpu.VMEM((width, 3 * cut), F32)] * early,
        )(spot_vec, labels, queries, keys, values, attended_grad, lse, delta, turned, *more)
        pieces.append(grads[:3])
        if early:
            keep, send = grads[3:]
            hidden_grad, return_grad = kernel_call(
                partial(weight_last_kernel, hidden // dp_size),
                (8 * block * hidden, 30 * block * hidden),
                pieces,
                in_specs=[pl.BlockSpec()] * half,
                out_shape=[sd((block, hidden), F32), sd((hidden // dp_size, width), F32)],
            )(weight_parts[0], *[swap(weight_parts[k], "dp", 2 * k) for k in range(1, half)])
        start += cut
    first, last = CUTS
    exact = 3 * first + width
    early = first_sum(keep, send, exact, pieces[1])
    pack = sd((half, block, 3 * last + 128), BF)
    tokens_grad, keep, send = kernel_call(
        partial(tokens_kernel, len(CUTS)),
        (6 * rows * width * (width + last), 16 * rows * width),
        early,
        grid=(seqs,),
        in_specs=[smem, turned_block, row_block, row_block] + [weight_spec] * 3 + [vec_spec] * 2
        + [pl.BlockSpec((length, cut), lambda s: (s, 0)) for cut in CUTS for _ in range(3)],
        out_specs=[row_block] + [whole(pack.shape)] * 2,
        out_shape=[sd((rows, width), BF)] + [pack] * 2,
        scratch_shapes=[pltpu.VMEM((128, width), F32), pltpu.VMEM((3, length, width), BF),
                        pltpu.VMEM((width, 3 * last), F32), pltpu.VMEM((width, 128), BF)],
    )(spot_vec, turned, layer_inputs_matrix, residual_grad, asker_matrix, lookup_label_matrix, content_matrix,
      gain_one, shift_one, *[piece for group_pieces in pieces for piece in group_pieces])
    early = second_sum(early, place_vec, exact, tokens_grad)
    late = first_sum(keep, send, None, early)
    layer_output = kernel_call(
        output_kernel,
        (2 * rows * spots * width, 12 * rows * width),
        late,
        grid=(seqs,),
        in_specs=[smem, row_block, line, line, whole((group, slots, width))],
        out_specs=row_block,
        out_shape=sd((rows, width), BF),
        scratch_shapes=[pltpu.VMEM((spots, width), BF)],
    )(place_vec, residual, weight, pos, produced_home)
    early = third_sum(early, exact, layer_output)
    late = third_sum(second_sum(late, place_vec, None, early))

    joined = lambda part: jnp.concatenate(
        [early[:, part * first : (part + 1) * first], late[:, part * last : (part + 1) * last]], axis=1
    )
    extra = early[:, exact : exact + 128]
    if group <= 8:
        table_grad, sharp = extra[:route, EXACT : EXACT + group].T, extra[0, EXACT + experts_padded].reshape(1)
    else:
        tiny = small_sum(tiny)
        table_grad, sharp = tiny[:group, :route], tiny[experts_padded, :1]
    return (
        layer_output,
        tokens_grad,
        late[:, 3 * last],
        late[:, 3 * last + 1],
        joined(0),
        joined(1),
        joined(2),
        early[:, 3 * first : exact],
        extra[:, route],
        extra[:, route + 1],
        extra[:, :route],
        table_grad,
        sharp,
        hidden_grad[None],
        return_grad[None],
    )


def solution(mesh):
    placed = (
        P(("dp", "expert"), None),
        P(("dp", "expert"), None),
        P(),
        P(),
        P(),
        P(),
        P(),
        P(),
        P(),
        P(),
        P(),
        P(),
        P(),
        P("expert", None, None),
        P("expert", None, None),
        P(("dp", "expert"), None),
        P(("dp", "expert"), None),
        P(("dp", "expert"), None),
    )
    return jax.shard_map(
        body,
        mesh=mesh,
        in_specs=placed,
        out_specs=(
            P(("dp", "expert"), None),
            P(("dp", "expert"), None),
            P(("dp", "expert")),
            P(("dp", "expert")),
            P(("dp", "expert"), None),
            P(("dp", "expert"), None),
            P(("dp", "expert"), None),
            P(("dp", "expert"), None),
            P(("dp", "expert")),
            P(("dp", "expert")),
            P(("dp", "expert"), None),
            P(),
            P(),
            P("expert", "dp", None),
            P("expert", "dp", None),
        ),
        check_vma=False,
    )
```

```python
from functools import partial

import jax
import jax.numpy as jnp
from jax import lax
from jax.experimental import pallas as pl
from jax.experimental.pallas import tpu as pltpu
from jax.sharding import PartitionSpec as P

HEAD_DIM = 64
EPSILON = 1e-05
MASKED = -1e30
BF = jnp.bfloat16
F32 = jnp.float32
TAIL = 16
ROUTE_VMEM = 24
ATTEND_VMEM = 54
HOME_VMEM = 18
SCORE_VMEM = 12
TOKENS_VMEM = 18
OUTPUT_VMEM = 10
WIDE_VMEM = 36
NARROW_VMEM = 36
SUM1_VMEM = 8
SUM2_VMEM = 8
SUM3_VMEM = 10
SUM4_VMEM = 8
SUM5_VMEM = 8
SUM6_VMEM = 8
EXPERT_VMEM = (36, 50)
NN = (((1,), (0,)), ((), ()))
NT = (((1,), (1,)), ((), ()))
TN = (((0,), (0,)), ((), ()))


def mxu(left, right, dims=NN):
    return lax.dot_general(left, right, dims, preferred_element_type=F32)


def split_high(values):
    high = values.astype(BF)
    low = (values - high.astype(F32)).astype(BF)
    return high, low


def mxu_wide(left, right, dims=NN):
    left_high, left_low = split_high(left)
    right_high, right_low = split_high(right)
    return (
        mxu(left_high, right_high, dims)
        + mxu(left_high, right_low, dims)
        + mxu(left_low, right_high, dims)
    )


def kernel_call(body, weight, deps=(), vmem=56, **kwargs):
    deps = jax.tree.leaves(deps)
    inputs, outputs = len(kwargs["in_specs"]), len(kwargs["out_shape"])
    first = inputs + len(deps)
    any_spec = pl.BlockSpec(memory_space=pl.ANY)
    kwargs["in_specs"] = list(kwargs["in_specs"]) + [any_spec] * len(deps)
    kwargs["out_shape"] = list(kwargs["out_shape"]) + [jax.ShapeDtypeStruct((8, 128), F32)]
    if "out_specs" in kwargs:
        done_spec = whole((8, 128)) if "grid" in kwargs else pl.BlockSpec(memory_space=pltpu.VMEM)
        kwargs["out_specs"] = list(kwargs["out_specs"]) + [done_spec]

    def run(*refs):
        refs[first + outputs][...] = jnp.zeros((8, 128), F32)
        body(*refs[:inputs], *refs[first : first + outputs], *refs[first + outputs + 1 :])

    call = pl.pallas_call(
        run,
        compiler_params=pltpu.CompilerParams(
            vmem_limit_bytes=vmem * 2**20,
            dimension_semantics=("arbitrary",) * len(kwargs.get("grid", ())),
        ),
        cost_estimate=pl.CostEstimate(flops=int(weight * 2**30), bytes_accessed=0, transcendentals=0),
        **kwargs,
    )

    def made(*args):
        *outs, done = call(*args, *deps)
        return outs, done

    return made


def hbm(array):
    return pltpu.with_memory_space_constraint(array, pltpu.HBM)


def whole(shape):
    return pl.BlockSpec(shape, lambda *_: (0,) * len(shape))


def route_kernel(slots, place_ref, order_ref, chosen_ref, rows_ref, pos_ref, rank_ref, sent_ref):
    group = sent_ref.shape[0]
    order = order_ref[...].astype(F32)
    count = order.shape[1]
    chosen = chosen_ref[...]
    chosen_wide = jnp.transpose(jnp.broadcast_to(chosen.astype(F32), (128, count)))
    order_col = jnp.transpose(jnp.broadcast_to(order, (128, count)))[:, :1]
    before = (order_col < order) & (chosen_wide[:, :1] == chosen.astype(F32))
    rank = jnp.sum(before.astype(F32), axis=0, keepdims=True).astype(jnp.int32)
    place = place_ref[0]
    pos = jnp.where(chosen >= place, chosen - place, chosen - place + group) * slots + rank
    pos_ref[...] = pos
    rank_ref[...] = rank
    lanes = lax.broadcasted_iota(jnp.int32, (count, 128), 1).astype(F32)
    rows = rows_ref[...]
    tally = jnp.sum((chosen_wide == lanes).astype(F32), axis=0, keepdims=True)
    upper = jnp.floor(tally * (1.0 / 256.0))
    place_row = lax.broadcasted_iota(jnp.int32, (TAIL, 128), 0)
    tail = jnp.where(place_row == 0, upper, jnp.where(place_row == 1, tally - 256.0 * upper, 0.0))
    tail = jnp.concatenate([tail, jnp.zeros((TAIL, rows.shape[1] - 128), F32)], axis=1).astype(BF)
    for k in range(group):
        spots = lax.broadcasted_iota(jnp.int32, (slots, count), 0) + k * slots
        sent_ref[k, :slots, :] = mxu((spots == chosen * slots + rank).astype(F32).astype(BF), rows).astype(BF)
        sent_ref[k, slots:, :] = tail


def norm_of(values, gain, shift):
    centered = values - jnp.mean(values, axis=-1, keepdims=True)
    scale = lax.rsqrt(jnp.mean(centered * centered, axis=-1, keepdims=True) + EPSILON)
    unit = centered * scale
    return unit, scale, unit * gain + shift


def router_of(projected, table, temper):
    scale = lax.rsqrt(jnp.sum(projected * projected, axis=0, keepdims=True) + 1.0)
    unit = projected * scale
    table_scale = lax.rsqrt(jnp.sum(table * table, axis=1, keepdims=True) + 1.0)
    unit_table = table * table_scale
    logits = lax.dot_general(
        unit_table, unit, NN, precision=lax.Precision.HIGHEST, preferred_element_type=F32
    ) / temper
    return scale, unit, table_scale, unit_table, logits


def softmax_rows(logits, experts):
    valid = lax.broadcasted_iota(jnp.int32, logits.shape, 0) < experts
    logits = jnp.where(valid, logits, MASKED)
    weights = jnp.exp(logits - jnp.max(logits, axis=0, keepdims=True))
    return weights / jnp.sum(weights, axis=0, keepdims=True)


def same_label(labels):
    labels = labels.astype(F32)
    column = jnp.transpose(jnp.broadcast_to(labels, (128, labels.shape[1])))[:, :1]
    return jnp.where(column == labels, 0.0, MASKED)


def attend_kernel(experts, slots, x_ref, label_ref, gain_one_ref, shift_one_ref, wq_ref,
                  wk_ref, wv_ref, wo_ref, gain_two_ref, shift_two_ref, router_ref, table_ref, temper_ref,
                  chosen_ref, pos_ref, turned_ref, q_ref, k_ref, v_ref, att_ref, lse_ref, residual_ref,
                  projected_ref, *rest):
    sent_refs, bias_ref, lse_cols_ref = rest[:-2], rest[-2], rest[-1]
    step = pl.program_id(0)
    x = x_ref[...].astype(F32)
    rows, width = x.shape
    normed = norm_of(x, gain_one_ref[...], shift_one_ref[...])[2].astype(BF)
    turned_ref[...] = jnp.transpose(normed)
    q_ref[...] = (mxu(normed, wq_ref[...]).astype(BF).astype(F32) * HEAD_DIM ** (-0.5)).astype(BF)
    k_ref[...] = mxu(normed, wk_ref[...]).astype(BF)
    v_ref[...] = mxu(normed, wv_ref[...]).astype(BF)
    bias_ref[...] = same_label(label_ref[0])
    lane = lax.broadcasted_iota(jnp.int32, (rows, 128), 1)
    low_lanes = lane < HEAD_DIM
    lse_cols = jnp.zeros((rows, 128), F32)
    for pair in range(width // 128):
        columns = slice(pair * 128, pair * 128 + 128)
        q_pair, k_pair, v_pair = q_ref[:, columns], k_ref[:, columns], v_ref[:, columns]
        outs = []
        for half in range(2):
            own = low_lanes if half == 0 else jnp.logical_not(low_lanes)
            q_own = jnp.where(own, q_pair.astype(F32), 0.0).astype(BF)
            scores = mxu(q_own, k_pair, NT) + bias_ref[...]
            largest = jnp.max(scores, axis=-1, keepdims=True)
            weights = jnp.exp(scores - largest)
            total = jnp.sum(weights, axis=-1, keepdims=True)
            outs.append(mxu(weights.astype(BF), v_pair) * (1.0 / total))
            lse_cols = jnp.where(lane == pair * 2 + half, largest + jnp.log(total), lse_cols)
        att_ref[:, columns] = jnp.where(low_lanes, outs[0], outs[1]).astype(BF)
    lse_cols_ref[...] = lse_cols
    lse_ref[...] = jnp.transpose(lse_cols_ref[...])[: lse_ref.shape[0]]
    residual = x + mxu(att_ref[...], wo_ref[...])
    residual_ref[...] = residual
    normed_two = norm_of(residual, gain_two_ref[...], shift_two_ref[...])[2]
    projected = lax.dot_general(
        router_ref[...], normed_two, NT, precision=lax.Precision.HIGHEST, preferred_element_type=F32
    )
    projected_ref[...] = projected
    logits = router_of(projected, table_ref[...], temper_ref[0])[4]
    routed = softmax_rows(logits, experts)
    selected = chosen_ref[...] == lax.broadcasted_iota(jnp.int32, logits.shape, 0)
    gate = jnp.sum(jnp.where(selected, routed, 0.0), axis=0, keepdims=True)
    high = gate.astype(BF).astype(F32)
    mid = (gate - high).astype(BF).astype(F32)
    low = gate - high - mid
    place = lax.broadcasted_iota(jnp.int32, (TAIL, rows), 0)
    pieces = jnp.where(place == 0, high, jnp.where(place == 1, mid, jnp.where(place == 2, low, 0.0)))
    pieces = pieces.astype(BF)
    entering = normed_two.astype(BF)
    pos = pos_ref[...]
    for k in range(len(sent_refs)):
        spots = lax.broadcasted_iota(jnp.int32, (slots, rows), 0) + k * slots
        here = (spots == pos).astype(F32).astype(BF)
        sent = mxu(here, entering)
        gates = mxu(pieces, here, NT)
        tail = jnp.concatenate([gates, jnp.zeros((TAIL, width - slots), F32)], axis=1)

        @pl.when(step == 0)
        def _():
            sent_refs[k][:slots, :] = sent.astype(BF)
            sent_refs[k][slots:, :] = tail.astype(BF)

        @pl.when(step > 0)
        def _():
            sent_refs[k][:slots, :] = (sent_refs[k][:slots, :].astype(F32) + sent).astype(BF)
            sent_refs[k][slots:, :] = (sent_refs[k][slots:, :].astype(F32) + tail).astype(BF)


def gelu_parts(values):
    share = 0.5 * lax.erf(values * 0.5**0.5) + 0.5
    return share, jnp.exp(values * values * (-0.5)) * (2.0 * 3.141592653589793) ** (-0.5)


def pack_offsets(counts_ref, ids):
    offsets, total = [], 0
    for k in ids:
        offsets.append(pl.multiple_of(total, 16))
        total = total + (counts_ref[k] + 15) // 16 * 16
    return offsets, total


def source_of(place_ref, k, group):
    return lax.rem(place_ref[0] - k + group, group)


def expert_kernel(ids, past, block, counts_ref, place_ref, u_ref, *refs):
    chunks = len(ids)
    x_refs = refs[:chunks]
    wide_ref, narrow_ref = refs[chunks : chunks + 2]
    rest = refs[chunks + 2 + past :]
    out_ref, back_refs = rest[0], rest[1 : 1 + chunks]
    act_ref, pre_ref, xs, us, out_sum, back_sum, sums, outs, sent = rest[1 + chunks :]
    step, steps = pl.program_id(0), pl.num_programs(0)
    rows = x_refs[0].shape[0] - TAIL
    offsets, total = pack_offsets(counts_ref, ids)

    @pl.when(step == 0)
    def _():
        xs[...] = jnp.zeros_like(xs)
        us[...] = jnp.zeros_like(us)
        out_sum[...] = jnp.zeros_like(out_sum)
        back_sum[...] = jnp.zeros_like(back_sum)
        for k in range(chunks):
            xs[pl.ds(offsets[k], rows), :] = x_refs[k][:rows, :]
            us[pl.ds(offsets[k], rows), :] = u_ref[source_of(place_ref, ids[k], u_ref.shape[0]), :rows, :]

    def one(i, carry):
        here = pl.ds(pl.multiple_of(i * block, block), block)
        wide, narrow = wide_ref[...], narrow_ref[...]
        hidden = mxu(xs[here, :], wide)
        grad = mxu(us[here, :], narrow, NT)
        share, density = gelu_parts(hidden)
        act = (hidden * share).astype(BF)
        act_ref[here, :] = act
        pre = (grad * (share + hidden * density)).astype(BF)
        pre_ref[here, :] = pre
        out_sum[here, :] += mxu(act, narrow)
        back_sum[here, :] += mxu(pre, wide, NT)
        return carry

    blocks = (total + block - 1) // block
    lax.fori_loop(0, blocks, one, 0)

    def none(i, carry):
        here = pl.ds(pl.multiple_of(i * block, block), block)
        act_ref[here, :] = jnp.zeros((block, act_ref.shape[1]), BF)
        pre_ref[here, :] = jnp.zeros((block, pre_ref.shape[1]), BF)
        return carry

    lax.fori_loop(blocks, act_ref.shape[0] // block, none, 0)

    @pl.when(step == steps - 1)
    def _():
        out = out_sum[...].astype(BF).astype(F32)
        gates = jnp.sum(out * us[...].astype(F32), axis=1, keepdims=True)
        sums[...] = jnp.broadcast_to(gates, sums.shape)
        moves = []
        for k in range(chunks):
            here = pl.ds(offsets[k], rows)
            outs[k] = out_sum[here, :].astype(BF)
            moves.append(
                pltpu.make_async_copy(
                    outs.at[k], out_ref.at[source_of(place_ref, ids[k], u_ref.shape[0])], sent.at[k]
                )
            )
            moves[k].start()
            back_refs[k][:rows, :] = back_sum[here, :].astype(BF)
            gate = jnp.transpose(sums[here, :])[:1]
            high = gate.astype(BF).astype(F32)
            mid = (gate - high).astype(BF).astype(F32)
            place = lax.broadcasted_iota(jnp.int32, (TAIL, rows), 0)
            tail = jnp.where(place == 0, high, jnp.where(place == 1, mid, jnp.where(place == 2, gate - high - mid, 0.0)))
            tail = jnp.concatenate([tail, jnp.zeros((TAIL, out.shape[1] - rows), F32)], axis=1)
            back_refs[k][rows:, :] = tail.astype(BF)
        for move in moves:
            move.wait()


def expert_call(counts, place, ids, past, xs, us, wide, narrow, deps, block=384, parts=4):
    chunks, (tailed, width), hidden = len(xs), xs[0].shape, wide.shape[1]
    rows = tailed - TAIL
    cut, most = hidden // parts, chunks * rows
    sd = jax.ShapeDtypeStruct
    smem, anywhere = (pl.BlockSpec(memory_space=space) for space in (pltpu.SMEM, pl.ANY))
    chunk, every = whole((tailed, width)), (us.shape[0], rows, width)
    inner = pl.BlockSpec((most, cut), lambda f: (0, f))
    outs, done = kernel_call(
        partial(expert_kernel, ids, len(past), block),
        10,
        deps,
        vmem=EXPERT_VMEM[len(ids) - 1],
        grid=(parts,),
        in_specs=[smem] * 2 + [whole(us.shape)] + [chunk] * chunks
        + [pl.BlockSpec((width, cut), lambda f: (0, f)), pl.BlockSpec((cut, width), lambda f: (f, 0))]
        + [anywhere] * len(past),
        out_specs=[anywhere] + [chunk] * chunks + [inner, inner],
        out_shape=[pltpu.HBM(every, BF)] + [sd((tailed, width), BF)] * chunks + [pltpu.HBM((most, hidden), BF)] * 2,
        input_output_aliases={5 + chunks: 0} if past else {},
        scratch_shapes=[pltpu.VMEM((most, width), BF)] * 2
        + [pltpu.VMEM((most, width), F32)] * 2 + [pltpu.VMEM((most, 128), F32)]
        + [pltpu.VMEM((chunks, rows, width), BF), pltpu.SemaphoreType.DMA((chunks,))],
    )(counts, place, us, *xs, hbm(wide), hbm(narrow), *map(hbm, past))
    return outs[0], outs[1 : 1 + chunks], outs[-2], outs[-1], done


def pack_weighed(ids, counts_ref, x_refs, rows_of, depth, packed_ref, turned_ref):
    rows = x_refs[0].shape[0] - TAIL
    offsets, _ = pack_offsets(counts_ref, ids)
    packed_ref[...] = jnp.zeros_like(packed_ref)
    lanes = lax.broadcasted_iota(jnp.int32, (128, rows), 1)
    for k in range(len(ids)):
        gates = jnp.sum(x_refs[k][rows:, :rows].astype(F32), axis=0, keepdims=True)
        gates = jnp.where(lanes < counts_ref[ids[k]], gates, 0.0)
        gates = jnp.transpose(gates)[:, :1]
        packed_ref[pl.ds(offsets[k], rows), :] = (rows_of(k).astype(F32) * gates).astype(BF)
    turned_ref[...] = jnp.transpose(packed_ref[:depth])


def pack_units(sets, counts_ref, part_refs, packed_ref):
    offsets, _ = pack_offsets(counts_ref, sum(sets, ()))
    first = 0
    for part, part_ref in zip(sets, part_refs):
        packed_ref[pl.ds(offsets[first], part_ref.shape[0]), :] = part_ref[...]
        first += len(part)


def wide_kernel(sets, depth, counts_ref, spot_ref, *refs):
    ids = sum(sets, ())
    x_refs, pre_refs = refs[: len(ids)], refs[len(ids) : len(ids) + len(sets)]
    keep_ref, send_ref, packed, turned, pres = refs[len(ids) + len(sets) :]
    rows = x_refs[0].shape[0] - TAIL

    @pl.when(pl.program_id(0) == 0)
    def _():
        pres[...] = jnp.zeros_like(pres)
        pack_weighed(ids, counts_ref, x_refs, lambda k: x_refs[k][:rows, :], depth, packed, turned)

    pack_units(sets, counts_ref, pre_refs, pres)
    put_halves(spot_ref[0], keep_ref, [send_ref], slice(None), mxu(turned[...], pres[:depth]).astype(BF))


def narrow_kernel(sets, depth, counts_ref, spot_ref, place_ref, u_ref, *refs):
    ids = sum(sets, ())
    x_refs, act_refs = refs[: len(ids)], refs[len(ids) : len(ids) + len(sets)]
    keep_ref, send_ref, packed, turned, acts = refs[len(ids) + len(sets) :]
    rows = x_refs[0].shape[0] - TAIL
    step = pl.program_id(0)

    @pl.when(step == 0)
    def _():
        acts[...] = jnp.zeros_like(acts)
        rows_of = lambda k: u_ref[source_of(place_ref, ids[k], u_ref.shape[0]), :rows, :]
        pack_weighed(ids, counts_ref, x_refs, rows_of, depth, packed, turned)

    pack_units(sets, counts_ref, act_refs, acts)
    narrow = mxu(turned[...], acts[:depth]).astype(BF)
    spot = spot_ref[0]
    cut = keep_ref.shape[2]
    count = narrow.shape[1] // cut
    for k in range(count):
        part = narrow[:, k * cut : (k + 1) * cut]
        at = (step * count + k) // 2 ^ (spot // 2)

        @pl.when(spot % 2 == k % 2)
        def _():
            keep_ref[at] = part

        @pl.when(spot % 2 != k % 2)
        def _():
            send_ref[at] = part


def weight_calls(counts, spot, place, sets, xs, us, acts, pres, blocks, depth, deps, parts=4):
    chunks, (tailed, width), hidden = len(xs), xs[0].shape, acts[0].shape[1]
    half = blocks // 2
    cut, most = hidden // parts, chunks * (tailed - TAIL)
    smem = pl.BlockSpec(memory_space=pltpu.SMEM)
    inner = [pl.BlockSpec((act.shape[0], cut), lambda f: (0, f)) for act in acts]
    common = dict(
        grid=(parts,),
        scratch_shapes=[pltpu.VMEM((most, width), BF), pltpu.VMEM((width, depth), BF), pltpu.VMEM((most, cut), BF)],
    )
    chunk_specs = [whole((tailed, width))] * chunks
    wide, wide_done = kernel_call(
        partial(wide_kernel, sets, depth),
        5,
        vmem=WIDE_VMEM,
        in_specs=[smem] * 2 + chunk_specs + inner,
        out_specs=[pl.BlockSpec((half, width // blocks, cut), lambda f: (0, 0, f))] * 2,
        out_shape=[jax.ShapeDtypeStruct((half, width // blocks, hidden), BF)] * 2,
        **common,
    )(counts, spot, *xs, *map(hbm, pres))
    narrow, _ = kernel_call(
        partial(narrow_kernel, sets, depth),
        1,
        [deps, wide_done],
        vmem=NARROW_VMEM,
        in_specs=[smem] * 3 + [whole(us.shape)] + chunk_specs + inner,
        out_specs=[whole((half, width, hidden // blocks))] * 2,
        out_shape=[jax.ShapeDtypeStruct((half, width, hidden // blocks), BF)] * 2,
        **common,
    )(counts, spot, place, us, *xs, *map(hbm, acts))
    return *wide, *narrow


def weight_first_kernel(keep_wide, came_wide, keep_narrow, came_narrow, own_ref, x_keep, x_send, y_keep, y_send):
    rows, hidden = keep_wide.shape[1:]
    cut = keep_narrow.shape[2]
    for k in range(4):
        wide = (keep_wide[k].astype(F32) + came_wide[k].astype(F32)).astype(BF)
        if k == 0:
            own_ref[:, :hidden] = wide
        elif k == 2:
            x_keep[...] = wide
        else:
            x_send[k // 2] = wide
        for slab in range(keep_narrow.shape[1] // rows):
            here = slice(slab * rows, (slab + 1) * rows)
            columns = slice(slab * cut, (slab + 1) * cut)
            total = (keep_narrow[k, here, :].astype(F32) + came_narrow[k, here, :].astype(F32)).astype(BF)
            if k == 0:
                own_ref[:, hidden + slab * cut : hidden + (slab + 1) * cut] = total
            elif k == 1:
                y_keep[:, columns] = total
            else:
                y_send[k - 2, :, columns] = total


def weight_second_kernel(own_ref, x_keep, x_came, y_keep, y_came, sum_ref, x_send, y_send):
    hidden = x_keep.shape[1]
    sum_ref[:, :hidden] = own_ref[:, :hidden].astype(F32) + x_came[0].astype(F32)
    sum_ref[:, hidden:] = own_ref[:, hidden:].astype(F32) + y_came[0].astype(F32)
    x_send[...] = (x_keep[...].astype(F32) + x_came[1].astype(F32)).astype(BF)
    y_send[...] = (y_keep[...].astype(F32) + y_came[1].astype(F32)).astype(BF)


def weight_last_kernel(sum_ref, x_came, y_came, wide_ref, narrow_ref):
    rows, hidden = wide_ref.shape
    cut = narrow_ref.shape[0]
    wide_ref[...] = sum_ref[:, :hidden] + x_came[...].astype(F32)
    for slab in range(narrow_ref.shape[1] // rows):
        columns = slice(slab * cut, (slab + 1) * cut)
        piece = sum_ref[:, hidden + slab * cut : hidden + (slab + 1) * cut] + y_came[:, columns].astype(F32)
        narrow_ref[:, slab * rows : (slab + 1) * rows] = jnp.transpose(piece)


def as_column(row):
    return jnp.transpose(jnp.broadcast_to(row, (128, row.shape[1])))[:, :1]


def put_halves(spot, keep_ref, send_refs, columns, values):
    half, rows = keep_ref.shape[:2]
    held = half // len(send_refs)
    for block in range(2 * half):
        part = values[block * rows : (block + 1) * rows]
        at = (block // 2) ^ (spot // 2)

        @pl.when(spot % 2 == block % 2)
        def _():
            keep_ref[at, :, columns] = part

        for k, send_ref in enumerate(send_refs):

            @pl.when((spot % 2 != block % 2) & (at // held == k))
            def _():
                send_ref[at % held, :, columns] = part


EXACT = 32


def split_exact(values):
    lane = lax.broadcasted_iota(jnp.int32, values.shape, 1)
    high = values.astype(BF).astype(F32)
    mid = (values - high).astype(BF).astype(F32)
    low = values - high - mid
    band = (lane - EXACT) // 16
    mid, low = pltpu.roll(mid, 16, 1), pltpu.roll(low, 32, 1)
    return jnp.where(band == 0, high, jnp.where(band == 1, mid, jnp.where(band == 2, low, values)))


def join_exact(values):
    lane = lax.broadcasted_iota(jnp.int32, values.shape, 1)
    total = values + pltpu.roll(values, 128 - 16, 1) + pltpu.roll(values, 128 - 32, 1)
    return jnp.where((lane >= EXACT) & (lane < EXACT + 16), total, values)


def home_kernel(experts, slots, capacity, chunks, extra_rows, temper_ref, prior_ref, chosen_ref, rank_ref, pos_ref,
                residual_ref, upstream_ref, att_ref, projected_ref, table_ref, router_ref, gain_ref, shift_ref,
                wo_ref, *refs):
    back_refs = refs[:chunks]
    (weight_ref, grad_ref, att_grad_ref, delta_ref, outer_ref, extra_ref, tiny_ref, spots_ref, extra_sum) = refs[
        chunks:
    ]
    rows, width = residual_ref.shape
    route = projected_ref.shape[0]
    for k in range(chunks):
        spots_ref[k * slots : (k + 1) * slots, :] = back_refs[k][:slots, :]
    temper = temper_ref[0]
    table = table_ref[...]
    projected = projected_ref[...]
    scale, unit, table_scale, unit_table, logits = router_of(projected, table, temper)
    routed = softmax_rows(logits, experts)
    chosen = chosen_ref[...]
    selected = chosen == lax.broadcasted_iota(jnp.int32, logits.shape, 0)
    before = sum(jnp.where(chosen == expert, prior_ref[expert], 0) for expert in range(experts))
    kept = (before + rank_ref[...] < capacity).astype(F32)
    gate = jnp.sum(jnp.where(selected, routed, 0.0), axis=0, keepdims=True)
    weight = gate * kept
    weight_ref[...] = weight
    pos = pos_ref[...]
    gate_grad = jnp.zeros((1, rows), F32)
    for k in range(chunks):
        here = (lax.broadcasted_iota(jnp.int32, (slots, rows), 0) + k * slots == pos).astype(F32).astype(BF)
        gate_grad += jnp.sum(mxu(back_refs[k][slots:, :slots], here), axis=0, keepdims=True)
    gate_grad = gate_grad * kept
    logit_grad = gate_grad * routed * (selected.astype(F32) - gate)
    highest = dict(precision=lax.Precision.HIGHEST, preferred_element_type=F32)
    unit_grad = lax.dot_general(unit_table, logit_grad, TN, **highest) / temper
    table_grad = lax.dot_general(logit_grad, unit, NT, **highest) / temper
    sharp = -jnp.sum(logit_grad * logits, keepdims=True) / temper
    projected_grad = scale * unit_grad - scale * scale * scale * projected * jnp.sum(
        projected * unit_grad, axis=0, keepdims=True
    )
    padded = jnp.concatenate([projected_grad, jnp.zeros((128 - route, rows), F32)], axis=0)
    router = jnp.concatenate([router_ref[...], jnp.zeros((128 - route, width), F32)], axis=0)
    column = pos.astype(F32)
    both = jnp.transpose(jnp.concatenate([column, weight, jnp.zeros((126, rows), F32)], axis=0))
    routed_grad = jnp.transpose(padded)
    head_lane = lax.broadcasted_iota(jnp.int32, (width, 128), 1)
    heads = (lax.broadcasted_iota(jnp.int32, (width, 128), 0) // HEAD_DIM == head_lane).astype(F32).astype(BF)
    gain, shift = gain_ref[...], shift_ref[...]
    pos_column, weight_column = both[:, :1].astype(jnp.int32), both[:, 1:2]
    lanes = lax.broadcasted_iota(jnp.int32, (rows, spots_ref.shape[0]), 1)
    home = mxu((lanes == pos_column).astype(F32).astype(BF), spots_ref[...])
    y_grad = home * weight_column + mxu_wide(routed_grad, router)
    unit_two, norm_scale, normed_two = norm_of(residual_ref[...], gain, shift)
    inner = y_grad * gain
    two_part = norm_scale * (
        inner
        - jnp.mean(inner, axis=-1, keepdims=True)
        - unit_two * jnp.mean(inner * unit_two, axis=-1, keepdims=True)
    )
    residual_grad = upstream_ref[...].astype(F32) + two_part
    grad_ref[...] = residual_grad
    branch = residual_grad.astype(BF)
    att_grad = mxu(branch, wo_ref[...], NT).astype(BF)
    att_grad_ref[...] = att_grad
    product_high, product_low = split_high(att_grad.astype(F32) * att_ref[...].astype(F32))
    delta = mxu(product_high, heads) + mxu(product_low, heads)
    delta_ref[...] = jnp.transpose(delta)[: delta_ref.shape[0]]
    outer_ref[...] = mxu(jnp.transpose(att_ref[...]), branch).astype(BF)
    extra_sum[...] = jnp.zeros_like(extra_sum)
    extra_sum[:route, :] = mxu_wide(projected_grad, normed_two)
    extra_sum[route : route + 1, :] = jnp.sum(y_grad * unit_two, axis=0, keepdims=True)
    extra_sum[route + 1 : route + 2, :] = jnp.sum(y_grad, axis=0, keepdims=True)
    wide_table = jnp.concatenate([table, jnp.zeros((table.shape[0], 128 - route), F32)], axis=1)
    table_grad = jnp.concatenate([table_grad, jnp.zeros((table.shape[0], 128 - route), F32)], axis=1)
    summed = jnp.sum(wide_table * table_grad, axis=1, keepdims=True)
    table_grad = table_scale * table_grad - table_scale * table_scale * table_scale * wide_table * summed
    tiny = jnp.concatenate([table_grad, jnp.broadcast_to(sharp, (8, 128))], axis=0)
    tiny_ref[...] = tiny
    extra = jnp.transpose(extra_sum[...])
    if chunks <= 8:
        tiny = jnp.concatenate([tiny, jnp.zeros((128 - tiny.shape[0], 128), F32)], axis=0)
        tiny = pltpu.roll(jnp.transpose(tiny)[: extra_rows], EXACT, 1)
        lane = lax.broadcasted_iota(jnp.int32, tiny.shape, 1)
        tiny = split_exact(jnp.where((lane >= EXACT) & (lane < EXACT + 16), tiny, 0.0))
        tiny = jnp.concatenate([tiny] * (extra.shape[0] // extra_rows), axis=0)
        lane = lax.broadcasted_iota(jnp.int32, tiny.shape, 1)
        extra = jnp.where(lane < EXACT, extra, tiny)
    extra_ref[...] = extra.astype(BF)


def score_back_kernel(first, pairs, weights, spot_ref, label_ref, q_ref, k_ref, v_ref, att_grad_ref, lse_ref, delta_ref,
                      turned_ref, *refs):
    count = 3 + 3 * weights
    more_refs, out_refs, bias_ref = refs[: -1 - count], refs[-1 - count : -1], refs[-1]
    dq_ref, dk_ref, dv_ref = out_refs[:3]
    rows = label_ref.shape[2]
    low_lanes = lax.broadcasted_iota(jnp.int32, (rows, 128), 1) < HEAD_DIM
    for seq in range(label_ref.shape[0]):
        here = slice(seq * rows, (seq + 1) * rows)
        bias_ref[...] = same_label(label_ref[seq])
        for pair in range(pairs):
            there = slice(pair * 128, pair * 128 + 128)
            columns = slice((first + pair) * 128, (first + pair) * 128 + 128)
            q_pair, k_pair, v_pair = q_ref[here, columns], k_ref[here, columns], v_ref[here, columns]
            g_pair = att_grad_ref[here, columns]
            k_turned = jnp.transpose(k_pair)
            dk = jnp.zeros((rows, 128), F32)
            dv = jnp.zeros((rows, 128), F32)
            dq_turned = []
            for half in range(2):
                own = low_lanes if half == 0 else jnp.logical_not(low_lanes)
                q_own = jnp.where(own, q_pair.astype(F32), 0.0).astype(BF)
                g_own = jnp.where(own, g_pair.astype(F32), 0.0).astype(BF)
                head = (first + pair) * 2 + half
                head = slice(head, head + 1)
                probs = jnp.exp(mxu(k_pair, q_own, NT) + bias_ref[...] - lse_ref[head, here])
                prob_grad = mxu(v_pair, g_own, NT)
                score_grad = (probs * (prob_grad - delta_ref[head, here])).astype(BF)
                dv += mxu(probs.astype(BF), g_own)
                dk += mxu(score_grad, q_own)
                dq_turned.append(mxu(k_turned[half * HEAD_DIM : (half + 1) * HEAD_DIM], score_grad))
            dq = jnp.transpose(jnp.concatenate(dq_turned, axis=0)) * HEAD_DIM ** (-0.5)
            dq_ref[here, there] = dq.astype(BF)
            dk_ref[here, there] = dk.astype(BF)
            dv_ref[here, there] = dv.astype(BF)
    if weights:
        weight_grads(spot_ref[0], turned_ref, (dq_ref, dk_ref, dv_ref), more_refs, out_refs[3], out_refs[4:])


def weight_grads(spot, turned_ref, grad_refs, more_refs, keep_ref, send_refs):
    start = 0
    for ref in grad_refs:
        columns = slice(start, start + ref.shape[1])
        put_halves(spot, keep_ref, send_refs, columns, mxu(turned_ref[...], ref[...]).astype(BF))
        start += ref.shape[1]
    for more_ref in more_refs:
        columns = slice(start, start + more_ref.shape[1])
        put_halves(spot, keep_ref, send_refs, columns, more_ref[...])
        start += more_ref.shape[1]


def tokens_kernel(groups, spot_ref, turned_ref, x_ref, grad_ref, wq_ref, wk_ref, wv_ref, gain_ref, shift_ref, *refs):
    tokens_ref, keep_ref, send_ref, joined_ref, sums_ref, turned_sums_ref = refs[3 * groups :]
    one_grad = 0.0
    for part, w_ref in enumerate((wq_ref, wk_ref, wv_ref)):
        start = 0
        for group in range(groups):
            piece = refs[3 * group + part]
            joined_ref[part, :, start : start + piece.shape[1]] = piece[...]
            start += piece.shape[1]
        one_grad += mxu(joined_ref[part], w_ref[...], NT)
    unit, scale, _ = norm_of(x_ref[...].astype(F32), gain_ref[...], shift_ref[...])
    inner = one_grad * gain_ref[...]
    one_part = scale * (
        inner
        - jnp.mean(inner, axis=-1, keepdims=True)
        - unit * jnp.mean(inner * unit, axis=-1, keepdims=True)
    )
    tokens_ref[...] = (grad_ref[...] + one_part).astype(BF)
    sums_ref[...] = jnp.zeros_like(sums_ref)
    sums_ref[0:1, :] = jnp.sum(one_grad * unit, axis=0, keepdims=True)
    sums_ref[1:2, :] = jnp.sum(one_grad, axis=0, keepdims=True)
    turned_sums_ref[...] = jnp.transpose(sums_ref[...]).astype(BF)
    weight_grads(spot_ref[0], turned_ref, refs[3 * groups - 3 : 3 * groups], [turned_sums_ref], keep_ref, [send_ref])


def first_sum_kernel(exact, count, keep_ref, *refs):
    came_refs, out_refs = refs[:count], refs[count:]
    held = len(out_refs) // count
    for k, out_ref in enumerate(out_refs):
        came = came_refs[k // held][k % held].astype(F32)
        out_ref[...] = (keep_ref[k].astype(F32) + came).astype(BF)
        if exact is not None:
            here = slice(exact, exact + 128)
            out_ref[:, here] = split_exact(join_exact(keep_ref[k, :, here].astype(F32) + came[:, here])).astype(BF)


def second_sum_kernel(exact, place_ref, *refs):
    own_ref, send_refs, sum_ref = refs[4], refs[5:-1], refs[-1]
    sum_ref[...] = sum(ref[...].astype(F32) for ref in refs[:4])
    if exact is not None:
        sum_ref[:, exact : exact + 128] = split_exact(join_exact(sum_ref[:, exact : exact + 128]))
    size = own_ref.shape[0]
    group = len(send_refs) + 1
    own_ref[...] = sum_ref[pl.ds(pl.multiple_of(place_ref[0] * size, 8), size), :]
    if len(send_refs) == 1:
        (send_ref,) = send_refs
        filler = jnp.zeros((send_ref.shape[1] - size, send_ref.shape[2]), F32)
        for k in range(send_ref.shape[0]):
            block = jnp.where(place_ref[0] == k, 0.0, sum_ref[k * size : (k + 1) * size, :])
            send_ref[k] = jnp.concatenate([block, filler], axis=0).astype(BF)
        return
    for k, send_ref in enumerate(send_refs):
        there = lax.rem(place_ref[0] + k + 1, group)
        block = sum_ref[pl.ds(pl.multiple_of(there * size, 8), size), :]
        filler = jnp.zeros((send_ref.shape[0] - size, block.shape[1]), F32)
        send_ref[...] = jnp.concatenate([block, filler], axis=0).astype(BF)


def last_sum_kernel(first, last, route, group, experts_padded, counts, *refs):
    query_ref, key_ref, value_ref, outer_ref, router_ref, norms_ref, table_ref, sharp_ref = refs[sum(counts) :]
    rows, width = outer_ref.shape

    def total(parts, columns):
        value = parts[0][:, columns]
        for ref in parts[1:]:
            for sent in [ref] if len(ref.shape) == 2 else [ref.at[k] for k in range(ref.shape[0])]:
                value = value + sent[:, columns].astype(F32)[:rows]
        return value

    def turned(extra):
        return jnp.transpose(jnp.concatenate([extra, jnp.zeros((128 - rows, 128), F32)], axis=0))

    early, late = refs[: counts[0]], refs[counts[0] : sum(counts)]
    for part, ref in enumerate((query_ref, key_ref, value_ref)):
        ref[:, :first] = total(early, slice(part * first, (part + 1) * first))
        ref[:, first:] = total(late, slice(part * last, (part + 1) * last))
    outer_ref[...] = total(early, slice(3 * first, 3 * first + width))
    extra = join_exact(total(early, slice(3 * first + width, 3 * first + width + 128)))
    router_ref[...] = extra[:, :route]
    extra = turned(extra)
    norms = turned(total(late, slice(3 * last, 3 * last + 128)))
    norms_ref[...] = jnp.concatenate([norms[:2, :rows], extra[route : route + 2, :rows]], axis=0)
    table_ref[...] = extra[EXACT : EXACT + group, :route]
    sharp_ref[...] = extra[EXACT + experts_padded : EXACT + experts_padded + 1, :1]


def output_kernel(place_ref, residual_ref, weight_ref, pos_ref, out_ref, layer_ref, spots_ref):
    chunks, slots = out_ref.shape[:2]
    for k in range(chunks):
        spots_ref[k * slots : (k + 1) * slots, :] = out_ref[lax.rem(place_ref[0] + k, chunks)]
    rows = residual_ref.shape[0]
    both = jnp.concatenate([pos_ref[...].astype(F32), weight_ref[...], jnp.zeros((126, rows), F32)], axis=0)
    both = jnp.transpose(both)
    pos_column, weight_column = both[:, :1].astype(jnp.int32), both[:, 1:2]
    lanes = lax.broadcasted_iota(jnp.int32, (rows, spots_ref.shape[0]), 1)
    home = mxu((lanes == pos_column).astype(F32).astype(BF), spots_ref[...])
    layer_ref[...] = (residual_ref[...] + home * weight_column).astype(BF)


def swap(values, axis, mask):
    size = lax.axis_size(axis)
    return lax.ppermute(values, axis, [(i, i ^ mask) for i in range(size)])


def shift(values, axis, step):
    size = lax.axis_size(axis)
    return lax.ppermute(values, axis, [(i, (i + step) % size) for i in range(size)])


def pick(values, index, axis):
    return lax.dynamic_index_in_dim(values, index, axis, keepdims=False)


def held(arrays, deps):
    anywhere = pl.BlockSpec(memory_space=pl.ANY)
    return kernel_call(
        lambda *refs: None,
        0,
        deps,
        in_specs=[anywhere] * len(arrays),
        out_specs=[anywhere] * len(arrays),
        out_shape=[jax.ShapeDtypeStruct(array.shape, array.dtype) for array in arrays],
        input_output_aliases={k: k for k in range(len(arrays))},
    )(*arrays)[0]


def first_sum(keep, sends, exact, deps, weight):
    half, rows, width = keep.shape
    return kernel_call(
        partial(first_sum_kernel, exact, len(sends)),
        weight,
        deps,
        vmem=SUM1_VMEM,
        in_specs=[pl.BlockSpec()] * (1 + len(sends)),
        out_shape=[jax.ShapeDtypeStruct((rows, width), BF)] * half,
    )(keep, *[swap(send, "dp", 1) for send in sends])


def second_sum(parts, place_vec, exact, deps, weight, together=False):
    group = lax.axis_size("expert")
    came = [parts[0]] + [swap(parts[k], "dp", 2 * k) for k in range(1, len(parts))]
    rows, width = parts[0].shape
    if group > 8:
        return [sum(part.astype(F32) for part in came)], ()
    size = rows // group
    padded = (size + 15) // 16 * 16
    sd = jax.ShapeDtypeStruct
    return kernel_call(
        partial(second_sum_kernel, exact),
        weight,
        deps,
        vmem=SUM2_VMEM,
        in_specs=[pl.BlockSpec(memory_space=pltpu.SMEM)] + [pl.BlockSpec()] * len(came),
        out_shape=[sd((size, width), F32)]
        + ([sd((group, padded, width), BF)] if together else [sd((padded, width), BF)] * (group - 1)),
        scratch_shapes=[pltpu.VMEM((rows, width), F32)],
    )(place_vec, *came)


def sent_on(parts):
    if lax.axis_size("expert") > 8:
        return [lax.psum_scatter(parts[0], "expert", scatter_dimension=0, tiled=True)]
    if len(parts) == 2:
        return [parts[0], lax.all_to_all(parts[1], "expert", 0, 0, tiled=True)]
    return [parts[0]] + [shift(parts[k], "expert", k) for k in range(1, len(parts))]


def small_sum(values):
    group = lax.axis_size("expert")
    if group > 8:
        return lax.psum(values, ("dp", "expert"))
    values = values + swap(values, "dp", 1)
    values = values + sum(swap(values, "dp", mask) for mask in range(2, lax.axis_size("dp"), 2))
    return values + sum(shift(values, "expert", k) for k in range(1, group))


def exchange(blocks, sign):
    size = lax.axis_size("expert")
    if size <= 8:
        return [blocks[0]] + [shift(blocks[k], "expert", sign * k) for k in range(1, size)]
    stacked = jnp.stack(blocks)
    place = lax.axis_index("expert")
    across = (jnp.arange(size) - place) * sign % size
    there = lax.all_to_all(stacked[across], "expert", 0, 0, tiled=True)
    source = (place - sign * jnp.arange(size)) % size
    home = there[source]
    return [home[k] for k in range(size)]


WAYS = 4
SETS = ((0,), (1, 3), (2,))
CUTS = (512, 256)
D0_WEIGHT, D1_WEIGHT, FIRST_WEIGHT, TOKENS_WEIGHT = 0.1, 0.1, 0.05, 0.1
MID_WEIGHT, LATE_FIRST_WEIGHT, SECOND_WEIGHT, LATE_SECOND_WEIGHT, LAST_WEIGHT, OUTPUT_WEIGHT = 18, 1, 1, 7, 0.1, 0.1


def body(
    layer_inputs_matrix,
    upstream_output_sensitivity,
    mixer_layernorm_scale,
    mixer_layernorm_offset,
    asker_matrix,
    lookup_label_matrix,
    content_matrix,
    mixer_result_matrix,
    specialist_layernorm_scale,
    specialist_layernorm_offset,
    dispatch_projection_matrix,
    specialist_centroids,
    learned_sharpness,
    specialist_widening_matrix,
    specialist_narrowing_matrix,
    document_labels,
    chosen_specialist,
    placement_ranks,
):
    rows, width = layer_inputs_matrix.shape
    seqs, length = document_labels.shape
    head_count = width // HEAD_DIM
    group = lax.axis_size("expert")
    place = lax.axis_index("expert")
    dp_size = lax.axis_size("dp")
    wide, narrow = specialist_widening_matrix[0], specialist_narrowing_matrix[0]
    hidden = wide.shape[1]
    route = dispatch_projection_matrix.shape[1]
    slots = 3 * rows // (2 * group)
    spots = group * slots
    experts_padded = (group + 7) // 8 * 8
    sd = jax.ShapeDtypeStruct
    smem, vmem = (pl.BlockSpec(memory_space=space) for space in (pltpu.SMEM, pltpu.VMEM))
    int32 = jnp.int32
    place_vec = place.astype(int32).reshape(1)
    spot_vec = lax.axis_index("dp").astype(int32).reshape(1)
    vec = lambda v: v.reshape(1, -1)
    gain_one, shift_one = vec(mixer_layernorm_scale), vec(mixer_layernorm_offset)
    gain_two, shift_two = vec(specialist_layernorm_scale), vec(specialist_layernorm_offset)
    router = dispatch_projection_matrix.T
    table = jnp.zeros((experts_padded, route), F32).at[:group].set(specialist_centroids)
    labels = document_labels.reshape(seqs, 1, length)
    chosen = chosen_specialist.reshape(1, rows)

    row_block = pl.BlockSpec((length, width), lambda s: (s, 0))
    line = pl.BlockSpec((1, length), lambda s: (0, s))
    label_spec = pl.BlockSpec((1, 1, length), lambda s: (s, 0, 0))
    turned_block = pl.BlockSpec((width, length), lambda s: (0, s))
    heads_block = pl.BlockSpec((16, length), lambda s: (0, s))
    weight_spec = whole((width, width))
    vec_spec = whole((1, width))
    chunk_spec, tailed_spec = whole((slots, width)), whole((slots + TAIL, width))
    table_spec = whole((experts_padded, route))

    tailed = slots + TAIL
    (pos, rank, upstream_sent), _ = kernel_call(
        partial(route_kernel, slots),
        5,
        vmem=ROUTE_VMEM,
        in_specs=[smem] + [pl.BlockSpec()] * 3,
        out_shape=[sd((1, rows), int32)] * 2 + [pltpu.HBM((group, tailed, width), BF)],
    )(place_vec, placement_ranks, chosen, upstream_output_sensitivity)
    upstream_there = lax.all_to_all(upstream_sent, "expert", 0, 0, tiled=True)

    (turned, queries, keys, values, attended, lse, residual, projected, *entering_sent), _ = kernel_call(
        partial(attend_kernel, group, slots),
        20,
        vmem=ATTEND_VMEM,
        grid=(seqs,),
        in_specs=[row_block, label_spec] + [vec_spec] * 2 + [weight_spec] * 4 + [vec_spec] * 2
        + [whole((route, width)), table_spec, smem, line, line],
        out_specs=[turned_block] + [row_block] * 4
        + [heads_block, row_block, pl.BlockSpec((route, length), lambda s: (0, s))] + [tailed_spec] * group,
        out_shape=[pltpu.HBM((width, rows), BF)] + [pltpu.HBM((rows, width), BF)] * 4
        + [sd((16, rows), F32), pltpu.HBM((rows, width), F32), sd((route, rows), F32)]
        + [pltpu.HBM((tailed, width), BF)] * group,
        scratch_shapes=[pltpu.VMEM((length, length), F32), pltpu.VMEM((length, 128), F32)],
    )(
        layer_inputs_matrix, labels, gain_one, shift_one, asker_matrix, lookup_label_matrix,
        content_matrix, mixer_result_matrix, gain_two, shift_two, router, table, learned_sharpness, chosen, pos,
    )
    tails = upstream_there[:, slots : slots + 2, :experts_padded].astype(F32)
    tallies = (tails[:, 0] * 256.0 + tails[:, 1]).astype(int32)
    sources = jnp.arange(group)
    prior = jnp.sum(jnp.where(sources[:, None] < place, tallies, 0), axis=0)
    named = jnp.sum(jnp.where(jnp.arange(experts_padded) == place, tallies, 0), axis=1)
    earlier = jnp.sum(jnp.where(sources[:, None] < sources[None, :], named[:, None], 0), axis=0)
    counts = jnp.clip(rows - earlier, 0, named)
    relative = (place - sources) % group
    counts = jnp.sum(jnp.where(relative[:, None] == sources[None, :], counts[None, :], 0), axis=1)

    each = group // WAYS
    backs, produced, acts, pres, order = [None] * WAYS, [], [], [], []

    def experts(ids, counts, entered, graded, turn, deps):
        out, some, act, pre, done = expert_call(
            counts, turn, ids, produced, entered, graded, wide, narrow, [deps, order]
        )
        produced[:] = [out]
        for k, back in zip(ids, some):
            backs[k] = back
        acts.append(act)
        pres.append(pre)
        order.append(done)

    if each == 1:
        split = lambda chunks, _: list(chunks)
        turn_vec, graded, entered = place_vec, upstream_there, list(entering_sent)
        alone = jnp.sum((chosen == place).astype(int32)).reshape(1)
        experts(SETS[0], alone, entered[:1], upstream_sent, turn_vec, ())
        ready = upstream_there
        for ids in SETS[1:]:
            for k, sent in zip(ids, held([entered[k] for k in ids], [ready, order[0]])):
                entered[k] = shift(sent, "expert", k)
            ready = [entered[k] for k in ids]
        for ids in SETS[1:]:
            experts(ids, counts, [entered[k] for k in ids], graded, turn_vec, prior)
    else:
        entering_there = exchange(entering_sent, 1)
        valid = jnp.arange(slots)[None, :] < counts[:, None]
        counts = jnp.full((WAYS,), each * slots, int32)
        turn_vec = jnp.zeros((1,), int32)

        def join(blocks, masks):
            chunks = []
            for k in range(0, group, each):
                tail = [jnp.where(masks[j], blocks[j][slots:, :slots], 0) for j in range(k, k + each)]
                tail = jnp.concatenate(tail, axis=1)
                tail = jnp.pad(tail, ((0, 0), (0, width - tail.shape[1])))
                chunks.append(jnp.concatenate([blocks[j][:slots] for j in range(k, k + each)] + [tail]))
            return chunks

        def split(chunks, with_tail):
            pieces = []
            for chunk in chunks:
                for j in range(each):
                    piece = chunk[j * slots : (j + 1) * slots]
                    if with_tail:
                        tail = chunk[each * slots :, j * slots : (j + 1) * slots]
                        piece = jnp.concatenate([piece, jnp.pad(tail, ((0, 0), (0, width - slots)))])
                    pieces.append(piece)
            return pieces

        entered = join(entering_there, valid)
        graded = join([pick(upstream_there, relative[k], 0) for k in range(group)], valid)
        graded = jnp.stack([graded[-k % WAYS] for k in range(WAYS)])
        for ids in SETS:
            experts(ids, counts, [entered[k] for k in ids], graded, turn_vec, ())
    returned_home = exchange(split(backs, True), -1)
    ordered = [k for ids in SETS for k in ids]
    arrange = lambda chunks: [chunks[k] for k in ordered]
    depth = rows + 128 if each == 1 else spots
    keep_wide, send_wide, keep_narrow, send_narrow = weight_calls(
        counts, spot_vec, turn_vec, SETS, arrange(entered), graded, acts, pres, dp_size, depth,
        [returned_home[k] for k in SETS[1]],
    )
    half, block = dp_size // 2, width // dp_size
    (weight, residual_grad, attended_grad, delta, outer_part, extra_part, tiny), done = kernel_call(
        partial(home_kernel, group, slots, rows, group, width // (dp_size * group)),
        500,
        vmem=HOME_VMEM,
        in_specs=[smem, smem] + [vmem] * (12 + group),
        out_specs=[vmem] * 7,
        out_shape=[sd((1, rows), F32), sd((rows, width), F32), sd((rows, width), BF), sd((16, rows), F32),
                   sd((width, width), BF), sd((width, 128), BF), sd((experts_padded + 8, 128), F32)],
        scratch_shapes=[pltpu.VMEM((spots, width), BF), pltpu.VMEM((128, width), F32)],
    )(
        learned_sharpness, prior, chosen, rank, pos, residual, upstream_output_sensitivity, attended,
        projected, table, router, gain_two, shift_two, mixer_result_matrix, *returned_home,
    )
    half_rows = sd((block, hidden), BF)
    (weight_own, x_keep, x_send, y_keep, y_send), first_done = kernel_call(
        weight_first_kernel,
        1,
        done,
        vmem=SUM3_VMEM,
        in_specs=[pl.BlockSpec()] * 4,
        out_shape=[sd((block, 2 * hidden), BF)] + [half_rows, sd((2, block, hidden), BF)] * 2,
    )(keep_wide, swap(send_wide, "dp", 1), keep_narrow, swap(send_narrow, "dp", 1))
    (produced,) = held(produced, first_done)
    if each > 1:
        produced = jnp.stack(split([produced[-k % WAYS] for k in range(WAYS)], False))[relative]
    produced_home = lax.all_to_all(produced, "expert", 0, 0, tiled=True)

    pieces, start, done = [], 0, first_done
    for cut in CUTS:
        early = start == 0
        more = [outer_part, extra_part] if early else []
        columns = 3 * cut + width + 128
        pack = [sd((half, block, columns), BF)] + [sd((half // 2, block, columns), BF)] * 2 if early else []
        grads, done = kernel_call(
            partial(score_back_kernel, start // 128, cut // 128, early),
            D0_WEIGHT if early else D1_WEIGHT,
            done,
            vmem=SCORE_VMEM,
            in_specs=[smem] + [vmem] * (8 + len(more)),
            out_specs=[vmem] * (3 + len(pack)),
            out_shape=[sd((rows, cut), BF)] * 3 + pack,
            scratch_shapes=[pltpu.VMEM((length, length), F32)],
        )(spot_vec, labels, queries, keys, values, attended_grad, lse, delta, turned, *more)
        pieces.append(grads[:3])
        if early:
            keep, *sends = grads[3:]
        start += cut
    first, last = CUTS
    exact = 3 * first + width
    early, done = first_sum(keep, sends, exact, done, FIRST_WEIGHT)
    pack = sd((half, block, 3 * last + 128), BF)
    (tokens_grad, keep, send), done = kernel_call(
        partial(tokens_kernel, len(CUTS)),
        TOKENS_WEIGHT,
        done,
        vmem=TOKENS_VMEM,
        in_specs=[smem] + [vmem] * (8 + 3 * len(CUTS)),
        out_specs=[vmem] * 3,
        out_shape=[sd((rows, width), BF)] + [pack] * 2,
        scratch_shapes=[pltpu.VMEM((3, rows, width), BF), pltpu.VMEM((128, width), F32), pltpu.VMEM((width, 128), BF)],
    )(spot_vec, turned, layer_inputs_matrix, residual_grad, asker_matrix, lookup_label_matrix, content_matrix,
      gain_one, shift_one, *[piece for group_pieces in pieces for piece in group_pieces])
    (weight_sum, x_more, y_more), done = kernel_call(
        weight_second_kernel,
        MID_WEIGHT,
        done,
        vmem=SUM4_VMEM,
        in_specs=[pl.BlockSpec()] * 5,
        out_shape=[sd((block, 2 * hidden), F32)] + [half_rows] * 2,
    )(weight_own, x_keep, swap(x_send, "dp", 2), y_keep, swap(y_send, "dp", 4))
    late, done = first_sum(keep, [send], None, done, LATE_FIRST_WEIGHT)
    early, done = second_sum(early, place_vec, exact, done, SECOND_WEIGHT, True)
    x_more, y_more = held([x_more, y_more], done)
    late, done = second_sum(late, place_vec, None, done, LATE_SECOND_WEIGHT)
    (layer_output,), done = kernel_call(
        output_kernel,
        OUTPUT_WEIGHT,
        done,
        vmem=OUTPUT_VMEM,
        in_specs=[smem] + [vmem] * 4,
        out_specs=[vmem],
        out_shape=[sd((rows, width), BF)],
        scratch_shapes=[pltpu.VMEM((spots, width), BF)],
    )(place_vec, residual, weight, pos, produced_home)
    early, late = sent_on(early), sent_on(late)
    own = width // (dp_size * group)
    (query_grad, key_grad, value_grad, outer_grad, router_grad, norms, table_grad, sharp), done = kernel_call(
        partial(last_sum_kernel, first, last, route, group, experts_padded, (len(early), len(late))),
        1,
        done,
        vmem=SUM6_VMEM,
        in_specs=[pl.BlockSpec()] * (len(early) + len(late)),
        out_shape=[sd((own, width), F32)] * 4
        + [sd((own, route), F32), sd((4, own), F32), sd((group, route), F32), sd((1, 1), F32)],
    )(*early, *late)
    (hidden_grad, return_grad), done = kernel_call(
        weight_last_kernel,
        LAST_WEIGHT,
        done,
        vmem=SUM5_VMEM,
        in_specs=[pl.BlockSpec()] * 3,
        out_shape=[sd((block, hidden), F32), sd((hidden // dp_size, width), F32)],
    )(weight_sum, swap(x_more, "dp", 4), swap(y_more, "dp", 2))
    if group > 8:
        tiny = small_sum(tiny)
        table_grad, sharp = tiny[:group, :route], tiny[experts_padded, :1]
    return (
        layer_output,
        tokens_grad,
        norms[0],
        norms[1],
        query_grad,
        key_grad,
        value_grad,
        outer_grad,
        norms[2],
        norms[3],
        router_grad,
        table_grad,
        sharp.reshape(1),
        hidden_grad[None],
        return_grad[None],
    )


def solution(mesh):
    placed = (
        P(("dp", "expert"), None),
        P(("dp", "expert"), None),
        P(),
        P(),
        P(),
        P(),
        P(),
        P(),
        P(),
        P(),
        P(),
        P(),
        P(),
        P("expert", None, None),
        P("expert", None, None),
        P(("dp", "expert"), None),
        P(("dp", "expert"), None),
        P(("dp", "expert"), None),
    )
    return jax.shard_map(
        body,
        mesh=mesh,
        in_specs=placed,
        out_specs=(
            P(("dp", "expert"), None),
            P(("dp", "expert"), None),
            P(("dp", "expert")),
            P(("dp", "expert")),
            P(("dp", "expert"), None),
            P(("dp", "expert"), None),
            P(("dp", "expert"), None),
            P(("dp", "expert"), None),
            P(("dp", "expert")),
            P(("dp", "expert")),
            P(("dp", "expert"), None),
            P(),
            P(),
            P("expert", "dp", None),
            P("expert", "dp", None),
        ),
        check_vma=False,
    )
```

```python
from functools import partial

import jax
import jax.numpy as jnp
from jax import lax
from jax.experimental import pallas as pl
from jax.experimental.pallas import tpu as pltpu
from jax.sharding import PartitionSpec as P

HEAD_DIM = 64
EPSILON = 1e-05
MASKED = -1e30
BF = jnp.bfloat16
F32 = jnp.float32
TAIL = 16
ROUTE_VMEM = 24
ATTEND_VMEM = 54
HOME_VMEM = 18
SCORE_VMEM = 12
TOKENS_VMEM = 18
OUTPUT_VMEM = 10
WIDE_VMEM = 28
NARROW_VMEM = 28
SUM1_VMEM = 8
SUM2_VMEM = 8
SUM3_VMEM = 10
SUM4_VMEM = 8
SUM5_VMEM = 8
SUM6_VMEM = 8
EXPERT_VMEM = (28, 38)
NN = (((1,), (0,)), ((), ()))
NT = (((1,), (1,)), ((), ()))
TN = (((0,), (0,)), ((), ()))


def mxu(left, right, dims=NN):
    return lax.dot_general(left, right, dims, preferred_element_type=F32)


def split_high(values):
    high = values.astype(BF)
    low = (values - high.astype(F32)).astype(BF)
    return high, low


def mxu_wide(left, right, dims=NN):
    left_high, left_low = split_high(left)
    right_high, right_low = split_high(right)
    return (
        mxu(left_high, right_high, dims)
        + mxu(left_high, right_low, dims)
        + mxu(left_low, right_high, dims)
    )


def kernel_call(body, weight, deps=(), vmem=2, **kwargs):
    deps = jax.tree.leaves(deps)
    inputs, outputs = len(kwargs["in_specs"]), len(kwargs["out_shape"])
    first = inputs + len(deps)
    kwargs["in_specs"] = list(kwargs["in_specs"]) + [
        pl.BlockSpec((1,) * (dep.ndim - 2) + (min(16, dep.shape[-2]), 128), lambda *_, rank=dep.ndim: (0,) * rank)
        if dep.ndim > 1 and "grid" in kwargs
        else pl.BlockSpec(memory_space=pl.ANY)
        for dep in deps
    ]
    kwargs["out_shape"] = list(kwargs["out_shape"]) + [jax.ShapeDtypeStruct((8, 128), F32)]
    if "out_specs" in kwargs:
        done_spec = whole((8, 128)) if "grid" in kwargs else pl.BlockSpec(memory_space=pltpu.VMEM)
        kwargs["out_specs"] = list(kwargs["out_specs"]) + [done_spec]

    def run(*refs):
        refs[first + outputs][...] = jnp.zeros((8, 128), F32)
        body(*refs[:inputs], *refs[first : first + outputs], *refs[first + outputs + 1 :])

    call = pl.pallas_call(
        run,
        compiler_params=pltpu.CompilerParams(
            vmem_limit_bytes=vmem * 2**20,
            dimension_semantics=("arbitrary",) * len(kwargs.get("grid", ())),
        ),
        cost_estimate=pl.CostEstimate(flops=int(weight * 2**30), bytes_accessed=0, transcendentals=0),
        **kwargs,
    )

    def made(*args):
        *outs, done = call(*args, *deps)
        return outs, done

    return made


def hbm(array):
    return pltpu.with_memory_space_constraint(array, pltpu.HBM)


def whole(shape):
    return pl.BlockSpec(shape, lambda *_: (0,) * len(shape))


def route_kernel(slots, place_ref, order_ref, chosen_ref, rows_ref, pos_ref, rank_ref, sent_ref):
    group = sent_ref.shape[0]
    order = order_ref[...].astype(F32)
    count = order.shape[1]
    chosen = chosen_ref[...]
    chosen_wide = jnp.transpose(jnp.broadcast_to(chosen.astype(F32), (128, count)))
    order_col = jnp.transpose(jnp.broadcast_to(order, (128, count)))[:, :1]
    before = (order_col < order) & (chosen_wide[:, :1] == chosen.astype(F32))
    rank = jnp.sum(before.astype(F32), axis=0, keepdims=True).astype(jnp.int32)
    place = place_ref[0]
    pos = jnp.where(chosen >= place, chosen - place, chosen - place + group) * slots + rank
    pos_ref[...] = pos
    rank_ref[...] = rank
    lanes = lax.broadcasted_iota(jnp.int32, (count, 128), 1).astype(F32)
    rows = rows_ref[...]
    tally = jnp.sum((chosen_wide == lanes).astype(F32), axis=0, keepdims=True)
    upper = jnp.floor(tally * (1.0 / 256.0))
    place_row = lax.broadcasted_iota(jnp.int32, (TAIL, 128), 0)
    tail = jnp.where(place_row == 0, upper, jnp.where(place_row == 1, tally - 256.0 * upper, 0.0))
    tail = jnp.concatenate([tail, jnp.zeros((TAIL, rows.shape[1] - 128), F32)], axis=1).astype(BF)
    for k in range(group):
        spots = lax.broadcasted_iota(jnp.int32, (slots, count), 0) + k * slots
        sent_ref[k, :slots, :] = mxu((spots == chosen * slots + rank).astype(F32).astype(BF), rows).astype(BF)
        sent_ref[k, slots:, :] = tail


def norm_of(values, gain, shift):
    centered = values - jnp.mean(values, axis=-1, keepdims=True)
    scale = lax.rsqrt(jnp.mean(centered * centered, axis=-1, keepdims=True) + EPSILON)
    unit = centered * scale
    return unit, scale, unit * gain + shift


def router_of(projected, table, temper):
    scale = lax.rsqrt(jnp.sum(projected * projected, axis=0, keepdims=True) + 1.0)
    unit = projected * scale
    table_scale = lax.rsqrt(jnp.sum(table * table, axis=1, keepdims=True) + 1.0)
    unit_table = table * table_scale
    logits = lax.dot_general(
        unit_table, unit, NN, precision=lax.Precision.HIGHEST, preferred_element_type=F32
    ) / temper
    return scale, unit, table_scale, unit_table, logits


def softmax_rows(logits, experts):
    valid = lax.broadcasted_iota(jnp.int32, logits.shape, 0) < experts
    logits = jnp.where(valid, logits, MASKED)
    weights = jnp.exp(logits - jnp.max(logits, axis=0, keepdims=True))
    return weights / jnp.sum(weights, axis=0, keepdims=True)


def same_label(labels):
    labels = labels.astype(F32)
    column = jnp.transpose(jnp.broadcast_to(labels, (128, labels.shape[1])))[:, :1]
    return jnp.where(column == labels, 0.0, MASKED)


def attend_kernel(experts, slots, x_ref, label_ref, gain_one_ref, shift_one_ref, wq_ref,
                  wk_ref, wv_ref, wo_ref, gain_two_ref, shift_two_ref, router_ref, table_ref, temper_ref,
                  chosen_ref, pos_ref, turned_ref, q_ref, k_ref, v_ref, att_ref, lse_ref, residual_ref,
                  projected_ref, *rest):
    sent_refs, bias_ref, lse_cols_ref = rest[:-2], rest[-2], rest[-1]
    step = pl.program_id(0)
    x = x_ref[...].astype(F32)
    rows, width = x.shape
    normed = norm_of(x, gain_one_ref[...], shift_one_ref[...])[2].astype(BF)
    turned_ref[...] = jnp.transpose(normed)
    q_ref[...] = (mxu(normed, wq_ref[...]).astype(BF).astype(F32) * HEAD_DIM ** (-0.5)).astype(BF)
    k_ref[...] = mxu(normed, wk_ref[...]).astype(BF)
    v_ref[...] = mxu(normed, wv_ref[...]).astype(BF)
    bias_ref[...] = same_label(label_ref[0])
    lane = lax.broadcasted_iota(jnp.int32, (rows, 128), 1)
    low_lanes = lane < HEAD_DIM
    lse_cols = jnp.zeros((rows, 128), F32)
    for pair in range(width // 128):
        columns = slice(pair * 128, pair * 128 + 128)
        q_pair, k_pair, v_pair = q_ref[:, columns], k_ref[:, columns], v_ref[:, columns]
        outs = []
        for half in range(2):
            own = low_lanes if half == 0 else jnp.logical_not(low_lanes)
            q_own = jnp.where(own, q_pair.astype(F32), 0.0).astype(BF)
            scores = mxu(q_own, k_pair, NT) + bias_ref[...]
            largest = jnp.max(scores, axis=-1, keepdims=True)
            weights = jnp.exp(scores - largest)
            total = jnp.sum(weights, axis=-1, keepdims=True)
            outs.append(mxu((weights * (1.0 / total)).astype(BF), v_pair))
            lse_cols = jnp.where(lane == pair * 2 + half, largest + jnp.log(total), lse_cols)
        att_ref[:, columns] = jnp.where(low_lanes, outs[0], outs[1]).astype(BF)
    lse_cols_ref[...] = lse_cols
    lse_ref[...] = jnp.transpose(lse_cols_ref[...])[: lse_ref.shape[0]]
    residual = x + mxu(att_ref[...], wo_ref[...])
    residual_ref[...] = residual
    normed_two = norm_of(residual, gain_two_ref[...], shift_two_ref[...])[2]
    projected = lax.dot_general(
        router_ref[...], normed_two, NT, precision=lax.Precision.HIGHEST, preferred_element_type=F32
    )
    projected_ref[...] = projected
    logits = router_of(projected, table_ref[...], temper_ref[0])[4]
    routed = softmax_rows(logits, experts)
    selected = chosen_ref[...] == lax.broadcasted_iota(jnp.int32, logits.shape, 0)
    gate = jnp.sum(jnp.where(selected, routed, 0.0), axis=0, keepdims=True)
    high = gate.astype(BF).astype(F32)
    mid = (gate - high).astype(BF).astype(F32)
    low = gate - high - mid
    place = lax.broadcasted_iota(jnp.int32, (TAIL, rows), 0)
    pieces = jnp.where(place == 0, high, jnp.where(place == 1, mid, jnp.where(place == 2, low, 0.0)))
    pieces = pieces.astype(BF)
    entering = normed_two.astype(BF)
    pos = pos_ref[...]
    for k in range(len(sent_refs)):
        spots = lax.broadcasted_iota(jnp.int32, (slots, rows), 0) + k * slots
        here = (spots == pos).astype(F32).astype(BF)
        sent = mxu(here, entering)
        gates = mxu(pieces, here, NT)
        tail = jnp.concatenate([gates, jnp.zeros((TAIL, width - slots), F32)], axis=1)

        @pl.when(step == 0)
        def _():
            sent_refs[k][:slots, :] = sent.astype(BF)
            sent_refs[k][slots:, :] = tail.astype(BF)

        @pl.when(step > 0)
        def _():
            sent_refs[k][:slots, :] = (sent_refs[k][:slots, :].astype(F32) + sent).astype(BF)
            sent_refs[k][slots:, :] = (sent_refs[k][slots:, :].astype(F32) + tail).astype(BF)


def gelu_parts(values):
    share = 0.5 * lax.erf(values * 0.5**0.5) + 0.5
    return share, jnp.exp(values * values * (-0.5)) * (2.0 * 3.141592653589793) ** (-0.5)


def pack_offsets(counts_ref, ids):
    offsets, total = [], 0
    for k in ids:
        offsets.append(pl.multiple_of(total, 16))
        total = total + (counts_ref[k] + 15) // 16 * 16
    return offsets, total


def source_of(place_ref, k, group):
    return lax.rem(place_ref[0] - k + group, group)


def expert_kernel(ids, block, counts_ref, place_ref, u_ref, *refs):
    chunks = len(ids)
    x_refs = refs[:chunks]
    wide_ref, narrow_ref = refs[chunks : chunks + 2]
    rest = refs[chunks + 2 :]
    out_refs, back_refs = rest[:chunks], rest[chunks : 2 * chunks]
    act_ref, pre_ref, xs, us, out_sum, back_sum, sums = rest[2 * chunks :]
    step, steps = pl.program_id(0), pl.num_programs(0)
    rows = x_refs[0].shape[0] - TAIL
    offsets, total = pack_offsets(counts_ref, ids)

    @pl.when(step == 0)
    def _():
        xs[...] = jnp.zeros_like(xs)
        us[...] = jnp.zeros_like(us)
        out_sum[...] = jnp.zeros_like(out_sum)
        back_sum[...] = jnp.zeros_like(back_sum)
        for k in range(chunks):
            xs[pl.ds(offsets[k], rows), :] = x_refs[k][:rows, :]
            us[pl.ds(offsets[k], rows), :] = u_ref[source_of(place_ref, ids[k], u_ref.shape[0]), :rows, :]

    def one(i, carry):
        here = pl.ds(pl.multiple_of(i * block, block), block)
        wide, narrow = wide_ref[...], narrow_ref[...]
        hidden = mxu(xs[here, :], wide)
        grad = mxu(us[here, :], narrow, NT)
        share, density = gelu_parts(hidden)
        act = (hidden * share).astype(BF)
        act_ref[here, :] = act
        pre = (grad * (share + hidden * density)).astype(BF)
        pre_ref[here, :] = pre
        out_sum[here, :] += mxu(act, narrow)
        back_sum[here, :] += mxu(pre, wide, NT)
        return carry

    blocks = (total + block - 1) // block
    lax.fori_loop(0, blocks, one, 0)

    def none(i, carry):
        here = pl.ds(pl.multiple_of(i * block, block), block)
        act_ref[here, :] = jnp.zeros((block, act_ref.shape[1]), BF)
        pre_ref[here, :] = jnp.zeros((block, pre_ref.shape[1]), BF)
        return carry

    lax.fori_loop(blocks, act_ref.shape[0] // block, none, 0)

    @pl.when(step == steps - 1)
    def _():
        out = out_sum[...].astype(BF).astype(F32)
        gates = jnp.sum(out * us[...].astype(F32), axis=1, keepdims=True)
        sums[...] = jnp.broadcast_to(gates, sums.shape)
        for k in range(chunks):
            here = pl.ds(offsets[k], rows)
            out_refs[k][...] = out_sum[here, :].astype(BF)
            back_refs[k][:rows, :] = back_sum[here, :].astype(BF)
            gate = jnp.transpose(sums[here, :])[:1]
            high = gate.astype(BF).astype(F32)
            mid = (gate - high).astype(BF).astype(F32)
            place = lax.broadcasted_iota(jnp.int32, (TAIL, rows), 0)
            tail = jnp.where(place == 0, high, jnp.where(place == 1, mid, jnp.where(place == 2, gate - high - mid, 0.0)))
            tail = jnp.concatenate([tail, jnp.zeros((TAIL, out.shape[1] - rows), F32)], axis=1)
            back_refs[k][rows:, :] = tail.astype(BF)


def expert_call(counts, place, ids, xs, us, wide, narrow, deps, block=384, parts=4):
    chunks, (tailed, width), hidden = len(xs), xs[0].shape, wide.shape[1]
    rows = tailed - TAIL
    cut, most = hidden // parts, chunks * rows
    sd = jax.ShapeDtypeStruct
    smem = pl.BlockSpec(memory_space=pltpu.SMEM)
    chunk, plain = whole((tailed, width)), whole((rows, width))
    inner = pl.BlockSpec((most, cut), lambda f: (0, f))
    outs, done = kernel_call(
        partial(expert_kernel, ids, block),
        10,
        deps,
        vmem=EXPERT_VMEM[len(ids) - 1],
        grid=(parts,),
        in_specs=[smem] * 2 + [whole(us.shape)] + [chunk] * chunks
        + [pl.BlockSpec((width, cut), lambda f: (0, f)), pl.BlockSpec((cut, width), lambda f: (f, 0))],
        out_specs=[plain] * chunks + [chunk] * chunks + [inner, inner],
        out_shape=[pltpu.HBM((rows, width), BF)] * chunks + [sd((tailed, width), BF)] * chunks
        + [pltpu.HBM((most, hidden), BF)] * 2,
        scratch_shapes=[pltpu.VMEM((most, width), BF)] * 2
        + [pltpu.VMEM((most, width), F32)] * 2 + [pltpu.VMEM((most, 128), F32)],
    )(counts, place, us, *xs, hbm(wide), hbm(narrow))
    return outs[:chunks], outs[chunks : 2 * chunks], outs[-2], outs[-1], done


def pack_weighed(ids, counts_ref, x_refs, rows_of, depth, packed_ref, turned_ref):
    rows = x_refs[0].shape[0] - TAIL
    offsets, _ = pack_offsets(counts_ref, ids)
    packed_ref[...] = jnp.zeros_like(packed_ref)
    lanes = lax.broadcasted_iota(jnp.int32, (128, rows), 1)
    for k in range(len(ids)):
        gates = jnp.sum(x_refs[k][rows:, :rows].astype(F32), axis=0, keepdims=True)
        gates = jnp.where(lanes < counts_ref[ids[k]], gates, 0.0)
        gates = jnp.transpose(gates)[:, :1]
        packed_ref[pl.ds(offsets[k], rows), :] = (rows_of(k).astype(F32) * gates).astype(BF)
    turned_ref[...] = jnp.transpose(packed_ref[:depth])


def pack_units(sets, counts_ref, part_refs, packed_ref):
    offsets, _ = pack_offsets(counts_ref, sum(sets, ()))
    first = 0
    for part, part_ref in zip(sets, part_refs):
        packed_ref[pl.ds(offsets[first], part_ref.shape[0]), :] = part_ref[...]
        first += len(part)


def wide_kernel(sets, depth, counts_ref, spot_ref, *refs):
    ids = sum(sets, ())
    x_refs, pre_refs = refs[: len(ids)], refs[len(ids) : len(ids) + len(sets)]
    keep_ref, send_ref, packed, turned, pres = refs[len(ids) + len(sets) :]
    rows = x_refs[0].shape[0] - TAIL

    @pl.when(pl.program_id(0) == 0)
    def _():
        pres[...] = jnp.zeros_like(pres)
        pack_weighed(ids, counts_ref, x_refs, lambda k: x_refs[k][:rows, :], depth, packed, turned)

    pack_units(sets, counts_ref, pre_refs, pres)
    put_halves(spot_ref[0], keep_ref, [send_ref], slice(None), mxu(turned[...], pres[:depth]).astype(BF))


def narrow_kernel(sets, depth, counts_ref, spot_ref, place_ref, u_ref, *refs):
    ids = sum(sets, ())
    x_refs, act_refs = refs[: len(ids)], refs[len(ids) : len(ids) + len(sets)]
    keep_ref, send_ref, packed, turned, acts = refs[len(ids) + len(sets) :]
    rows = x_refs[0].shape[0] - TAIL
    step = pl.program_id(0)

    @pl.when(step == 0)
    def _():
        acts[...] = jnp.zeros_like(acts)
        rows_of = lambda k: u_ref[source_of(place_ref, ids[k], u_ref.shape[0]), :rows, :]
        pack_weighed(ids, counts_ref, x_refs, rows_of, depth, packed, turned)

    pack_units(sets, counts_ref, act_refs, acts)
    narrow = mxu(turned[...], acts[:depth]).astype(BF)
    spot = spot_ref[0]
    cut = keep_ref.shape[2]
    count = narrow.shape[1] // cut
    for k in range(count):
        part = narrow[:, k * cut : (k + 1) * cut]
        at = (step * count + k) // 2 ^ (spot // 2)

        @pl.when(spot % 2 == k % 2)
        def _():
            keep_ref[at] = part

        @pl.when(spot % 2 != k % 2)
        def _():
            send_ref[at] = part


def weight_calls(counts, spot, place, sets, xs, us, acts, pres, blocks, depth, deps, parts=4):
    chunks, (tailed, width), hidden = len(xs), xs[0].shape, acts[0].shape[1]
    half = blocks // 2
    cut, most = hidden // parts, chunks * (tailed - TAIL)
    smem = pl.BlockSpec(memory_space=pltpu.SMEM)
    inner = [pl.BlockSpec((act.shape[0], cut), lambda f: (0, f)) for act in acts]
    common = dict(
        grid=(parts,),
        scratch_shapes=[pltpu.VMEM((most, width), BF), pltpu.VMEM((width, depth), BF), pltpu.VMEM((most, cut), BF)],
    )
    chunk_specs = [whole((tailed, width))] * chunks
    wide, wide_done = kernel_call(
        partial(wide_kernel, sets, depth),
        5,
        vmem=WIDE_VMEM,
        in_specs=[smem] * 2 + chunk_specs + inner,
        out_specs=[pl.BlockSpec((half, width // blocks, cut), lambda f: (0, 0, f))] * 2,
        out_shape=[jax.ShapeDtypeStruct((half, width // blocks, hidden), BF)] * 2,
        **common,
    )(counts, spot, *xs, *map(hbm, pres))
    narrow, _ = kernel_call(
        partial(narrow_kernel, sets, depth),
        1,
        [deps, wide_done],
        vmem=NARROW_VMEM,
        in_specs=[smem] * 3 + [whole(us.shape)] + chunk_specs + inner,
        out_specs=[whole((half, width, hidden // blocks))] * 2,
        out_shape=[jax.ShapeDtypeStruct((half, width, hidden // blocks), BF)] * 2,
        **common,
    )(counts, spot, place, us, *xs, *map(hbm, acts))
    return *wide, *narrow


def weight_first_kernel(keep_wide, came_wide, keep_narrow, came_narrow, own_ref, x_keep, x_send, y_keep, y_send):
    rows, hidden = keep_wide.shape[1:]
    cut = keep_narrow.shape[2]
    for k in range(4):
        wide = (keep_wide[k].astype(F32) + came_wide[k].astype(F32)).astype(BF)
        if k == 0:
            own_ref[:, :hidden] = wide
        elif k == 2:
            x_keep[...] = wide
        else:
            x_send[k // 2] = wide
        for slab in range(keep_narrow.shape[1] // rows):
            here = slice(slab * rows, (slab + 1) * rows)
            columns = slice(slab * cut, (slab + 1) * cut)
            total = (keep_narrow[k, here, :].astype(F32) + came_narrow[k, here, :].astype(F32)).astype(BF)
            if k == 0:
                own_ref[:, hidden + slab * cut : hidden + (slab + 1) * cut] = total
            elif k == 1:
                y_keep[:, columns] = total
            else:
                y_send[k - 2, :, columns] = total


def weight_second_kernel(own_ref, x_keep, x_came, y_keep, y_came, sum_ref, x_send, y_send):
    hidden = x_keep.shape[1]
    sum_ref[:, :hidden] = own_ref[:, :hidden].astype(F32) + x_came[0].astype(F32)
    sum_ref[:, hidden:] = own_ref[:, hidden:].astype(F32) + y_came[0].astype(F32)
    x_send[...] = (x_keep[...].astype(F32) + x_came[1].astype(F32)).astype(BF)
    y_send[...] = (y_keep[...].astype(F32) + y_came[1].astype(F32)).astype(BF)


def weight_last_kernel(sum_ref, x_came, y_came, wide_ref, narrow_ref):
    rows, hidden = wide_ref.shape
    cut = narrow_ref.shape[0]
    wide_ref[...] = sum_ref[:, :hidden] + x_came[...].astype(F32)
    for slab in range(narrow_ref.shape[1] // rows):
        columns = slice(slab * cut, (slab + 1) * cut)
        piece = sum_ref[:, hidden + slab * cut : hidden + (slab + 1) * cut] + y_came[:, columns].astype(F32)
        narrow_ref[:, slab * rows : (slab + 1) * rows] = jnp.transpose(piece)


def as_column(row):
    return jnp.transpose(jnp.broadcast_to(row, (128, row.shape[1])))[:, :1]


def put_halves(spot, keep_ref, send_refs, columns, values):
    half, rows = keep_ref.shape[:2]
    held = half // len(send_refs)
    for block in range(2 * half):
        part = values[block * rows : (block + 1) * rows]
        at = (block // 2) ^ (spot // 2)

        @pl.when(spot % 2 == block % 2)
        def _():
            keep_ref[at, :, columns] = part

        for k, send_ref in enumerate(send_refs):

            @pl.when((spot % 2 != block % 2) & (at // held == k))
            def _():
                send_ref[at % held, :, columns] = part


EXACT = 32


def split_exact(values):
    lane = lax.broadcasted_iota(jnp.int32, values.shape, 1)
    high = values.astype(BF).astype(F32)
    mid = (values - high).astype(BF).astype(F32)
    low = values - high - mid
    band = (lane - EXACT) // 16
    mid, low = pltpu.roll(mid, 16, 1), pltpu.roll(low, 32, 1)
    return jnp.where(band == 0, high, jnp.where(band == 1, mid, jnp.where(band == 2, low, values)))


def join_exact(values):
    lane = lax.broadcasted_iota(jnp.int32, values.shape, 1)
    total = values + pltpu.roll(values, 128 - 16, 1) + pltpu.roll(values, 128 - 32, 1)
    return jnp.where((lane >= EXACT) & (lane < EXACT + 16), total, values)


def home_kernel(experts, slots, capacity, chunks, extra_rows, temper_ref, prior_ref, chosen_ref, rank_ref, pos_ref,
                residual_ref, upstream_ref, att_ref, projected_ref, table_ref, router_ref, gain_ref, shift_ref,
                wo_ref, *refs):
    back_refs = refs[:chunks]
    (weight_ref, grad_ref, att_grad_ref, delta_ref, outer_ref, extra_ref, tiny_ref, spots_ref, extra_sum) = refs[
        chunks:
    ]
    rows, width = residual_ref.shape
    route = projected_ref.shape[0]
    for k in range(chunks):
        spots_ref[k * slots : (k + 1) * slots, :] = back_refs[k][:slots, :]
    temper = temper_ref[0]
    table = table_ref[...]
    projected = projected_ref[...]
    scale, unit, table_scale, unit_table, logits = router_of(projected, table, temper)
    routed = softmax_rows(logits, experts)
    chosen = chosen_ref[...]
    selected = chosen == lax.broadcasted_iota(jnp.int32, logits.shape, 0)
    before = sum(jnp.where(chosen == expert, prior_ref[expert], 0) for expert in range(experts))
    kept = (before + rank_ref[...] < capacity).astype(F32)
    gate = jnp.sum(jnp.where(selected, routed, 0.0), axis=0, keepdims=True)
    weight = gate * kept
    weight_ref[...] = weight
    pos = pos_ref[...]
    gate_grad = jnp.zeros((1, rows), F32)
    for k in range(chunks):
        here = (lax.broadcasted_iota(jnp.int32, (slots, rows), 0) + k * slots == pos).astype(F32).astype(BF)
        gate_grad += jnp.sum(mxu(back_refs[k][slots:, :slots], here), axis=0, keepdims=True)
    gate_grad = gate_grad * kept
    logit_grad = gate_grad * routed * (selected.astype(F32) - gate)
    highest = dict(precision=lax.Precision.HIGHEST, preferred_element_type=F32)
    unit_grad = lax.dot_general(unit_table, logit_grad, TN, **highest) / temper
    table_grad = lax.dot_general(logit_grad, unit, NT, **highest) / temper
    sharp = -jnp.sum(logit_grad * logits, keepdims=True) / temper
    projected_grad = scale * unit_grad - scale * scale * scale * projected * jnp.sum(
        projected * unit_grad, axis=0, keepdims=True
    )
    padded = jnp.concatenate([projected_grad, jnp.zeros((128 - route, rows), F32)], axis=0)
    router = jnp.concatenate([router_ref[...], jnp.zeros((128 - route, width), F32)], axis=0)
    column = pos.astype(F32)
    both = jnp.transpose(jnp.concatenate([column, weight, jnp.zeros((126, rows), F32)], axis=0))
    routed_grad = jnp.transpose(padded)
    head_lane = lax.broadcasted_iota(jnp.int32, (width, 128), 1)
    heads = (lax.broadcasted_iota(jnp.int32, (width, 128), 0) // HEAD_DIM == head_lane).astype(F32).astype(BF)
    gain, shift = gain_ref[...], shift_ref[...]
    pos_column, weight_column = both[:, :1].astype(jnp.int32), both[:, 1:2]
    lanes = lax.broadcasted_iota(jnp.int32, (rows, spots_ref.shape[0]), 1)
    home = mxu((lanes == pos_column).astype(F32).astype(BF), spots_ref[...])
    y_grad = home * weight_column + mxu_wide(routed_grad, router)
    unit_two, norm_scale, normed_two = norm_of(residual_ref[...], gain, shift)
    inner = y_grad * gain
    two_part = norm_scale * (
        inner
        - jnp.mean(inner, axis=-1, keepdims=True)
        - unit_two * jnp.mean(inner * unit_two, axis=-1, keepdims=True)
    )
    residual_grad = upstream_ref[...].astype(F32) + two_part
    grad_ref[...] = residual_grad
    branch = residual_grad.astype(BF)
    att_grad = mxu(branch, wo_ref[...], NT).astype(BF)
    att_grad_ref[...] = att_grad
    product_high, product_low = split_high(att_grad.astype(F32) * att_ref[...].astype(F32))
    delta = mxu(product_high, heads) + mxu(product_low, heads)
    delta_ref[...] = jnp.transpose(delta)[: delta_ref.shape[0]]
    outer_ref[...] = mxu(jnp.transpose(att_ref[...]), branch).astype(BF)
    extra_sum[...] = jnp.zeros_like(extra_sum)
    extra_sum[:route, :] = mxu_wide(projected_grad, normed_two)
    extra_sum[route : route + 1, :] = jnp.sum(y_grad * unit_two, axis=0, keepdims=True)
    extra_sum[route + 1 : route + 2, :] = jnp.sum(y_grad, axis=0, keepdims=True)
    wide_table = jnp.concatenate([table, jnp.zeros((table.shape[0], 128 - route), F32)], axis=1)
    table_grad = jnp.concatenate([table_grad, jnp.zeros((table.shape[0], 128 - route), F32)], axis=1)
    summed = jnp.sum(wide_table * table_grad, axis=1, keepdims=True)
    table_grad = table_scale * table_grad - table_scale * table_scale * table_scale * wide_table * summed
    tiny = jnp.concatenate([table_grad, jnp.broadcast_to(sharp, (8, 128))], axis=0)
    tiny_ref[...] = tiny
    extra = jnp.transpose(extra_sum[...])
    if chunks <= 8:
        tiny = jnp.concatenate([tiny, jnp.zeros((128 - tiny.shape[0], 128), F32)], axis=0)
        tiny = pltpu.roll(jnp.transpose(tiny)[: extra_rows], EXACT, 1)
        lane = lax.broadcasted_iota(jnp.int32, tiny.shape, 1)
        tiny = split_exact(jnp.where((lane >= EXACT) & (lane < EXACT + 16), tiny, 0.0))
        tiny = jnp.concatenate([tiny] * (extra.shape[0] // extra_rows), axis=0)
        lane = lax.broadcasted_iota(jnp.int32, tiny.shape, 1)
        extra = jnp.where(lane < EXACT, extra, tiny)
    extra_ref[...] = extra.astype(BF)


def score_back_kernel(first, pairs, weights, spot_ref, label_ref, q_ref, k_ref, v_ref, att_grad_ref, lse_ref, delta_ref,
                      turned_ref, *refs):
    count = 3 + (1 + SENDS) * weights
    more_refs, out_refs, bias_ref = refs[: -1 - count], refs[-1 - count : -1], refs[-1]
    dq_ref, dk_ref, dv_ref = out_refs[:3]
    rows = label_ref.shape[2]
    low_lanes = lax.broadcasted_iota(jnp.int32, (rows, 128), 1) < HEAD_DIM
    for seq in range(label_ref.shape[0]):
        here = slice(seq * rows, (seq + 1) * rows)
        bias_ref[...] = same_label(label_ref[seq])
        for pair in range(pairs):
            there = slice(pair * 128, pair * 128 + 128)
            columns = slice((first + pair) * 128, (first + pair) * 128 + 128)
            q_pair, k_pair, v_pair = q_ref[here, columns], k_ref[here, columns], v_ref[here, columns]
            g_pair = att_grad_ref[here, columns]
            k_turned = jnp.transpose(k_pair)
            dk = jnp.zeros((rows, 128), F32)
            dv = jnp.zeros((rows, 128), F32)
            dq_turned = []
            for half in range(2):
                own = low_lanes if half == 0 else jnp.logical_not(low_lanes)
                q_own = jnp.where(own, q_pair.astype(F32), 0.0).astype(BF)
                g_own = jnp.where(own, g_pair.astype(F32), 0.0).astype(BF)
                head = (first + pair) * 2 + half
                head = slice(head, head + 1)
                probs = jnp.exp(mxu(k_pair, q_own, NT) + bias_ref[...] - lse_ref[head, here])
                prob_grad = mxu(v_pair, g_own, NT)
                score_grad = (probs * (prob_grad - delta_ref[head, here])).astype(BF)
                dv += mxu(probs.astype(BF), g_own)
                dk += mxu(score_grad, q_own)
                dq_turned.append(mxu(k_turned[half * HEAD_DIM : (half + 1) * HEAD_DIM], score_grad))
            dq = jnp.transpose(jnp.concatenate(dq_turned, axis=0)) * HEAD_DIM ** (-0.5)
            dq_ref[here, there] = dq.astype(BF)
            dk_ref[here, there] = dk.astype(BF)
            dv_ref[here, there] = dv.astype(BF)
    if weights:
        weight_grads(spot_ref[0], turned_ref, (dq_ref, dk_ref, dv_ref), more_refs, out_refs[3], out_refs[4:])


def weight_grads(spot, turned_ref, grad_refs, more_refs, keep_ref, send_refs):
    start = 0
    for ref in grad_refs:
        columns = slice(start, start + ref.shape[1])
        put_halves(spot, keep_ref, send_refs, columns, mxu(turned_ref[...], ref[...]).astype(BF))
        start += ref.shape[1]
    for more_ref in more_refs:
        columns = slice(start, start + more_ref.shape[1])
        put_halves(spot, keep_ref, send_refs, columns, more_ref[...])
        start += more_ref.shape[1]


def tokens_kernel(groups, spot_ref, turned_ref, x_ref, grad_ref, wq_ref, wk_ref, wv_ref, gain_ref, shift_ref, *refs):
    tokens_ref, keep_ref, send_ref, joined_ref, sums_ref, turned_sums_ref = refs[3 * groups :]
    one_grad = 0.0
    for part, w_ref in enumerate((wq_ref, wk_ref, wv_ref)):
        start = 0
        for group in range(groups):
            piece = refs[3 * group + part]
            joined_ref[part, :, start : start + piece.shape[1]] = piece[...]
            start += piece.shape[1]
        one_grad += mxu(joined_ref[part], w_ref[...], NT)
    unit, scale, _ = norm_of(x_ref[...].astype(F32), gain_ref[...], shift_ref[...])
    inner = one_grad * gain_ref[...]
    one_part = scale * (
        inner
        - jnp.mean(inner, axis=-1, keepdims=True)
        - unit * jnp.mean(inner * unit, axis=-1, keepdims=True)
    )
    tokens_ref[...] = (grad_ref[...] + one_part).astype(BF)
    sums_ref[...] = jnp.zeros_like(sums_ref)
    sums_ref[0:1, :] = jnp.sum(one_grad * unit, axis=0, keepdims=True)
    sums_ref[1:2, :] = jnp.sum(one_grad, axis=0, keepdims=True)
    turned_sums_ref[...] = jnp.transpose(sums_ref[...]).astype(BF)
    weight_grads(spot_ref[0], turned_ref, refs[3 * groups - 3 : 3 * groups], [turned_sums_ref], keep_ref, [send_ref])


def first_sum_kernel(exact, count, keep_ref, *refs):
    came_refs, out_refs = refs[:count], refs[count:]
    held = len(out_refs) // count
    for k, out_ref in enumerate(out_refs):
        came = came_refs[k // held][k % held].astype(F32)
        out_ref[...] = (keep_ref[k].astype(F32) + came).astype(BF)
        if exact is not None:
            here = slice(exact, exact + 128)
            out_ref[:, here] = split_exact(join_exact(keep_ref[k, :, here].astype(F32) + came[:, here])).astype(BF)


def second_sum_kernel(exact, place_ref, *refs):
    own_ref, send_refs, sum_ref = refs[4], refs[5:-1], refs[-1]
    sum_ref[...] = sum(ref[...].astype(F32) for ref in refs[:4])
    if exact is not None:
        sum_ref[:, exact : exact + 128] = split_exact(join_exact(sum_ref[:, exact : exact + 128]))
    size = own_ref.shape[0]
    group = len(send_refs) + 1
    own_ref[...] = sum_ref[pl.ds(pl.multiple_of(place_ref[0] * size, 8), size), :]
    if len(send_refs) == 1:
        (send_ref,) = send_refs
        filler = jnp.zeros((send_ref.shape[1] - size, send_ref.shape[2]), F32)
        for k in range(send_ref.shape[0]):
            block = jnp.where(place_ref[0] == k, 0.0, sum_ref[k * size : (k + 1) * size, :])
            send_ref[k] = jnp.concatenate([block, filler], axis=0).astype(BF)
        return
    for k, send_ref in enumerate(send_refs):
        there = lax.rem(place_ref[0] + k + 1, group)
        block = sum_ref[pl.ds(pl.multiple_of(there * size, 8), size), :]
        filler = jnp.zeros((send_ref.shape[0] - size, block.shape[1]), F32)
        send_ref[...] = jnp.concatenate([block, filler], axis=0).astype(BF)


def last_sum_kernel(first, last, route, group, experts_padded, counts, *refs):
    query_ref, key_ref, value_ref, outer_ref, router_ref, norms_ref, table_ref, sharp_ref = refs[sum(counts) :]
    rows, width = outer_ref.shape

    def total(parts, columns):
        value = parts[0][:, columns]
        for ref in parts[1:]:
            for sent in [ref] if len(ref.shape) == 2 else [ref.at[k] for k in range(ref.shape[0])]:
                value = value + sent[:, columns].astype(F32)[:rows]
        return value

    def turned(extra):
        return jnp.transpose(jnp.concatenate([extra, jnp.zeros((128 - rows, 128), F32)], axis=0))

    early, late = refs[: counts[0]], refs[counts[0] : sum(counts)]
    for part, ref in enumerate((query_ref, key_ref, value_ref)):
        ref[:, :first] = total(early, slice(part * first, (part + 1) * first))
        ref[:, first:] = total(late, slice(part * last, (part + 1) * last))
    outer_ref[...] = total(early, slice(3 * first, 3 * first + width))
    extra = join_exact(total(early, slice(3 * first + width, 3 * first + width + 128)))
    router_ref[...] = extra[:, :route]
    extra = turned(extra)
    norms = turned(total(late, slice(3 * last, 3 * last + 128)))
    norms_ref[...] = jnp.concatenate([norms[:2, :rows], extra[route : route + 2, :rows]], axis=0)
    table_ref[...] = extra[EXACT : EXACT + group, :route]
    sharp_ref[...] = extra[EXACT + experts_padded : EXACT + experts_padded + 1, :1]


def output_kernel(residual_ref, weight_ref, pos_ref, *refs):
    out_refs, layer_ref, spots_ref = refs[:-2], refs[-2], refs[-1]
    slots = out_refs[0].shape[0]
    for k, out_ref in enumerate(out_refs):
        spots_ref[k * slots : (k + 1) * slots, :] = out_ref[...]
    rows = residual_ref.shape[0]
    both = jnp.concatenate([pos_ref[...].astype(F32), weight_ref[...], jnp.zeros((126, rows), F32)], axis=0)
    both = jnp.transpose(both)
    pos_column, weight_column = both[:, :1].astype(jnp.int32), both[:, 1:2]
    lanes = lax.broadcasted_iota(jnp.int32, (rows, spots_ref.shape[0]), 1)
    home = mxu((lanes == pos_column).astype(F32).astype(BF), spots_ref[...])
    layer_ref[...] = (residual_ref[...] + home * weight_column).astype(BF)


def swap(values, axis, mask):
    size = lax.axis_size(axis)
    return lax.ppermute(values, axis, [(i, i ^ mask) for i in range(size)])


def shift(values, axis, step):
    size = lax.axis_size(axis)
    return lax.ppermute(values, axis, [(i, (i + step) % size) for i in range(size)])


def pick(values, index, axis):
    return lax.dynamic_index_in_dim(values, index, axis, keepdims=False)


def held(arrays, deps):
    anywhere = pl.BlockSpec(memory_space=pl.ANY)
    return kernel_call(
        lambda *refs: None,
        0,
        deps,
        grid=(1,),
        in_specs=[anywhere] * len(arrays),
        out_specs=[anywhere] * len(arrays),
        out_shape=[jax.ShapeDtypeStruct(array.shape, array.dtype) for array in arrays],
        input_output_aliases={k: k for k in range(len(arrays))},
    )(*arrays)


def seen(arrays):
    return kernel_call(lambda *refs: None, 0, jax.tree.leaves(arrays), grid=(1,), in_specs=[], out_specs=[], out_shape=[])()[1]


def first_sum(keep, sends, exact, deps, weight):
    half, rows, width = keep.shape
    return kernel_call(
        partial(first_sum_kernel, exact, len(sends)),
        weight,
        deps,
        vmem=SUM1_VMEM,
        in_specs=[pl.BlockSpec()] * (1 + len(sends)),
        out_shape=[jax.ShapeDtypeStruct((rows, width), BF)] * half,
    )(keep, *[swap(send, "dp", 1) for send in sends])


def second_sum(parts, place_vec, exact, deps, weight, together=False):
    group = lax.axis_size("expert")
    came = [parts[0]] + [swap(parts[k], "dp", 2 * k) for k in range(1, len(parts))]
    rows, width = parts[0].shape
    if group > 8:
        return [sum(part.astype(F32) for part in came)], ()
    size = rows // group
    padded = (size + 15) // 16 * 16
    sd = jax.ShapeDtypeStruct
    return kernel_call(
        partial(second_sum_kernel, exact),
        weight,
        deps,
        vmem=SUM2_VMEM,
        in_specs=[pl.BlockSpec(memory_space=pltpu.SMEM)] + [pl.BlockSpec()] * len(came),
        out_shape=[sd((size, width), F32)]
        + ([sd((group, padded, width), BF)] if together else [sd((padded, width), BF)] * (group - 1)),
        scratch_shapes=[pltpu.VMEM((rows, width), F32)],
    )(place_vec, *came)


def sent_on(parts):
    if lax.axis_size("expert") > 8:
        return [lax.psum_scatter(parts[0], "expert", scatter_dimension=0, tiled=True)]
    if len(parts) == 2:
        return [parts[0], lax.all_to_all(parts[1], "expert", 0, 0, tiled=True)]
    return [parts[0]] + [shift(parts[k], "expert", k) for k in range(1, len(parts))]


def small_sum(values):
    group = lax.axis_size("expert")
    if group > 8:
        return lax.psum(values, ("dp", "expert"))
    values = values + swap(values, "dp", 1)
    values = values + sum(swap(values, "dp", mask) for mask in range(2, lax.axis_size("dp"), 2))
    return values + sum(shift(values, "expert", k) for k in range(1, group))


def exchange(blocks, sign):
    size = lax.axis_size("expert")
    if size <= 8:
        return [blocks[0]] + [shift(blocks[k], "expert", sign * k) for k in range(1, size)]
    stacked = jnp.stack(blocks)
    place = lax.axis_index("expert")
    across = (jnp.arange(size) - place) * sign % size
    there = lax.all_to_all(stacked[across], "expert", 0, 0, tiled=True)
    source = (place - sign * jnp.arange(size)) % size
    home = there[source]
    return [home[k] for k in range(size)]


WAYS = 4
SETS = ((0,), (1, 3), (2,))
CUTS = (512, 256)
SENDS = 2
D0_WEIGHT, D1_WEIGHT, FIRST_WEIGHT, TOKENS_WEIGHT = 0.1, 0.1, 0.05, 0.1
MID_WEIGHT, LATE_FIRST_WEIGHT, SECOND_WEIGHT, LATE_SECOND_WEIGHT, LAST_WEIGHT, OUTPUT_WEIGHT = 18, 1, 1, 7, 0.1, 0.1


def body(
    layer_inputs_matrix,
    upstream_output_sensitivity,
    mixer_layernorm_scale,
    mixer_layernorm_offset,
    asker_matrix,
    lookup_label_matrix,
    content_matrix,
    mixer_result_matrix,
    specialist_layernorm_scale,
    specialist_layernorm_offset,
    dispatch_projection_matrix,
    specialist_centroids,
    learned_sharpness,
    specialist_widening_matrix,
    specialist_narrowing_matrix,
    document_labels,
    chosen_specialist,
    placement_ranks,
):
    rows, width = layer_inputs_matrix.shape
    seqs, length = document_labels.shape
    head_count = width // HEAD_DIM
    group = lax.axis_size("expert")
    place = lax.axis_index("expert")
    dp_size = lax.axis_size("dp")
    wide, narrow = specialist_widening_matrix[0], specialist_narrowing_matrix[0]
    hidden = wide.shape[1]
    route = dispatch_projection_matrix.shape[1]
    slots = 3 * rows // (2 * group)
    spots = group * slots
    experts_padded = (group + 7) // 8 * 8
    sd = jax.ShapeDtypeStruct
    smem, vmem = (pl.BlockSpec(memory_space=space) for space in (pltpu.SMEM, pltpu.VMEM))
    int32 = jnp.int32
    place_vec = place.astype(int32).reshape(1)
    spot_vec = lax.axis_index("dp").astype(int32).reshape(1)
    vec = lambda v: v.reshape(1, -1)
    gain_one, shift_one = vec(mixer_layernorm_scale), vec(mixer_layernorm_offset)
    gain_two, shift_two = vec(specialist_layernorm_scale), vec(specialist_layernorm_offset)
    router = dispatch_projection_matrix.T
    table = jnp.zeros((experts_padded, route), F32).at[:group].set(specialist_centroids)
    labels = document_labels.reshape(seqs, 1, length)
    chosen = chosen_specialist.reshape(1, rows)

    row_block = pl.BlockSpec((length, width), lambda s: (s, 0))
    line = pl.BlockSpec((1, length), lambda s: (0, s))
    label_spec = pl.BlockSpec((1, 1, length), lambda s: (s, 0, 0))
    turned_block = pl.BlockSpec((width, length), lambda s: (0, s))
    heads_block = pl.BlockSpec((16, length), lambda s: (0, s))
    weight_spec = whole((width, width))
    vec_spec = whole((1, width))
    chunk_spec, tailed_spec = whole((slots, width)), whole((slots + TAIL, width))
    table_spec = whole((experts_padded, route))

    tailed = slots + TAIL
    (pos, rank, upstream_sent), _ = kernel_call(
        partial(route_kernel, slots),
        5,
        vmem=ROUTE_VMEM,
        in_specs=[smem] + [pl.BlockSpec()] * 3,
        out_shape=[sd((1, rows), int32)] * 2 + [pltpu.HBM((group, tailed, width), BF)],
    )(place_vec, placement_ranks, chosen, upstream_output_sensitivity)
    upstream_there = lax.all_to_all(upstream_sent, "expert", 0, 0, tiled=True)

    (turned, queries, keys, values, attended, lse, residual, projected, *entering_sent), _ = kernel_call(
        partial(attend_kernel, group, slots),
        20,
        vmem=ATTEND_VMEM,
        grid=(seqs,),
        in_specs=[row_block, label_spec] + [vec_spec] * 2 + [weight_spec] * 4 + [vec_spec] * 2
        + [whole((route, width)), table_spec, smem, line, line],
        out_specs=[turned_block] + [row_block] * 4
        + [heads_block, row_block, pl.BlockSpec((route, length), lambda s: (0, s))] + [tailed_spec] * group,
        out_shape=[pltpu.HBM((width, rows), BF)] + [pltpu.HBM((rows, width), BF)] * 4
        + [sd((16, rows), F32), pltpu.HBM((rows, width), F32), sd((route, rows), F32)]
        + [pltpu.HBM((tailed, width), BF)] * group,
        scratch_shapes=[pltpu.VMEM((length, length), F32), pltpu.VMEM((length, 128), F32)],
    )(
        layer_inputs_matrix, labels, gain_one, shift_one, asker_matrix, lookup_label_matrix,
        content_matrix, mixer_result_matrix, gain_two, shift_two, router, table, learned_sharpness, chosen, pos,
    )
    tails = upstream_there[:, slots : slots + 2, :experts_padded].astype(F32)
    tallies = (tails[:, 0] * 256.0 + tails[:, 1]).astype(int32)
    sources = jnp.arange(group)
    prior = jnp.sum(jnp.where(sources[:, None] < place, tallies, 0), axis=0)
    named = jnp.sum(jnp.where(jnp.arange(experts_padded) == place, tallies, 0), axis=1)
    earlier = jnp.sum(jnp.where(sources[:, None] < sources[None, :], named[:, None], 0), axis=0)
    counts = jnp.clip(rows - earlier, 0, named)
    relative = (place - sources) % group
    counts = jnp.sum(jnp.where(relative[:, None] == sources[None, :], counts[None, :], 0), axis=1)

    each = group // WAYS
    backs, produced, acts, pres, order = [None] * WAYS, [None] * WAYS, [], [], []

    def experts(ids, counts, entered, graded, turn, deps):
        outs, some, act, pre, done = expert_call(counts, turn, ids, entered, graded, wide, narrow, [deps, order])
        for k, out, back in zip(ids, outs, some):
            produced[k], backs[k] = out, back
        acts.append(act)
        pres.append(pre)
        order.append(done)

    if each == 1:
        split = lambda chunks, _: list(chunks)
        turn_vec, graded, entered = place_vec, upstream_there, list(entering_sent)
        alone = jnp.sum((chosen == place).astype(int32)).reshape(1)
        experts(SETS[0], alone, entered[:1], upstream_sent, turn_vec, ())
        ready = []
        for ids in SETS[1:]:
            for k, sent in zip(ids, held([entered[k] for k in ids], ready)[0] if ready else [entered[k] for k in ids]):
                entered[k] = shift(sent, "expert", k)
            ready = [entered[k] for k in ids]
        for ids in SETS[1:]:
            experts(ids, counts, [entered[k] for k in ids], graded, turn_vec, prior)
    else:
        entering_there = exchange(entering_sent, 1)
        valid = jnp.arange(slots)[None, :] < counts[:, None]
        counts = jnp.full((WAYS,), each * slots, int32)
        turn_vec = jnp.zeros((1,), int32)

        def join(blocks, masks):
            chunks = []
            for k in range(0, group, each):
                tail = [jnp.where(masks[j], blocks[j][slots:, :slots], 0) for j in range(k, k + each)]
                tail = jnp.concatenate(tail, axis=1)
                tail = jnp.pad(tail, ((0, 0), (0, width - tail.shape[1])))
                chunks.append(jnp.concatenate([blocks[j][:slots] for j in range(k, k + each)] + [tail]))
            return chunks

        def split(chunks, with_tail):
            pieces = []
            for chunk in chunks:
                for j in range(each):
                    piece = chunk[j * slots : (j + 1) * slots]
                    if with_tail:
                        tail = chunk[each * slots :, j * slots : (j + 1) * slots]
                        piece = jnp.concatenate([piece, jnp.pad(tail, ((0, 0), (0, width - slots)))])
                    pieces.append(piece)
            return pieces

        entered = join(entering_there, valid)
        graded = join([pick(upstream_there, relative[k], 0) for k in range(group)], valid)
        graded = jnp.stack([graded[-k % WAYS] for k in range(WAYS)])
        for ids in SETS:
            experts(ids, counts, [entered[k] for k in ids], graded, turn_vec, ())
    returned_home = exchange(split(backs, True), -1)
    ordered = [k for ids in SETS for k in ids]
    arrange = lambda chunks: [chunks[k] for k in ordered]
    depth = rows + 128 if each == 1 else spots
    keep_wide, send_wide, keep_narrow, send_narrow = weight_calls(
        counts, spot_vec, turn_vec, SETS, arrange(entered), graded, acts, pres, dp_size, depth,
        [returned_home[k] for k in SETS[1]],
    )
    half, block = dp_size // 2, width // dp_size
    (weight, residual_grad, attended_grad, delta, outer_part, extra_part, tiny), done = kernel_call(
        partial(home_kernel, group, slots, rows, group, width // (dp_size * group)),
        500,
        vmem=HOME_VMEM,
        in_specs=[smem, smem] + [vmem] * (12 + group),
        out_specs=[vmem] * 7,
        out_shape=[sd((1, rows), F32), sd((rows, width), F32), sd((rows, width), BF), sd((16, rows), F32),
                   sd((width, width), BF), sd((width, 128), BF), sd((experts_padded + 8, 128), F32)],
        scratch_shapes=[pltpu.VMEM((spots, width), BF), pltpu.VMEM((128, width), F32)],
    )(
        learned_sharpness, prior, chosen, rank, pos, residual, upstream_output_sensitivity, attended,
        projected, table, router, gain_two, shift_two, mixer_result_matrix, *returned_home,
    )
    half_rows = sd((block, hidden), BF)
    (weight_own, x_keep, x_send, y_keep, y_send), first_done = kernel_call(
        weight_first_kernel,
        1,
        done,
        vmem=SUM3_VMEM,
        in_specs=[pl.BlockSpec()] * 4,
        out_shape=[sd((block, 2 * hidden), BF)] + [half_rows, sd((2, block, hidden), BF)] * 2,
    )(keep_wide, swap(send_wide, "dp", 1), keep_narrow, swap(send_narrow, "dp", 1))
    if each == 1:
        ready, starts = [first_done], []
        for ids in SETS[1:]:
            sends, held_done = held([produced[k] for k in ids], ready)
            for k, sent in zip(ids, sends):
                produced[k] = shift(sent, "expert", -k)
            ready = [produced[k] for k in ids]
            starts.append(held_done)
        produced_home = produced
    else:
        produced_home, starts, ready = exchange(split(produced, False), -1), [(), ()], []

    x_came, y_came = swap(x_send, "dp", 2), swap(y_send, "dp", 4)
    pieces, start, done = [], 0, first_done
    for cut in CUTS:
        early = start == 0
        more = [outer_part, extra_part] if early else []
        columns = 3 * cut + width + 128
        pack = [sd((half, block, columns), BF)] + [sd((half // SENDS, block, columns), BF)] * SENDS if early else []
        grads, done = kernel_call(
            partial(score_back_kernel, start // 128, cut // 128, early),
            D0_WEIGHT if early else D1_WEIGHT,
            done if early else [done, starts[1]],
            vmem=SCORE_VMEM,
            in_specs=[smem] + [vmem] * (8 + len(more)),
            out_specs=[vmem] * (3 + len(pack)),
            out_shape=[sd((rows, cut), BF)] * 3 + pack,
            scratch_shapes=[pltpu.VMEM((length, length), F32)],
        )(spot_vec, labels, queries, keys, values, attended_grad, lse, delta, turned, *more)
        pieces.append(grads[:3])
        if early:
            keep, *sends = grads[3:]
        start += cut
    first, last = CUTS
    exact = 3 * first + width
    early, done = first_sum(keep, sends, exact, done, FIRST_WEIGHT)
    pack = sd((half, block, 3 * last + 128), BF)
    (tokens_grad, keep, send), done = kernel_call(
        partial(tokens_kernel, len(CUTS)),
        TOKENS_WEIGHT,
        [done, seen([x_came, y_came])],
        vmem=TOKENS_VMEM,
        in_specs=[smem] + [vmem] * (8 + 3 * len(CUTS)),
        out_specs=[vmem] * 3,
        out_shape=[sd((rows, width), BF)] + [pack] * 2,
        scratch_shapes=[pltpu.VMEM((3, rows, width), BF), pltpu.VMEM((128, width), F32), pltpu.VMEM((width, 128), BF)],
    )(spot_vec, turned, layer_inputs_matrix, residual_grad, asker_matrix, lookup_label_matrix, content_matrix,
      gain_one, shift_one, *[piece for group_pieces in pieces for piece in group_pieces])
    (weight_sum, x_more, y_more), done = kernel_call(
        weight_second_kernel,
        MID_WEIGHT,
        seen([done, ready]),
        vmem=SUM4_VMEM,
        in_specs=[pl.BlockSpec()] * 5,
        out_shape=[sd((block, 2 * hidden), F32)] + [half_rows] * 2,
    )(weight_own, x_keep, x_came, y_keep, y_came)
    late, done = first_sum(keep, [send], None, done, LATE_FIRST_WEIGHT)
    early, done = second_sum(early, place_vec, exact, done, SECOND_WEIGHT, True)
    (x_more, y_more), _ = held([x_more, y_more], done)
    late, done = second_sum(late, place_vec, None, done, LATE_SECOND_WEIGHT)
    (layer_output,), done = kernel_call(
        output_kernel,
        OUTPUT_WEIGHT,
        done,
        vmem=OUTPUT_VMEM,
        in_specs=[vmem] * (3 + group),
        out_specs=[vmem],
        out_shape=[sd((rows, width), BF)],
        scratch_shapes=[pltpu.VMEM((spots, width), BF)],
    )(residual, weight, pos, *produced_home)
    early, late = sent_on(early), sent_on(late)
    own = width // (dp_size * group)
    (query_grad, key_grad, value_grad, outer_grad, router_grad, norms, table_grad, sharp), done = kernel_call(
        partial(last_sum_kernel, first, last, route, group, experts_padded, (len(early), len(late))),
        1,
        done,
        vmem=SUM6_VMEM,
        in_specs=[pl.BlockSpec()] * (len(early) + len(late)),
        out_shape=[sd((own, width), F32)] * 4
        + [sd((own, route), F32), sd((4, own), F32), sd((group, route), F32), sd((1, 1), F32)],
    )(*early, *late)
    (hidden_grad, return_grad), done = kernel_call(
        weight_last_kernel,
        LAST_WEIGHT,
        done,
        vmem=SUM5_VMEM,
        in_specs=[pl.BlockSpec()] * 3,
        out_shape=[sd((block, hidden), F32), sd((hidden // dp_size, width), F32)],
    )(weight_sum, swap(x_more, "dp", 4), swap(y_more, "dp", 2))
    if group > 8:
        tiny = small_sum(tiny)
        table_grad, sharp = tiny[:group, :route], tiny[experts_padded, :1]
    return (
        layer_output,
        tokens_grad,
        norms[0],
        norms[1],
        query_grad,
        key_grad,
        value_grad,
        outer_grad,
        norms[2],
        norms[3],
        router_grad,
        table_grad,
        sharp.reshape(1),
        hidden_grad[None],
        return_grad[None],
    )


def solution(mesh):
    placed = (
        P(("dp", "expert"), None),
        P(("dp", "expert"), None),
        P(),
        P(),
        P(),
        P(),
        P(),
        P(),
        P(),
        P(),
        P(),
        P(),
        P(),
        P("expert", None, None),
        P("expert", None, None),
        P(("dp", "expert"), None),
        P(("dp", "expert"), None),
        P(("dp", "expert"), None),
    )
    return jax.shard_map(
        body,
        mesh=mesh,
        in_specs=placed,
        out_specs=(
            P(("dp", "expert"), None),
            P(("dp", "expert"), None),
            P(("dp", "expert")),
            P(("dp", "expert")),
            P(("dp", "expert"), None),
            P(("dp", "expert"), None),
            P(("dp", "expert"), None),
            P(("dp", "expert"), None),
            P(("dp", "expert")),
            P(("dp", "expert")),
            P(("dp", "expert"), None),
            P(),
            P(),
            P("expert", "dp", None),
            P("expert", "dp", None),
        ),
        check_vma=False,
    )
```

```python
from functools import partial

import jax
import jax.numpy as jnp
from jax import lax
from jax.experimental import pallas as pl
from jax.experimental.pallas import tpu as pltpu
from jax.sharding import PartitionSpec as P

HEAD_DIM = 64
EPSILON = 1e-05
MASKED = -1e30
BF = jnp.bfloat16
F32 = jnp.float32
TAIL = 16
ROUTE_VMEM = 24
ATTEND_VMEM = 54
HOME_VMEM = 18
SCORE_VMEM = 12
TOKENS_VMEM = 18
OUTPUT_VMEM = 10
WIDE_VMEM = 28
NARROW_VMEM = 28
SUM1_VMEM = 8
SUM2_VMEM = 8
SUM3_VMEM = 10
SUM4_VMEM = 8
SUM5_VMEM = 8
SUM6_VMEM = 8
EXPERT_VMEM = (28, 38)
NN = (((1,), (0,)), ((), ()))
NT = (((1,), (1,)), ((), ()))
TN = (((0,), (0,)), ((), ()))


def mxu(left, right, dims=NN):
    return lax.dot_general(left, right, dims, preferred_element_type=F32)


def split_high(values):
    high = values.astype(BF)
    low = (values - high.astype(F32)).astype(BF)
    return high, low


def mxu_wide(left, right, dims=NN):
    left_high, left_low = split_high(left)
    right_high, right_low = split_high(right)
    return (
        mxu(left_high, right_high, dims)
        + mxu(left_high, right_low, dims)
        + mxu(left_low, right_high, dims)
    )


def kernel_call(body, weight, deps=(), vmem=2, **kwargs):
    deps = jax.tree.leaves(deps)
    inputs, outputs = len(kwargs["in_specs"]), len(kwargs["out_shape"])
    first = inputs + len(deps)
    kwargs["in_specs"] = list(kwargs["in_specs"]) + [
        pl.BlockSpec((1,) * (dep.ndim - 2) + (min(16, dep.shape[-2]), 128), lambda *_, rank=dep.ndim: (0,) * rank)
        if dep.ndim > 1 and "grid" in kwargs
        else pl.BlockSpec(memory_space=pl.ANY)
        for dep in deps
    ]
    kwargs["out_shape"] = list(kwargs["out_shape"]) + [jax.ShapeDtypeStruct((8, 128), F32)]
    if "out_specs" in kwargs:
        done_spec = whole((8, 128)) if "grid" in kwargs else pl.BlockSpec(memory_space=pltpu.VMEM)
        kwargs["out_specs"] = list(kwargs["out_specs"]) + [done_spec]

    def run(*refs):
        refs[first + outputs][...] = jnp.zeros((8, 128), F32)
        body(*refs[:inputs], *refs[first : first + outputs], *refs[first + outputs + 1 :])

    call = pl.pallas_call(
        run,
        compiler_params=pltpu.CompilerParams(
            vmem_limit_bytes=vmem * 2**20,
            dimension_semantics=("arbitrary",) * len(kwargs.get("grid", ())),
        ),
        cost_estimate=pl.CostEstimate(flops=int(weight * 2**30), bytes_accessed=0, transcendentals=0),
        **kwargs,
    )

    def made(*args):
        *outs, done = call(*args, *deps)
        return outs, done

    return made


def hbm(array):
    return pltpu.with_memory_space_constraint(array, pltpu.HBM)


def whole(shape):
    return pl.BlockSpec(shape, lambda *_: (0,) * len(shape))


def route_kernel(slots, place_ref, order_ref, chosen_ref, rows_ref, pos_ref, rank_ref, sent_ref):
    group = sent_ref.shape[0]
    order = order_ref[...].astype(F32)
    count = order.shape[1]
    chosen = chosen_ref[...]
    chosen_wide = jnp.transpose(jnp.broadcast_to(chosen.astype(F32), (128, count)))
    order_col = jnp.transpose(jnp.broadcast_to(order, (128, count)))[:, :1]
    before = (order_col < order) & (chosen_wide[:, :1] == chosen.astype(F32))
    rank = jnp.sum(before.astype(F32), axis=0, keepdims=True).astype(jnp.int32)
    place = place_ref[0]
    pos = jnp.where(chosen >= place, chosen - place, chosen - place + group) * slots + rank
    pos_ref[...] = pos
    rank_ref[...] = rank
    lanes = lax.broadcasted_iota(jnp.int32, (count, 128), 1).astype(F32)
    rows = rows_ref[...]
    tally = jnp.sum((chosen_wide == lanes).astype(F32), axis=0, keepdims=True)
    upper = jnp.floor(tally * (1.0 / 256.0))
    place_row = lax.broadcasted_iota(jnp.int32, (TAIL, 128), 0)
    tail = jnp.where(place_row == 0, upper, jnp.where(place_row == 1, tally - 256.0 * upper, 0.0))
    tail = jnp.concatenate([tail, jnp.zeros((TAIL, rows.shape[1] - 128), F32)], axis=1).astype(BF)
    for k in range(group):
        spots = lax.broadcasted_iota(jnp.int32, (slots, count), 0) + k * slots
        sent_ref[k, :slots, :] = mxu((spots == chosen * slots + rank).astype(F32).astype(BF), rows).astype(BF)
        sent_ref[k, slots:, :] = tail


def norm_of(values, gain, shift):
    centered = values - jnp.mean(values, axis=-1, keepdims=True)
    scale = lax.rsqrt(jnp.mean(centered * centered, axis=-1, keepdims=True) + EPSILON)
    unit = centered * scale
    return unit, scale, unit * gain + shift


def router_of(projected, table, temper):
    scale = lax.rsqrt(jnp.sum(projected * projected, axis=0, keepdims=True) + 1.0)
    unit = projected * scale
    table_scale = lax.rsqrt(jnp.sum(table * table, axis=1, keepdims=True) + 1.0)
    unit_table = table * table_scale
    logits = lax.dot_general(
        unit_table, unit, NN, precision=lax.Precision.HIGHEST, preferred_element_type=F32
    ) / temper
    return scale, unit, table_scale, unit_table, logits


def softmax_rows(logits, experts):
    valid = lax.broadcasted_iota(jnp.int32, logits.shape, 0) < experts
    logits = jnp.where(valid, logits, MASKED)
    weights = jnp.exp(logits - jnp.max(logits, axis=0, keepdims=True))
    return weights / jnp.sum(weights, axis=0, keepdims=True)


def same_label(labels):
    labels = labels.astype(F32)
    column = jnp.transpose(jnp.broadcast_to(labels, (128, labels.shape[1])))[:, :1]
    return jnp.where(column == labels, 0.0, MASKED)


def attend_kernel(experts, slots, x_ref, label_ref, gain_one_ref, shift_one_ref, wq_ref,
                  wk_ref, wv_ref, wo_ref, gain_two_ref, shift_two_ref, router_ref, table_ref, temper_ref,
                  chosen_ref, pos_ref, turned_ref, q_ref, k_ref, v_ref, att_ref, lse_ref, residual_ref,
                  projected_ref, *rest):
    sent_refs, bias_ref, lse_cols_ref = rest[:-2], rest[-2], rest[-1]
    step = pl.program_id(0)
    x = x_ref[...].astype(F32)
    rows, width = x.shape
    normed = norm_of(x, gain_one_ref[...], shift_one_ref[...])[2].astype(BF)
    turned_ref[...] = jnp.transpose(normed)
    q_ref[...] = (mxu(normed, wq_ref[...]).astype(BF).astype(F32) * HEAD_DIM ** (-0.5)).astype(BF)
    k_ref[...] = mxu(normed, wk_ref[...]).astype(BF)
    v_ref[...] = mxu(normed, wv_ref[...]).astype(BF)
    bias_ref[...] = same_label(label_ref[0])
    lane = lax.broadcasted_iota(jnp.int32, (rows, 128), 1)
    low_lanes = lane < HEAD_DIM
    lse_cols = jnp.zeros((rows, 128), F32)
    for pair in range(width // 128):
        columns = slice(pair * 128, pair * 128 + 128)
        q_pair, k_pair, v_pair = q_ref[:, columns], k_ref[:, columns], v_ref[:, columns]
        outs = []
        for half in range(2):
            own = low_lanes if half == 0 else jnp.logical_not(low_lanes)
            q_own = jnp.where(own, q_pair.astype(F32), 0.0).astype(BF)
            scores = mxu(q_own, k_pair, NT) + bias_ref[...]
            largest = jnp.max(scores, axis=-1, keepdims=True)
            weights = jnp.exp(scores - largest)
            total = jnp.sum(weights, axis=-1, keepdims=True)
            outs.append(mxu((weights * (1.0 / total)).astype(BF), v_pair))
            lse_cols = jnp.where(lane == pair * 2 + half, largest + jnp.log(total), lse_cols)
        att_ref[:, columns] = jnp.where(low_lanes, outs[0], outs[1]).astype(BF)
    lse_cols_ref[...] = lse_cols
    lse_ref[...] = jnp.transpose(lse_cols_ref[...])[: lse_ref.shape[0]]
    residual = x + mxu(att_ref[...], wo_ref[...])
    residual_ref[...] = residual
    normed_two = norm_of(residual, gain_two_ref[...], shift_two_ref[...])[2]
    projected = lax.dot_general(
        router_ref[...], normed_two, NT, precision=lax.Precision.HIGHEST, preferred_element_type=F32
    )
    projected_ref[...] = projected
    logits = router_of(projected, table_ref[...], temper_ref[0])[4]
    routed = softmax_rows(logits, experts)
    selected = chosen_ref[...] == lax.broadcasted_iota(jnp.int32, logits.shape, 0)
    gate = jnp.sum(jnp.where(selected, routed, 0.0), axis=0, keepdims=True)
    high = gate.astype(BF).astype(F32)
    mid = (gate - high).astype(BF).astype(F32)
    low = gate - high - mid
    place = lax.broadcasted_iota(jnp.int32, (TAIL, rows), 0)
    pieces = jnp.where(place == 0, high, jnp.where(place == 1, mid, jnp.where(place == 2, low, 0.0)))
    pieces = pieces.astype(BF)
    entering = normed_two.astype(BF)
    pos = pos_ref[...]
    for k in range(len(sent_refs)):
        spots = lax.broadcasted_iota(jnp.int32, (slots, rows), 0) + k * slots
        here = (spots == pos).astype(F32).astype(BF)
        sent = mxu(here, entering)
        gates = mxu(pieces, here, NT)
        tail = jnp.concatenate([gates, jnp.zeros((TAIL, width - slots), F32)], axis=1)

        @pl.when(step == 0)
        def _():
            sent_refs[k][:slots, :] = sent.astype(BF)
            sent_refs[k][slots:, :] = tail.astype(BF)

        @pl.when(step > 0)
        def _():
            sent_refs[k][:slots, :] = (sent_refs[k][:slots, :].astype(F32) + sent).astype(BF)
            sent_refs[k][slots:, :] = (sent_refs[k][slots:, :].astype(F32) + tail).astype(BF)


def gelu_parts(values):
    share = 0.5 * lax.erf(values * 0.5**0.5) + 0.5
    return share, jnp.exp(values * values * (-0.5)) * (2.0 * 3.141592653589793) ** (-0.5)


def pack_offsets(counts_ref, ids):
    offsets, total = [], 0
    for k in ids:
        offsets.append(pl.multiple_of(total, 16))
        total = total + (counts_ref[k] + 15) // 16 * 16
    return offsets, total


def source_of(place_ref, k, group):
    return lax.rem(place_ref[0] - k + group, group)


def expert_kernel(ids, block, counts_ref, place_ref, u_ref, *refs):
    chunks = len(ids)
    x_refs = refs[:chunks]
    wide_ref, narrow_ref = refs[chunks : chunks + 2]
    rest = refs[chunks + 2 :]
    out_refs, back_refs = rest[:chunks], rest[chunks : 2 * chunks]
    act_ref, pre_ref, xs, us, out_sum, back_sum, sums = rest[2 * chunks :]
    step, steps = pl.program_id(0), pl.num_programs(0)
    rows = x_refs[0].shape[0] - TAIL
    offsets, total = pack_offsets(counts_ref, ids)

    @pl.when(step == 0)
    def _():
        xs[...] = jnp.zeros_like(xs)
        us[...] = jnp.zeros_like(us)
        out_sum[...] = jnp.zeros_like(out_sum)
        back_sum[...] = jnp.zeros_like(back_sum)
        for k in range(chunks):
            xs[pl.ds(offsets[k], rows), :] = x_refs[k][:rows, :]
            us[pl.ds(offsets[k], rows), :] = u_ref[source_of(place_ref, ids[k], u_ref.shape[0]), :rows, :]

    def one(i, carry):
        here = pl.ds(pl.multiple_of(i * block, block), block)
        wide, narrow = wide_ref[...], narrow_ref[...]
        hidden = mxu(xs[here, :], wide)
        grad = mxu(us[here, :], narrow, NT)
        share, density = gelu_parts(hidden)
        act = (hidden * share).astype(BF)
        act_ref[here, :] = act
        pre = (grad * (share + hidden * density)).astype(BF)
        pre_ref[here, :] = pre
        out_sum[here, :] += mxu(act, narrow)
        back_sum[here, :] += mxu(pre, wide, NT)
        return carry

    blocks = (total + block - 1) // block
    lax.fori_loop(0, blocks, one, 0)

    def none(i, carry):
        here = pl.ds(pl.multiple_of(i * block, block), block)
        act_ref[here, :] = jnp.zeros((block, act_ref.shape[1]), BF)
        pre_ref[here, :] = jnp.zeros((block, pre_ref.shape[1]), BF)
        return carry

    lax.fori_loop(blocks, act_ref.shape[0] // block, none, 0)

    @pl.when(step == steps - 1)
    def _():
        out = out_sum[...].astype(BF).astype(F32)
        gates = jnp.sum(out * us[...].astype(F32), axis=1, keepdims=True)
        sums[...] = jnp.broadcast_to(gates, sums.shape)
        for k in range(chunks):
            here = pl.ds(offsets[k], rows)
            out_refs[k][...] = out_sum[here, :].astype(BF)
            back_refs[k][:rows, :] = back_sum[here, :].astype(BF)
            gate = jnp.transpose(sums[here, :])[:1]
            high = gate.astype(BF).astype(F32)
            mid = (gate - high).astype(BF).astype(F32)
            place = lax.broadcasted_iota(jnp.int32, (TAIL, rows), 0)
            tail = jnp.where(place == 0, high, jnp.where(place == 1, mid, jnp.where(place == 2, gate - high - mid, 0.0)))
            tail = jnp.concatenate([tail, jnp.zeros((TAIL, out.shape[1] - rows), F32)], axis=1)
            back_refs[k][rows:, :] = tail.astype(BF)


def expert_call(counts, place, ids, xs, us, wide, narrow, deps, block=384, parts=4):
    chunks, (tailed, width), hidden = len(xs), xs[0].shape, wide.shape[1]
    rows = tailed - TAIL
    cut, most = hidden // parts, chunks * rows
    sd = jax.ShapeDtypeStruct
    smem = pl.BlockSpec(memory_space=pltpu.SMEM)
    chunk, plain = whole((tailed, width)), whole((rows, width))
    inner = pl.BlockSpec((most, cut), lambda f: (0, f))
    outs, done = kernel_call(
        partial(expert_kernel, ids, block),
        10,
        deps,
        vmem=EXPERT_VMEM[len(ids) - 1],
        grid=(parts,),
        in_specs=[smem] * 2 + [whole(us.shape)] + [chunk] * chunks
        + [pl.BlockSpec((width, cut), lambda f: (0, f)), pl.BlockSpec((cut, width), lambda f: (f, 0))],
        out_specs=[plain] * chunks + [chunk] * chunks + [inner, inner],
        out_shape=[pltpu.HBM((rows, width), BF)] * chunks + [sd((tailed, width), BF)] * chunks
        + [pltpu.HBM((most, hidden), BF)] * 2,
        scratch_shapes=[pltpu.VMEM((most, width), BF)] * 2
        + [pltpu.VMEM((most, width), F32)] * 2 + [pltpu.VMEM((most, 128), F32)],
    )(counts, place, us, *xs, hbm(wide), hbm(narrow))
    return outs[:chunks], outs[chunks : 2 * chunks], outs[-2], outs[-1], done


def pack_weighed(ids, counts_ref, x_refs, rows_of, depth, packed_ref, turned_ref):
    rows = x_refs[0].shape[0] - TAIL
    offsets, _ = pack_offsets(counts_ref, ids)
    packed_ref[...] = jnp.zeros_like(packed_ref)
    lanes = lax.broadcasted_iota(jnp.int32, (128, rows), 1)
    for k in range(len(ids)):
        gates = jnp.sum(x_refs[k][rows:, :rows].astype(F32), axis=0, keepdims=True)
        gates = jnp.where(lanes < counts_ref[ids[k]], gates, 0.0)
        gates = jnp.transpose(gates)[:, :1]
        packed_ref[pl.ds(offsets[k], rows), :] = (rows_of(k).astype(F32) * gates).astype(BF)
    turned_ref[...] = jnp.transpose(packed_ref[:depth])


def pack_units(sets, counts_ref, part_refs, packed_ref):
    offsets, _ = pack_offsets(counts_ref, sum(sets, ()))
    first = 0
    for part, part_ref in zip(sets, part_refs):
        packed_ref[pl.ds(offsets[first], part_ref.shape[0]), :] = part_ref[...]
        first += len(part)


def wide_kernel(sets, depth, counts_ref, spot_ref, *refs):
    ids = sum(sets, ())
    x_refs, pre_refs = refs[: len(ids)], refs[len(ids) : len(ids) + len(sets)]
    keep_ref, send_ref, packed, turned, pres = refs[len(ids) + len(sets) :]
    rows = x_refs[0].shape[0] - TAIL

    @pl.when(pl.program_id(0) == 0)
    def _():
        pres[...] = jnp.zeros_like(pres)
        pack_weighed(ids, counts_ref, x_refs, lambda k: x_refs[k][:rows, :], depth, packed, turned)

    pack_units(sets, counts_ref, pre_refs, pres)
    put_halves(spot_ref[0], keep_ref, [send_ref], slice(None), mxu(turned[...], pres[:depth]).astype(BF))


def narrow_kernel(sets, depth, counts_ref, spot_ref, place_ref, u_ref, *refs):
    ids = sum(sets, ())
    x_refs, act_refs = refs[: len(ids)], refs[len(ids) : len(ids) + len(sets)]
    keep_ref, send_ref, packed, turned, acts = refs[len(ids) + len(sets) :]
    rows = x_refs[0].shape[0] - TAIL
    step = pl.program_id(0)

    @pl.when(step == 0)
    def _():
        acts[...] = jnp.zeros_like(acts)
        rows_of = lambda k: u_ref[source_of(place_ref, ids[k], u_ref.shape[0]), :rows, :]
        pack_weighed(ids, counts_ref, x_refs, rows_of, depth, packed, turned)

    pack_units(sets, counts_ref, act_refs, acts)
    narrow = mxu(turned[...], acts[:depth]).astype(BF)
    spot = spot_ref[0]
    cut = keep_ref.shape[2]
    count = narrow.shape[1] // cut
    for k in range(count):
        part = narrow[:, k * cut : (k + 1) * cut]
        at = (step * count + k) // 2 ^ (spot // 2)

        @pl.when(spot % 2 == k % 2)
        def _():
            keep_ref[at] = part

        @pl.when(spot % 2 != k % 2)
        def _():
            send_ref[at] = part


def weight_calls(counts, spot, place, sets, xs, us, acts, pres, blocks, depth, deps, parts=4):
    chunks, (tailed, width), hidden = len(xs), xs[0].shape, acts[0].shape[1]
    half = blocks // 2
    cut, most = hidden // parts, chunks * (tailed - TAIL)
    smem = pl.BlockSpec(memory_space=pltpu.SMEM)
    inner = [pl.BlockSpec((act.shape[0], cut), lambda f: (0, f)) for act in acts]
    common = dict(
        grid=(parts,),
        scratch_shapes=[pltpu.VMEM((most, width), BF), pltpu.VMEM((width, depth), BF), pltpu.VMEM((most, cut), BF)],
    )
    chunk_specs = [whole((tailed, width))] * chunks
    wide, wide_done = kernel_call(
        partial(wide_kernel, sets, depth),
        5,
        vmem=WIDE_VMEM,
        in_specs=[smem] * 2 + chunk_specs + inner,
        out_specs=[pl.BlockSpec((half, width // blocks, cut), lambda f: (0, 0, f))] * 2,
        out_shape=[jax.ShapeDtypeStruct((half, width // blocks, hidden), BF)] * 2,
        **common,
    )(counts, spot, *xs, *map(hbm, pres))
    narrow, _ = kernel_call(
        partial(narrow_kernel, sets, depth),
        1,
        [deps, wide_done],
        vmem=NARROW_VMEM,
        in_specs=[smem] * 3 + [whole(us.shape)] + chunk_specs + inner,
        out_specs=[whole((half, width, hidden // blocks))] * 2,
        out_shape=[jax.ShapeDtypeStruct((half, width, hidden // blocks), BF)] * 2,
        **common,
    )(counts, spot, place, us, *xs, *map(hbm, acts))
    return *wide, *narrow


def weight_first_kernel(keep_wide, came_wide, keep_narrow, came_narrow, own_ref, x_keep, x_send, y_keep, y_send):
    rows, hidden = keep_wide.shape[1:]
    cut = keep_narrow.shape[2]
    for k in range(4):
        wide = (keep_wide[k].astype(F32) + came_wide[k].astype(F32)).astype(BF)
        if k == 0:
            own_ref[:, :hidden] = wide
        elif k == 2:
            x_keep[...] = wide
        else:
            x_send[k // 2] = wide
        for slab in range(keep_narrow.shape[1] // rows):
            here = slice(slab * rows, (slab + 1) * rows)
            columns = slice(slab * cut, (slab + 1) * cut)
            total = (keep_narrow[k, here, :].astype(F32) + came_narrow[k, here, :].astype(F32)).astype(BF)
            if k == 0:
                own_ref[:, hidden + slab * cut : hidden + (slab + 1) * cut] = total
            elif k == 1:
                y_keep[:, columns] = total
            else:
                y_send[k - 2, :, columns] = total


def weight_second_kernel(own_ref, x_keep, x_came, y_keep, y_came, sum_ref, x_send, y_send):
    hidden = x_keep.shape[1]
    sum_ref[:, :hidden] = own_ref[:, :hidden].astype(F32) + x_came[0].astype(F32)
    sum_ref[:, hidden:] = own_ref[:, hidden:].astype(F32) + y_came[0].astype(F32)
    x_send[...] = (x_keep[...].astype(F32) + x_came[1].astype(F32)).astype(BF)
    y_send[...] = (y_keep[...].astype(F32) + y_came[1].astype(F32)).astype(BF)


def weight_last_kernel(sum_ref, x_came, y_came, wide_ref, narrow_ref):
    rows, hidden = wide_ref.shape
    cut = narrow_ref.shape[0]
    wide_ref[...] = sum_ref[:, :hidden] + x_came[...].astype(F32)
    for slab in range(narrow_ref.shape[1] // rows):
        columns = slice(slab * cut, (slab + 1) * cut)
        piece = sum_ref[:, hidden + slab * cut : hidden + (slab + 1) * cut] + y_came[:, columns].astype(F32)
        narrow_ref[:, slab * rows : (slab + 1) * rows] = jnp.transpose(piece)


def as_column(row):
    return jnp.transpose(jnp.broadcast_to(row, (128, row.shape[1])))[:, :1]


def put_halves(spot, keep_ref, send_refs, columns, values):
    half, rows = keep_ref.shape[:2]
    held = half // len(send_refs)
    for block in range(2 * half):
        part = values[block * rows : (block + 1) * rows]
        at = (block // 2) ^ (spot // 2)

        @pl.when(spot % 2 == block % 2)
        def _():
            keep_ref[at, :, columns] = part

        for k, send_ref in enumerate(send_refs):

            @pl.when((spot % 2 != block % 2) & (at // held == k))
            def _():
                send_ref[at % held, :, columns] = part


EXACT = 32


def split_exact(values):
    lane = lax.broadcasted_iota(jnp.int32, values.shape, 1)
    high = values.astype(BF).astype(F32)
    mid = (values - high).astype(BF).astype(F32)
    low = values - high - mid
    band = (lane - EXACT) // 16
    mid, low = pltpu.roll(mid, 16, 1), pltpu.roll(low, 32, 1)
    return jnp.where(band == 0, high, jnp.where(band == 1, mid, jnp.where(band == 2, low, values)))


def join_exact(values):
    lane = lax.broadcasted_iota(jnp.int32, values.shape, 1)
    total = values + pltpu.roll(values, 128 - 16, 1) + pltpu.roll(values, 128 - 32, 1)
    return jnp.where((lane >= EXACT) & (lane < EXACT + 16), total, values)


def home_kernel(experts, slots, capacity, chunks, extra_rows, temper_ref, prior_ref, chosen_ref, rank_ref, pos_ref,
                residual_ref, upstream_ref, att_ref, projected_ref, table_ref, router_ref, gain_ref, shift_ref,
                wo_ref, *refs):
    back_refs = refs[:chunks]
    (weight_ref, grad_ref, att_grad_ref, delta_ref, outer_ref, extra_ref, tiny_ref, spots_ref, extra_sum) = refs[
        chunks:
    ]
    rows, width = residual_ref.shape
    route = projected_ref.shape[0]
    for k in range(chunks):
        spots_ref[k * slots : (k + 1) * slots, :] = back_refs[k][:slots, :]
    temper = temper_ref[0]
    table = table_ref[...]
    projected = projected_ref[...]
    scale, unit, table_scale, unit_table, logits = router_of(projected, table, temper)
    routed = softmax_rows(logits, experts)
    chosen = chosen_ref[...]
    selected = chosen == lax.broadcasted_iota(jnp.int32, logits.shape, 0)
    before = sum(jnp.where(chosen == expert, prior_ref[expert], 0) for expert in range(experts))
    kept = (before + rank_ref[...] < capacity).astype(F32)
    gate = jnp.sum(jnp.where(selected, routed, 0.0), axis=0, keepdims=True)
    weight = gate * kept
    weight_ref[...] = weight
    pos = pos_ref[...]
    gate_grad = jnp.zeros((1, rows), F32)
    for k in range(chunks):
        here = (lax.broadcasted_iota(jnp.int32, (slots, rows), 0) + k * slots == pos).astype(F32).astype(BF)
        gate_grad += jnp.sum(mxu(back_refs[k][slots:, :slots], here), axis=0, keepdims=True)
    gate_grad = gate_grad * kept
    logit_grad = gate_grad * routed * (selected.astype(F32) - gate)
    highest = dict(precision=lax.Precision.HIGHEST, preferred_element_type=F32)
    unit_grad = lax.dot_general(unit_table, logit_grad, TN, **highest) / temper
    table_grad = lax.dot_general(logit_grad, unit, NT, **highest) / temper
    sharp = -jnp.sum(logit_grad * logits, keepdims=True) / temper
    projected_grad = scale * unit_grad - scale * scale * scale * projected * jnp.sum(
        projected * unit_grad, axis=0, keepdims=True
    )
    padded = jnp.concatenate([projected_grad, jnp.zeros((128 - route, rows), F32)], axis=0)
    router = jnp.concatenate([router_ref[...], jnp.zeros((128 - route, width), F32)], axis=0)
    column = pos.astype(F32)
    both = jnp.transpose(jnp.concatenate([column, weight, jnp.zeros((126, rows), F32)], axis=0))
    routed_grad = jnp.transpose(padded)
    head_lane = lax.broadcasted_iota(jnp.int32, (width, 128), 1)
    heads = (lax.broadcasted_iota(jnp.int32, (width, 128), 0) // HEAD_DIM == head_lane).astype(F32).astype(BF)
    gain, shift = gain_ref[...], shift_ref[...]
    pos_column, weight_column = both[:, :1].astype(jnp.int32), both[:, 1:2]
    lanes = lax.broadcasted_iota(jnp.int32, (rows, spots_ref.shape[0]), 1)
    home = mxu((lanes == pos_column).astype(F32).astype(BF), spots_ref[...])
    y_grad = home * weight_column + mxu_wide(routed_grad, router)
    unit_two, norm_scale, normed_two = norm_of(residual_ref[...], gain, shift)
    inner = y_grad * gain
    two_part = norm_scale * (
        inner
        - jnp.mean(inner, axis=-1, keepdims=True)
        - unit_two * jnp.mean(inner * unit_two, axis=-1, keepdims=True)
    )
    residual_grad = upstream_ref[...].astype(F32) + two_part
    grad_ref[...] = residual_grad
    branch = residual_grad.astype(BF)
    att_grad = mxu(branch, wo_ref[...], NT).astype(BF)
    att_grad_ref[...] = att_grad
    product_high, product_low = split_high(att_grad.astype(F32) * att_ref[...].astype(F32))
    delta = mxu(product_high, heads) + mxu(product_low, heads)
    delta_ref[...] = jnp.transpose(delta)[: delta_ref.shape[0]]
    outer_ref[...] = mxu(jnp.transpose(att_ref[...]), branch).astype(BF)
    extra_sum[...] = jnp.zeros_like(extra_sum)
    extra_sum[:route, :] = mxu_wide(projected_grad, normed_two)
    extra_sum[route : route + 1, :] = jnp.sum(y_grad * unit_two, axis=0, keepdims=True)
    extra_sum[route + 1 : route + 2, :] = jnp.sum(y_grad, axis=0, keepdims=True)
    wide_table = jnp.concatenate([table, jnp.zeros((table.shape[0], 128 - route), F32)], axis=1)
    table_grad = jnp.concatenate([table_grad, jnp.zeros((table.shape[0], 128 - route), F32)], axis=1)
    summed = jnp.sum(wide_table * table_grad, axis=1, keepdims=True)
    table_grad = table_scale * table_grad - table_scale * table_scale * table_scale * wide_table * summed
    tiny = jnp.concatenate([table_grad, jnp.broadcast_to(sharp, (8, 128))], axis=0)
    tiny_ref[...] = tiny
    extra = jnp.transpose(extra_sum[...])
    if chunks <= 8:
        tiny = jnp.concatenate([tiny, jnp.zeros((128 - tiny.shape[0], 128), F32)], axis=0)
        tiny = pltpu.roll(jnp.transpose(tiny)[: extra_rows], EXACT, 1)
        lane = lax.broadcasted_iota(jnp.int32, tiny.shape, 1)
        tiny = split_exact(jnp.where((lane >= EXACT) & (lane < EXACT + 16), tiny, 0.0))
        tiny = jnp.concatenate([tiny] * (extra.shape[0] // extra_rows), axis=0)
        lane = lax.broadcasted_iota(jnp.int32, tiny.shape, 1)
        extra = jnp.where(lane < EXACT, extra, tiny)
    extra_ref[...] = extra.astype(BF)


def score_back_kernel(first, pairs, weights, spot_ref, label_ref, q_ref, k_ref, v_ref, att_grad_ref, lse_ref, delta_ref,
                      turned_ref, *refs):
    count = 3 + (1 + SENDS) * weights
    more_refs, out_refs, bias_ref = refs[: -1 - count], refs[-1 - count : -1], refs[-1]
    dq_ref, dk_ref, dv_ref = out_refs[:3]
    rows = label_ref.shape[2]
    low_lanes = lax.broadcasted_iota(jnp.int32, (rows, 128), 1) < HEAD_DIM
    for seq in range(label_ref.shape[0]):
        here = slice(seq * rows, (seq + 1) * rows)
        bias_ref[...] = same_label(label_ref[seq])
        for pair in range(pairs):
            there = slice(pair * 128, pair * 128 + 128)
            columns = slice((first + pair) * 128, (first + pair) * 128 + 128)
            q_pair, k_pair, v_pair = q_ref[here, columns], k_ref[here, columns], v_ref[here, columns]
            g_pair = att_grad_ref[here, columns]
            k_turned = jnp.transpose(k_pair)
            dk = jnp.zeros((rows, 128), F32)
            dv = jnp.zeros((rows, 128), F32)
            dq_turned = []
            for half in range(2):
                own = low_lanes if half == 0 else jnp.logical_not(low_lanes)
                q_own = jnp.where(own, q_pair.astype(F32), 0.0).astype(BF)
                g_own = jnp.where(own, g_pair.astype(F32), 0.0).astype(BF)
                head = (first + pair) * 2 + half
                head = slice(head, head + 1)
                probs = jnp.exp(mxu(k_pair, q_own, NT) + bias_ref[...] - lse_ref[head, here])
                prob_grad = mxu(v_pair, g_own, NT)
                score_grad = (probs * (prob_grad - delta_ref[head, here])).astype(BF)
                dv += mxu(probs.astype(BF), g_own)
                dk += mxu(score_grad, q_own)
                dq_turned.append(mxu(k_turned[half * HEAD_DIM : (half + 1) * HEAD_DIM], score_grad))
            dq = jnp.transpose(jnp.concatenate(dq_turned, axis=0)) * HEAD_DIM ** (-0.5)
            dq_ref[here, there] = dq.astype(BF)
            dk_ref[here, there] = dk.astype(BF)
            dv_ref[here, there] = dv.astype(BF)
    if weights:
        weight_grads(spot_ref[0], turned_ref, (dq_ref, dk_ref, dv_ref), more_refs, out_refs[3], out_refs[4:])


def weight_grads(spot, turned_ref, grad_refs, more_refs, keep_ref, send_refs):
    start = 0
    for ref in grad_refs:
        columns = slice(start, start + ref.shape[1])
        put_halves(spot, keep_ref, send_refs, columns, mxu(turned_ref[...], ref[...]).astype(BF))
        start += ref.shape[1]
    for more_ref in more_refs:
        columns = slice(start, start + more_ref.shape[1])
        put_halves(spot, keep_ref, send_refs, columns, more_ref[...])
        start += more_ref.shape[1]


def tokens_kernel(groups, spot_ref, turned_ref, x_ref, grad_ref, wq_ref, wk_ref, wv_ref, gain_ref, shift_ref, *refs):
    tokens_ref, keep_ref, send_ref, joined_ref, sums_ref, turned_sums_ref = refs[3 * groups :]
    one_grad = 0.0
    for part, w_ref in enumerate((wq_ref, wk_ref, wv_ref)):
        start = 0
        for group in range(groups):
            piece = refs[3 * group + part]
            joined_ref[part, :, start : start + piece.shape[1]] = piece[...]
            start += piece.shape[1]
        one_grad += mxu(joined_ref[part], w_ref[...], NT)
    unit, scale, _ = norm_of(x_ref[...].astype(F32), gain_ref[...], shift_ref[...])
    inner = one_grad * gain_ref[...]
    one_part = scale * (
        inner
        - jnp.mean(inner, axis=-1, keepdims=True)
        - unit * jnp.mean(inner * unit, axis=-1, keepdims=True)
    )
    tokens_ref[...] = (grad_ref[...] + one_part).astype(BF)
    sums_ref[...] = jnp.zeros_like(sums_ref)
    sums_ref[0:1, :] = jnp.sum(one_grad * unit, axis=0, keepdims=True)
    sums_ref[1:2, :] = jnp.sum(one_grad, axis=0, keepdims=True)
    turned_sums_ref[...] = jnp.transpose(sums_ref[...]).astype(BF)
    weight_grads(spot_ref[0], turned_ref, refs[3 * groups - 3 : 3 * groups], [turned_sums_ref], keep_ref, [send_ref])


def first_sum_kernel(exact, count, keep_ref, *refs):
    came_refs, out_refs = refs[:count], refs[count:]
    held = len(out_refs) // count
    for k, out_ref in enumerate(out_refs):
        came = came_refs[k // held][k % held].astype(F32)
        out_ref[...] = (keep_ref[k].astype(F32) + came).astype(BF)
        if exact is not None:
            here = slice(exact, exact + 128)
            out_ref[:, here] = split_exact(join_exact(keep_ref[k, :, here].astype(F32) + came[:, here])).astype(BF)


def second_sum_kernel(exact, place_ref, *refs):
    own_ref, send_refs, sum_ref = refs[4], refs[5:-1], refs[-1]
    sum_ref[...] = sum(ref[...].astype(F32) for ref in refs[:4])
    if exact is not None:
        sum_ref[:, exact : exact + 128] = split_exact(join_exact(sum_ref[:, exact : exact + 128]))
    size = own_ref.shape[0]
    group = len(send_refs) + 1
    own_ref[...] = sum_ref[pl.ds(pl.multiple_of(place_ref[0] * size, 8), size), :]
    if len(send_refs) == 1:
        (send_ref,) = send_refs
        filler = jnp.zeros((send_ref.shape[1] - size, send_ref.shape[2]), F32)
        for k in range(send_ref.shape[0]):
            block = jnp.where(place_ref[0] == k, 0.0, sum_ref[k * size : (k + 1) * size, :])
            send_ref[k] = jnp.concatenate([block, filler], axis=0).astype(BF)
        return
    for k, send_ref in enumerate(send_refs):
        there = lax.rem(place_ref[0] + k + 1, group)
        block = sum_ref[pl.ds(pl.multiple_of(there * size, 8), size), :]
        filler = jnp.zeros((send_ref.shape[0] - size, block.shape[1]), F32)
        send_ref[...] = jnp.concatenate([block, filler], axis=0).astype(BF)


def last_sum_kernel(first, last, route, group, experts_padded, counts, *refs):
    query_ref, key_ref, value_ref, outer_ref, router_ref, norms_ref, table_ref, sharp_ref = refs[sum(counts) :]
    rows, width = outer_ref.shape

    def total(parts, columns):
        value = parts[0][:, columns]
        for ref in parts[1:]:
            for sent in [ref] if len(ref.shape) == 2 else [ref.at[k] for k in range(ref.shape[0])]:
                value = value + sent[:, columns].astype(F32)[:rows]
        return value

    def turned(extra):
        return jnp.transpose(jnp.concatenate([extra, jnp.zeros((128 - rows, 128), F32)], axis=0))

    early, late = refs[: counts[0]], refs[counts[0] : sum(counts)]
    for part, ref in enumerate((query_ref, key_ref, value_ref)):
        ref[:, :first] = total(early, slice(part * first, (part + 1) * first))
        ref[:, first:] = total(late, slice(part * last, (part + 1) * last))
    outer_ref[...] = total(early, slice(3 * first, 3 * first + width))
    extra = join_exact(total(early, slice(3 * first + width, 3 * first + width + 128)))
    router_ref[...] = extra[:, :route]
    extra = turned(extra)
    norms = turned(total(late, slice(3 * last, 3 * last + 128)))
    norms_ref[...] = jnp.concatenate([norms[:2, :rows], extra[route : route + 2, :rows]], axis=0)
    table_ref[...] = extra[EXACT : EXACT + group, :route]
    sharp_ref[...] = extra[EXACT + experts_padded : EXACT + experts_padded + 1, :1]


def output_kernel(residual_ref, weight_ref, pos_ref, *refs):
    out_refs, layer_ref, spots_ref = refs[:-2], refs[-2], refs[-1]
    slots = out_refs[0].shape[0]
    for k, out_ref in enumerate(out_refs):
        spots_ref[k * slots : (k + 1) * slots, :] = out_ref[...]
    rows = residual_ref.shape[0]
    both = jnp.concatenate([pos_ref[...].astype(F32), weight_ref[...], jnp.zeros((126, rows), F32)], axis=0)
    both = jnp.transpose(both)
    pos_column, weight_column = both[:, :1].astype(jnp.int32), both[:, 1:2]
    lanes = lax.broadcasted_iota(jnp.int32, (rows, spots_ref.shape[0]), 1)
    home = mxu((lanes == pos_column).astype(F32).astype(BF), spots_ref[...])
    layer_ref[...] = (residual_ref[...] + home * weight_column).astype(BF)


def swap(values, axis, mask):
    size = lax.axis_size(axis)
    return lax.ppermute(values, axis, [(i, i ^ mask) for i in range(size)])


def shift(values, axis, step):
    size = lax.axis_size(axis)
    return lax.ppermute(values, axis, [(i, (i + step) % size) for i in range(size)])


def pick(values, index, axis):
    return lax.dynamic_index_in_dim(values, index, axis, keepdims=False)


def held(arrays, deps):
    anywhere = pl.BlockSpec(memory_space=pl.ANY)
    return kernel_call(
        lambda *refs: None,
        0,
        deps,
        grid=(1,),
        in_specs=[anywhere] * len(arrays),
        out_specs=[anywhere] * len(arrays),
        out_shape=[jax.ShapeDtypeStruct(array.shape, array.dtype) for array in arrays],
        input_output_aliases={k: k for k in range(len(arrays))},
    )(*arrays)


def seen(arrays):
    return kernel_call(lambda *refs: None, 0, jax.tree.leaves(arrays), grid=(1,), in_specs=[], out_specs=[], out_shape=[])()[1]


def first_sum(keep, sends, exact, deps, weight):
    half, rows, width = keep.shape
    return kernel_call(
        partial(first_sum_kernel, exact, len(sends)),
        weight,
        deps,
        vmem=SUM1_VMEM,
        in_specs=[pl.BlockSpec()] * (1 + len(sends)),
        out_shape=[jax.ShapeDtypeStruct((rows, width), BF)] * half,
    )(keep, *[swap(send, "dp", 1) for send in sends])


def second_sum(parts, place_vec, exact, deps, weight, together=False):
    group = lax.axis_size("expert")
    came = [parts[0]] + [swap(parts[k], "dp", 2 * k) for k in range(1, len(parts))]
    rows, width = parts[0].shape
    if group > 8:
        return [sum(part.astype(F32) for part in came)], ()
    size = rows // group
    padded = (size + 15) // 16 * 16
    sd = jax.ShapeDtypeStruct
    return kernel_call(
        partial(second_sum_kernel, exact),
        weight,
        deps,
        vmem=SUM2_VMEM,
        in_specs=[pl.BlockSpec(memory_space=pltpu.SMEM)] + [pl.BlockSpec()] * len(came),
        out_shape=[sd((size, width), F32)]
        + ([sd((group, padded, width), BF)] if together else [sd((padded, width), BF)] * (group - 1)),
        scratch_shapes=[pltpu.VMEM((rows, width), F32)],
    )(place_vec, *came)


def sent_on(parts):
    if lax.axis_size("expert") > 8:
        return [lax.psum_scatter(parts[0], "expert", scatter_dimension=0, tiled=True)]
    if len(parts) == 2:
        return [parts[0], lax.all_to_all(parts[1], "expert", 0, 0, tiled=True)]
    return [parts[0]] + [shift(parts[k], "expert", k) for k in range(1, len(parts))]


def small_sum(values):
    group = lax.axis_size("expert")
    if group > 8:
        return lax.psum(values, ("dp", "expert"))
    values = values + swap(values, "dp", 1)
    values = values + sum(swap(values, "dp", mask) for mask in range(2, lax.axis_size("dp"), 2))
    return values + sum(shift(values, "expert", k) for k in range(1, group))


def exchange(blocks, sign):
    size = lax.axis_size("expert")
    if size <= 8:
        return [blocks[0]] + [shift(blocks[k], "expert", sign * k) for k in range(1, size)]
    stacked = jnp.stack(blocks)
    place = lax.axis_index("expert")
    across = (jnp.arange(size) - place) * sign % size
    there = lax.all_to_all(stacked[across], "expert", 0, 0, tiled=True)
    source = (place - sign * jnp.arange(size)) % size
    home = there[source]
    return [home[k] for k in range(size)]


WAYS = 4
SETS = ((0,), (1, 3), (2,))
CUTS = (512, 256)
SENDS = 2
D0_WEIGHT, D1_WEIGHT, FIRST_WEIGHT, TOKENS_WEIGHT = 0.1, 0.1, 0.05, 0.1
MID_WEIGHT, LATE_FIRST_WEIGHT, SECOND_WEIGHT, LATE_SECOND_WEIGHT, LAST_WEIGHT, OUTPUT_WEIGHT = 18, 1, 1, 7, 0.1, 0.1


def body(
    layer_inputs_matrix,
    upstream_output_sensitivity,
    mixer_layernorm_scale,
    mixer_layernorm_offset,
    asker_matrix,
    lookup_label_matrix,
    content_matrix,
    mixer_result_matrix,
    specialist_layernorm_scale,
    specialist_layernorm_offset,
    dispatch_projection_matrix,
    specialist_centroids,
    learned_sharpness,
    specialist_widening_matrix,
    specialist_narrowing_matrix,
    document_labels,
    chosen_specialist,
    placement_ranks,
):
    rows, width = layer_inputs_matrix.shape
    seqs, length = document_labels.shape
    head_count = width // HEAD_DIM
    group = lax.axis_size("expert")
    place = lax.axis_index("expert")
    dp_size = lax.axis_size("dp")
    wide, narrow = specialist_widening_matrix[0], specialist_narrowing_matrix[0]
    hidden = wide.shape[1]
    route = dispatch_projection_matrix.shape[1]
    slots = 3 * rows // (2 * group)
    spots = group * slots
    experts_padded = (group + 7) // 8 * 8
    sd = jax.ShapeDtypeStruct
    smem, vmem = (pl.BlockSpec(memory_space=space) for space in (pltpu.SMEM, pltpu.VMEM))
    int32 = jnp.int32
    place_vec = place.astype(int32).reshape(1)
    spot_vec = lax.axis_index("dp").astype(int32).reshape(1)
    vec = lambda v: v.reshape(1, -1)
    gain_one, shift_one = vec(mixer_layernorm_scale), vec(mixer_layernorm_offset)
    gain_two, shift_two = vec(specialist_layernorm_scale), vec(specialist_layernorm_offset)
    router = dispatch_projection_matrix.T
    table = jnp.zeros((experts_padded, route), F32).at[:group].set(specialist_centroids)
    labels = document_labels.reshape(seqs, 1, length)
    chosen = chosen_specialist.reshape(1, rows)

    row_block = pl.BlockSpec((length, width), lambda s: (s, 0))
    line = pl.BlockSpec((1, length), lambda s: (0, s))
    label_spec = pl.BlockSpec((1, 1, length), lambda s: (s, 0, 0))
    turned_block = pl.BlockSpec((width, length), lambda s: (0, s))
    heads_block = pl.BlockSpec((16, length), lambda s: (0, s))
    weight_spec = whole((width, width))
    vec_spec = whole((1, width))
    chunk_spec, tailed_spec = whole((slots, width)), whole((slots + TAIL, width))
    table_spec = whole((experts_padded, route))

    tailed = slots + TAIL
    (pos, rank, upstream_sent), _ = kernel_call(
        partial(route_kernel, slots),
        5,
        vmem=ROUTE_VMEM,
        in_specs=[smem] + [pl.BlockSpec()] * 3,
        out_shape=[sd((1, rows), int32)] * 2 + [pltpu.HBM((group, tailed, width), BF)],
    )(place_vec, placement_ranks, chosen, upstream_output_sensitivity)
    upstream_there = lax.all_to_all(upstream_sent, "expert", 0, 0, tiled=True)

    (turned, queries, keys, values, attended, lse, residual, projected, *entering_sent), _ = kernel_call(
        partial(attend_kernel, group, slots),
        20,
        vmem=ATTEND_VMEM,
        grid=(seqs,),
        in_specs=[row_block, label_spec] + [vec_spec] * 2 + [weight_spec] * 4 + [vec_spec] * 2
        + [whole((route, width)), table_spec, smem, line, line],
        out_specs=[turned_block] + [row_block] * 4
        + [heads_block, row_block, pl.BlockSpec((route, length), lambda s: (0, s))] + [tailed_spec] * group,
        out_shape=[pltpu.HBM((width, rows), BF)] + [pltpu.HBM((rows, width), BF)] * 4
        + [sd((16, rows), F32), pltpu.HBM((rows, width), F32), sd((route, rows), F32)]
        + [pltpu.HBM((tailed, width), BF)] * group,
        scratch_shapes=[pltpu.VMEM((length, length), F32), pltpu.VMEM((length, 128), F32)],
    )(
        layer_inputs_matrix, labels, gain_one, shift_one, asker_matrix, lookup_label_matrix,
        content_matrix, mixer_result_matrix, gain_two, shift_two, router, table, learned_sharpness, chosen, pos,
    )
    tails = upstream_there[:, slots : slots + 2, :experts_padded].astype(F32)
    tallies = (tails[:, 0] * 256.0 + tails[:, 1]).astype(int32)
    sources = jnp.arange(group)
    prior = jnp.sum(jnp.where(sources[:, None] < place, tallies, 0), axis=0)
    named = jnp.sum(jnp.where(jnp.arange(experts_padded) == place, tallies, 0), axis=1)
    earlier = jnp.sum(jnp.where(sources[:, None] < sources[None, :], named[:, None], 0), axis=0)
    counts = jnp.clip(rows - earlier, 0, named)
    relative = (place - sources) % group
    counts = jnp.sum(jnp.where(relative[:, None] == sources[None, :], counts[None, :], 0), axis=1)

    each = group // WAYS
    backs, produced, acts, pres, order = [None] * WAYS, [None] * WAYS, [], [], []

    def experts(ids, counts, entered, graded, turn, deps):
        outs, some, act, pre, done = expert_call(counts, turn, ids, entered, graded, wide, narrow, [deps, order])
        for k, out, back in zip(ids, outs, some):
            produced[k], backs[k] = out, back
        acts.append(act)
        pres.append(pre)
        order.append(done)

    if each == 1:
        split = lambda chunks, _: list(chunks)
        turn_vec, graded, entered = place_vec, upstream_there, list(entering_sent)
        alone = jnp.sum((chosen == place).astype(int32)).reshape(1)
        experts(SETS[0], alone, entered[:1], upstream_sent, turn_vec, ())
        ready = []
        for ids in SETS[1:]:
            for k, sent in zip(ids, held([entered[k] for k in ids], ready)[0] if ready else [entered[k] for k in ids]):
                entered[k] = shift(sent, "expert", k)
            ready = [entered[k] for k in ids]
        for ids in SETS[1:]:
            experts(ids, counts, [entered[k] for k in ids], graded, turn_vec, prior)
    else:
        entering_there = exchange(entering_sent, 1)
        valid = jnp.arange(slots)[None, :] < counts[:, None]
        counts = jnp.full((WAYS,), each * slots, int32)
        turn_vec = jnp.zeros((1,), int32)

        def join(blocks, masks):
            chunks = []
            for k in range(0, group, each):
                tail = [jnp.where(masks[j], blocks[j][slots:, :slots], 0) for j in range(k, k + each)]
                tail = jnp.concatenate(tail, axis=1)
                tail = jnp.pad(tail, ((0, 0), (0, width - tail.shape[1])))
                chunks.append(jnp.concatenate([blocks[j][:slots] for j in range(k, k + each)] + [tail]))
            return chunks

        def split(chunks, with_tail):
            pieces = []
            for chunk in chunks:
                for j in range(each):
                    piece = chunk[j * slots : (j + 1) * slots]
                    if with_tail:
                        tail = chunk[each * slots :, j * slots : (j + 1) * slots]
                        piece = jnp.concatenate([piece, jnp.pad(tail, ((0, 0), (0, width - slots)))])
                    pieces.append(piece)
            return pieces

        entered = join(entering_there, valid)
        graded = join([pick(upstream_there, relative[k], 0) for k in range(group)], valid)
        graded = jnp.stack([graded[-k % WAYS] for k in range(WAYS)])
        for ids in SETS:
            experts(ids, counts, [entered[k] for k in ids], graded, turn_vec, ())
    returned_home = exchange(split(backs, True), -1)
    ordered = [k for ids in SETS for k in ids]
    arrange = lambda chunks: [chunks[k] for k in ordered]
    depth = rows + 128 if each == 1 else spots
    keep_wide, send_wide, keep_narrow, send_narrow = weight_calls(
        counts, spot_vec, turn_vec, SETS, arrange(entered), graded, acts, pres, dp_size, depth,
        [returned_home[k] for k in SETS[1]],
    )
    half, block = dp_size // 2, width // dp_size
    (weight, residual_grad, attended_grad, delta, outer_part, extra_part, tiny), done = kernel_call(
        partial(home_kernel, group, slots, rows, group, width // (dp_size * group)),
        500,
        vmem=HOME_VMEM,
        in_specs=[smem, smem] + [vmem] * (12 + group),
        out_specs=[vmem] * 7,
        out_shape=[sd((1, rows), F32), sd((rows, width), F32), sd((rows, width), BF), sd((16, rows), F32),
                   sd((width, width), BF), sd((width, 128), BF), sd((experts_padded + 8, 128), F32)],
        scratch_shapes=[pltpu.VMEM((spots, width), BF), pltpu.VMEM((128, width), F32)],
    )(
        learned_sharpness, prior, chosen, rank, pos, residual, upstream_output_sensitivity, attended,
        projected, table, router, gain_two, shift_two, mixer_result_matrix, *returned_home,
    )
    half_rows = sd((block, hidden), BF)
    (weight_own, x_keep, x_send, y_keep, y_send), first_done = kernel_call(
        weight_first_kernel,
        1,
        done,
        vmem=SUM3_VMEM,
        in_specs=[pl.BlockSpec()] * 4,
        out_shape=[sd((block, 2 * hidden), BF)] + [half_rows, sd((2, block, hidden), BF)] * 2,
    )(keep_wide, swap(send_wide, "dp", 1), keep_narrow, swap(send_narrow, "dp", 1))
    if each == 1:
        ready, starts = [first_done], []
        for ids in SETS[1:]:
            sends, held_done = held([produced[k] for k in ids], ready)
            for k, sent in zip(ids, sends):
                produced[k] = shift(sent, "expert", -k)
            ready = [produced[k] for k in ids]
            starts.append(held_done)
        produced_home = produced
    else:
        produced_home, starts, ready = exchange(split(produced, False), -1), [(), ()], []

    x_came, y_came = swap(x_send, "dp", 2), swap(y_send, "dp", 4)
    pieces, start, done = [], 0, first_done
    for cut in CUTS:
        early = start == 0
        more = [outer_part, extra_part] if early else []
        columns = 3 * cut + width + 128
        pack = [sd((half, block, columns), BF)] + [sd((half // SENDS, block, columns), BF)] * SENDS if early else []
        grads, done = kernel_call(
            partial(score_back_kernel, start // 128, cut // 128, early),
            D0_WEIGHT if early else D1_WEIGHT,
            done if early else [done, starts[1]],
            vmem=SCORE_VMEM,
            in_specs=[smem] + [vmem] * (8 + len(more)),
            out_specs=[vmem] * (3 + len(pack)),
            out_shape=[sd((rows, cut), BF)] * 3 + pack,
            scratch_shapes=[pltpu.VMEM((length, length), F32)],
        )(spot_vec, labels, queries, keys, values, attended_grad, lse, delta, turned, *more)
        pieces.append(grads[:3])
        if early:
            keep, *sends = grads[3:]
        start += cut
    first, last = CUTS
    exact = 3 * first + width
    early, done = first_sum(keep, sends, exact, done, FIRST_WEIGHT)
    pack = sd((half, block, 3 * last + 128), BF)
    (tokens_grad, keep, send), done = kernel_call(
        partial(tokens_kernel, len(CUTS)),
        TOKENS_WEIGHT,
        [done, seen([x_came, y_came])],
        vmem=TOKENS_VMEM,
        in_specs=[smem] + [vmem] * (8 + 3 * len(CUTS)),
        out_specs=[vmem] * 3,
        out_shape=[sd((rows, width), BF)] + [pack] * 2,
        scratch_shapes=[pltpu.VMEM((3, rows, width), BF), pltpu.VMEM((128, width), F32), pltpu.VMEM((width, 128), BF)],
    )(spot_vec, turned, layer_inputs_matrix, residual_grad, asker_matrix, lookup_label_matrix, content_matrix,
      gain_one, shift_one, *[piece for group_pieces in pieces for piece in group_pieces])
    (weight_sum, x_more, y_more), done = kernel_call(
        weight_second_kernel,
        MID_WEIGHT,
        seen([done, ready]),
        vmem=SUM4_VMEM,
        in_specs=[pl.BlockSpec()] * 5,
        out_shape=[sd((block, 2 * hidden), F32)] + [half_rows] * 2,
    )(weight_own, x_keep, x_came, y_keep, y_came)
    late, done = first_sum(keep, [send], None, done, LATE_FIRST_WEIGHT)
    early, done = second_sum(early, place_vec, exact, done, SECOND_WEIGHT, True)
    (x_more, y_more), _ = held([x_more, y_more], done)
    late, done = second_sum(late, place_vec, None, done, LATE_SECOND_WEIGHT)
    (layer_output,), done = kernel_call(
        output_kernel,
        OUTPUT_WEIGHT,
        done,
        vmem=OUTPUT_VMEM,
        in_specs=[vmem] * (3 + group),
        out_specs=[vmem],
        out_shape=[sd((rows, width), BF)],
        scratch_shapes=[pltpu.VMEM((spots, width), BF)],
    )(residual, weight, pos, *produced_home)
    (hidden_grad, return_grad), done = kernel_call(
        weight_last_kernel,
        LAST_WEIGHT,
        done,
        vmem=SUM5_VMEM,
        in_specs=[pl.BlockSpec()] * 3,
        out_shape=[sd((block, hidden), F32), sd((hidden // dp_size, width), F32)],
    )(weight_sum, swap(x_more, "dp", 4), swap(y_more, "dp", 2))
    early, late = sent_on(early), sent_on(late)
    own = width // (dp_size * group)
    (query_grad, key_grad, value_grad, outer_grad, router_grad, norms, table_grad, sharp), done = kernel_call(
        partial(last_sum_kernel, first, last, route, group, experts_padded, (len(early), len(late))),
        1,
        done,
        vmem=SUM6_VMEM,
        in_specs=[pl.BlockSpec()] * (len(early) + len(late)),
        out_shape=[sd((own, width), F32)] * 4
        + [sd((own, route), F32), sd((4, own), F32), sd((group, route), F32), sd((1, 1), F32)],
    )(*early, *late)
    if group > 8:
        tiny = small_sum(tiny)
        table_grad, sharp = tiny[:group, :route], tiny[experts_padded, :1]
    return (
        layer_output,
        tokens_grad,
        norms[0],
        norms[1],
        query_grad,
        key_grad,
        value_grad,
        outer_grad,
        norms[2],
        norms[3],
        router_grad,
        table_grad,
        sharp.reshape(1),
        hidden_grad[None],
        return_grad[None],
    )


def solution(mesh):
    placed = (
        P(("dp", "expert"), None),
        P(("dp", "expert"), None),
        P(),
        P(),
        P(),
        P(),
        P(),
        P(),
        P(),
        P(),
        P(),
        P(),
        P(),
        P("expert", None, None),
        P("expert", None, None),
        P(("dp", "expert"), None),
        P(("dp", "expert"), None),
        P(("dp", "expert"), None),
    )
    return jax.shard_map(
        body,
        mesh=mesh,
        in_specs=placed,
        out_specs=(
            P(("dp", "expert"), None),
            P(("dp", "expert"), None),
            P(("dp", "expert")),
            P(("dp", "expert")),
            P(("dp", "expert"), None),
            P(("dp", "expert"), None),
            P(("dp", "expert"), None),
            P(("dp", "expert"), None),
            P(("dp", "expert")),
            P(("dp", "expert")),
            P(("dp", "expert"), None),
            P(),
            P(),
            P("expert", "dp", None),
            P("expert", "dp", None),
        ),
        check_vma=False,
    )
```
